32 devices in a mesh: rows: 8 (over z, y), cols: 4 (over x, core).
Axes of the slice: x: 2, y: 2, z: 4, core: 2. Of those that a mesh axis runs over, the one named last changes fastest.
Arguments:
- crawl: bfloat16 [8192, 128], P('rows'), may hold values from -16 to 16
- bench: bfloat16 [16384, 128], P('cols'), may hold values from -2 to 2
- start_duals: float32 [16384], P('cols'), may hold values from -0.15 to 0.15
- row_cotangent: float32 [8192], P('rows'), may hold values from -24 to 24
- col_cotangent: float32 [16384], P('cols'), may hold values from -24 to 24
Outputs:
- crawl_grad: float32 [8192, 128], P('rows')
- bench_grad: float32 [16384, 128], P('cols')
The draws below stay inside these ranges and needn't reach their ends.
All inputs are finite; a program needn't handle non-finite values.
Results may differ from the reference program's by a relative error of at most 0.0039.
Values sent between devices are 32-bit elements; how exact they have to be, the bound alone decides.
No kernel may reach another device: no remote copies, remote signals or barrier semaphores. Data moves between devices by JAX's collectives and lax.ppermute only.
A program may use at most 64 MiB of HBM per device.

```python
import math
import jax
import jax.numpy as jnp
from jax import lax

D = 128
N = 8192
M = 16384


def lowered_columns(key):
    marks = jax.random.randint(jax.random.fold_in(key, 7), (M,), 0, 64)
    return (marks == 0) & (jnp.roll(marks, 1) != 0)


def bench_parts(key, spread, shrink):
    normal = jax.random.normal(jax.random.fold_in(key, 5), (M, D), jnp.float32)
    factor = jnp.exp(spread * jax.random.uniform(jax.random.fold_in(key, 6), (M, 1), jnp.float32, -1.0, 1.0))
    lowered = lowered_columns(key)
    scale = factor * jnp.where(lowered[:, None], shrink, 1.0)
    return (normal, scale)


def draw_bench(key, part):
    normal, scale = bench_parts(key, 0.0, 1.0)
    return (0.12 * normal * scale).astype(jnp.bfloat16)


def draw_crawl(key, part):
    key = jax.random.fold_in(key, 1)
    values = 0.12 * jax.random.normal(key, (N, D), jnp.float32)
    return values.astype(jnp.bfloat16)


def steps_of(rng, extent, pieces, low, largest):
    loudness = 1.0
    for axis_at, parts in pieces:
        steps = jax.random.uniform(jax.random.fold_in(jax.random.fold_in(rng, 6), axis_at), (parts,), jnp.float32, low / len(pieces), largest / len(pieces))
        loudness = loudness * jnp.repeat(jnp.exp(steps), extent[axis_at] // parts).reshape((-1,) + (1,) * (len(extent) - 1 - axis_at))
    return loudness


def scatter_about(own_key, shape, scale, bound, shards=(), kind=jnp.bfloat16):
    result = jax.random.normal(own_key, shape, jnp.float32) * scale
    if len(shards) > 0:
        result = steps_of(own_key, shape, shards, -0.22, 0.18) * result
    return jnp.clip(result, min=-bound, max=bound).astype(kind)


def setup_inputs(seed: int = 0) -> dict:
    key_list = jax.random.split(jax.random.key(seed), 6)
    return {
        "crawl": draw_crawl(jax.random.fold_in(key_list[5], 71), 0),
        "bench": draw_bench(jax.random.fold_in(key_list[5], 71), 0),
        "start_duals": jnp.clip(jax.random.uniform(key_list[2], (M,), jnp.float32, -0.15, 0.15) * steps_of(key_list[2], (M,), ((0, 4),), -0.4, 0.0), -0.15, 0.15),
        "row_cotangent": scatter_about(key_list[3], (N,), 4.0, 24.0, ((0, 8),), jnp.float32),
        "col_cotangent": scatter_about(key_list[4], (M,), 4.0, 24.0, ((0, 4),), jnp.float32),
    }


EPSILON = 0.05


def reference(crawl, bench, start_duals, row_cotangent, col_cotangent):
    block_rows = math.gcd(N, 1024)
    block_count = N // block_rows
    crawl_blocks = crawl.reshape(block_count, block_rows, D)
    log_bench = math.log(M)
    log_crawl = math.log(N)

    def scores(crawl_block):
        return lax.dot_general(crawl_block, bench, (((1,), (1,)), ((), ())), preferred_element_type=jnp.float32)

    def row_lse(col_duals):
        def block_levels(crawl_block):
            logits = (col_duals[None, :] + scores(crawl_block)) / EPSILON
            highest = jnp.max(logits, 1)
            return highest + jnp.log(jnp.sum(jnp.exp(logits - highest[:, None]), 1))
        return lax.map(block_levels, crawl_blocks).reshape(N)

    def col_lse(row_duals):
        dual_blocks = row_duals.reshape(block_count, block_rows)

        def peak(running, element):
            logits = (element[1][:, None] + scores(element[0])) / EPSILON
            return jnp.maximum(running, jnp.max(logits, 0)), None

        highest, _ = lax.scan(peak, jnp.full((M,), -jnp.inf, jnp.float32), (crawl_blocks, dual_blocks))

        def accumulate(running, element):
            logits = (element[1][:, None] + scores(element[0])) / EPSILON
            return running + jnp.sum(jnp.exp(logits - highest[None, :]), 0), None

        summed, _ = lax.scan(accumulate, jnp.zeros((M,), jnp.float32), (crawl_blocks, dual_blocks))
        return highest + jnp.log(summed)

    row_level1 = row_lse(start_duals)
    row_dual1 = -EPSILON * (row_level1 - log_bench)
    col_level1 = col_lse(row_dual1)
    col_dual1 = -EPSILON * (col_level1 - log_crawl)
    row_level2 = row_lse(col_dual1)
    row_dual2 = -EPSILON * (row_level2 - log_bench)
    col_level2 = col_lse(row_dual2)

    def split(vector):
        return vector.reshape(block_count, block_rows)

    def first_pass(running, element):
        crawl_block, dual_block, level_block, cot_block = element
        tile = scores(crawl_block)
        col_soft2 = jnp.exp((dual_block[:, None] + tile) / EPSILON - col_level2[None, :])
        row_back2 = cot_block - jnp.sum(col_soft2 * col_cotangent[None, :], 1)
        row_soft2 = jnp.exp((col_dual1[None, :] + tile) / EPSILON - level_block[:, None])
        return running - jnp.sum(row_soft2 * row_back2[:, None], 0), row_back2

    col_back1, row_back2 = lax.scan(first_pass, jnp.zeros((M,), jnp.float32),
                                    (crawl_blocks, split(row_dual2), split(row_level2), split(row_cotangent)))

    def second_pass(element):
        crawl_block, dual_block = element
        col_soft1 = jnp.exp((dual_block[:, None] + scores(crawl_block)) / EPSILON - col_level1[None, :])
        return -jnp.sum(col_soft1 * col_back1[None, :], 1)

    row_back1 = lax.map(second_pass, (crawl_blocks, split(row_dual1)))

    def third_pass(running, element):
        crawl_block, dual1, dual2, level1, level2, back1, back2 = element
        tile = scores(crawl_block)
        col_soft2 = jnp.exp((dual2[:, None] + tile) / EPSILON - col_level2[None, :])
        row_soft2 = jnp.exp((col_dual1[None, :] + tile) / EPSILON - level2[:, None])
        col_soft1 = jnp.exp((dual1[:, None] + tile) / EPSILON - col_level1[None, :])
        row_soft1 = jnp.exp((start_duals[None, :] + tile) / EPSILON - level1[:, None])
        score_grad = -(col_soft2 * col_cotangent[None, :] + row_soft2 * back2[:, None]
                       + col_soft1 * col_back1[None, :] + row_soft1 * back1[:, None])
        score_grad = score_grad.astype(jnp.bfloat16)
        crawl_part = jnp.dot(score_grad, bench, preferred_element_type=jnp.float32)
        bench_part = lax.dot_general(score_grad, crawl_block, (((0,), (0,)), ((), ())), preferred_element_type=jnp.float32)
        return running + bench_part, crawl_part

    bench_grad, crawl_parts = lax.scan(third_pass, jnp.zeros((M, D), jnp.float32),
                                       (crawl_blocks, split(row_dual1), split(row_dual2), split(row_level1),
                                        split(row_level2), row_back1, row_back2))
    return crawl_parts.reshape(N, D), bench_grad
```

```python
import functools
import math

import jax
import jax.numpy as jnp
from jax import lax
from jax.experimental import pallas as pl
from jax.experimental.pallas import tpu as pltpu
from jax.sharding import PartitionSpec as P

EPSILON = 0.05
KAPPA = math.log2(math.e) / EPSILON
LOWEST = -90.0
LANES = 128
WIDE = 512
TALL = 256
F32 = jnp.float32


def transposed_dot(a, b):
    return lax.dot_general(a, b, (((1,), (1,)), ((), ())), preferred_element_type=F32)


def column_form(row):
    return jnp.transpose(jnp.broadcast_to(row, (LANES, row.shape[1])))


def row_form(partial):
    return jnp.sum(jnp.transpose(partial), axis=0, keepdims=True)


def log_sum(parts):
    top = functools.reduce(jnp.maximum, parts)
    return top + jnp.log2(sum(jnp.exp2(p - top) for p in parts))


def row_sums(tile_ref, weights_ref, partial_ref):
    height = 64

    def body(block, _):
        rows = pl.ds(pl.multiple_of(block * height, height), height)
        acc = jnp.zeros((height, LANES), F32)
        for at in range(0, tile_ref.shape[1], LANES):
            acc += tile_ref[rows, at:at + LANES] * weights_ref[:, at:at + LANES]
        partial_ref[rows, :] = acc
        return _

    lax.fori_loop(0, tile_ref.shape[0] // height, body, 0)
    return row_form(partial_ref[...])


def column_sums(tile_ref, weights_ref, out_ref):
    starts = range(0, tile_ref.shape[1], LANES)

    def body(block, accs):
        for half in range(2):
            rows = pl.ds(pl.multiple_of(block * 16 + half * 8, 8), 8)
            weights = weights_ref[rows, :]
            accs = tuple(acc + tile_ref[rows, at:at + LANES] * weights for acc, at in zip(accs, starts))
        return accs

    accs = lax.fori_loop(0, tile_ref.shape[0] // 16, body, tuple(jnp.zeros((8, LANES), F32) for _ in starts))
    for acc, at in zip(accs, starts):
        out_ref[:, at:at + LANES] = jnp.sum(acc, axis=0, keepdims=True)


def exponent_block(crawl_ref, bench_ref, shift_ref, rows, columns):
    scores = transposed_dot(crawl_ref[rows, :], bench_ref[columns, :])
    return scores * KAPPA + shift_ref[:, columns]


def row_level_kernel(crawl_ref, bench_ref, shift_ref, tile_ref, top_ref, level_ref, top_scratch, sum_scratch):
    height = 64

    def fill(block, _):
        rows = pl.ds(pl.multiple_of(block * TALL, TALL), TALL)
        top = jnp.full((TALL, LANES), -jnp.inf, F32)
        for at in range(0, tile_ref.shape[1], WIDE):
            exponent = exponent_block(crawl_ref, bench_ref, shift_ref, rows, pl.ds(at, WIDE))
            tile_ref[rows, at:at + WIDE] = exponent
            for lane in range(0, WIDE, LANES):
                top = jnp.maximum(top, exponent[:, lane:lane + LANES])
        top_scratch[rows, :] = top
        return _

    lax.fori_loop(0, tile_ref.shape[0] // TALL, fill, 0)

    def power(block, _):
        rows = pl.ds(pl.multiple_of(block * height, height), height)
        top = jnp.broadcast_to(jnp.max(top_scratch[rows, :], axis=1, keepdims=True), (height, LANES))
        acc = jnp.zeros((height, LANES), F32)
        for at in range(0, tile_ref.shape[1], LANES):
            value = jnp.exp2(tile_ref[rows, at:at + LANES] - top)
            tile_ref[rows, at:at + LANES] = value
            acc += value
        top_scratch[rows, :] = top
        sum_scratch[rows, :] = acc
        return _

    lax.fori_loop(0, tile_ref.shape[0] // height, power, 0)
    top = jnp.transpose(top_scratch[...])[0:1, :]
    top_ref[...] = top
    level_ref[...] = top + jnp.log2(row_form(sum_scratch[...]))


def column_level_kernel(parts, tile_ref, top_ref, *refs):
    part_refs, (crawl_ref, bench_ref, shift_ref, level_ref, out_ref, weights) = refs[:parts], refs[parts:]
    level = log_sum([p[...] for p in part_refs])
    level_ref[...] = level
    weights[...] = column_form(jnp.exp2(top_ref[...] - level))
    column_sums(tile_ref, weights, out_ref)
    out_ref[...] = jnp.log2(out_ref[...])

    @pl.when(jnp.min(out_ref[...]) < LOWEST)
    def _():
        weights[...] = column_form(level)
        blocks = tile_ref.shape[0] // TALL

        def column_block(column, _):
            columns = pl.ds(pl.multiple_of(column * WIDE, WIDE), WIDE)

            def logs(block):
                rows = pl.ds(pl.multiple_of(block * TALL, TALL), TALL)
                return exponent_block(crawl_ref, bench_ref, shift_ref, rows, columns) - weights[rows, 0:1]

            top = lax.fori_loop(
                0, blocks, lambda b, t: jnp.maximum(t, jnp.max(logs(b), axis=0, keepdims=True)),
                jnp.full((1, WIDE), -jnp.inf, F32))
            total = lax.fori_loop(
                0, blocks, lambda b, t: t + jnp.sum(jnp.exp2(logs(b) - top), axis=0, keepdims=True),
                jnp.zeros((1, WIDE), F32))
            out_ref[:, columns] = top + jnp.log2(total)
            return _

        lax.fori_loop(0, tile_ref.shape[1] // WIDE, column_block, 0)


def soft_kernel(parts, tile_ref, top_ref, level_ref, *refs):
    part_refs = refs[:parts]
    crawl_ref, bench_ref, shift_ref, soft_ref, mass_ref, sums_ref, partial, weights, scale = refs[parts:]
    logs = log_sum([p[...] for p in part_refs])
    mass_ref[...] = jnp.exp2(logs)
    lowest = jnp.min(logs)
    height = 64

    @pl.when(lowest >= LOWEST)
    def _():
        weights[...] = column_form(jnp.exp2(top_ref[...] - level_ref[...]))
        scale[...] = jnp.exp2(-logs)

        def body(block, _):
            rows = pl.ds(pl.multiple_of(block * height, height), height)
            weight = weights[rows, :]
            acc = jnp.zeros((height, LANES), F32)
            for at in range(0, tile_ref.shape[1], LANES):
                value = tile_ref[rows, at:at + LANES] * weight * scale[:, at:at + LANES]
                soft_ref[rows, at:at + LANES] = value
                acc += value
            partial[rows, :] = acc
            return _

        lax.fori_loop(0, tile_ref.shape[0] // height, body, 0)

    @pl.when(lowest < LOWEST)
    def _():
        weights[...] = column_form(level_ref[...])
        scale[...] = logs
        partial[...] = jnp.zeros_like(partial)

        def body(block, _):
            rows = pl.ds(pl.multiple_of(block * TALL, TALL), TALL)
            level = weights[rows, 0:1]

            def column_block(column, _):
                columns = pl.ds(pl.multiple_of(column * WIDE, WIDE), WIDE)
                exponent = exponent_block(crawl_ref, bench_ref, shift_ref, rows, columns)
                value = jnp.exp2(exponent - level - scale[:, columns])
                soft_ref[rows, columns] = value
                partial[rows, :] += sum(value[:, lane:lane + LANES] for lane in range(0, WIDE, LANES))
                return _

            return lax.fori_loop(0, tile_ref.shape[1] // WIDE, column_block, _)

        lax.fori_loop(0, tile_ref.shape[0] // TALL, body, 0)

    sums_ref[...] = row_form(partial[...])


def second_column_kernel(parts, soft_ref, *refs):
    part_refs, (inverse_ref, out_ref, weights) = refs[:parts], refs[parts:]
    inverse = 1.0 / sum(p[...] for p in part_refs)
    inverse_ref[...] = inverse
    weights[...] = column_form(inverse)
    column_sums(soft_ref, weights, out_ref)


def second_row_kernel(parts, soft_ref, inverse_ref, cotangent_ref, *refs):
    part_refs, (scaled_ref, out_ref, partial) = refs[:parts], refs[parts:]
    scaled_ref[...] = cotangent_ref[...] / sum(p[...] for p in part_refs)
    out_ref[...] = row_sums(soft_ref, scaled_ref, partial) * inverse_ref[...]


def first_column_kernel(parts, soft_ref, inverse_ref, cotangent_ref, *refs):
    part_refs, (scaled_ref, out_ref, weights) = refs[:parts], refs[parts:]
    scaled = (cotangent_ref[...] - sum(p[...] for p in part_refs)) * inverse_ref[...]
    scaled_ref[...] = scaled
    weights[...] = column_form(-scaled)
    column_sums(soft_ref, weights, out_ref)


def first_row_kernel(parts, soft_ref, *refs):
    part_refs, (back_ref, out_ref, partial) = refs[:parts], refs[parts:]
    back_ref[...] = sum(p[...] for p in part_refs)
    out_ref[...] = -row_sums(soft_ref, back_ref, partial)


def ring_order(n):
    return [*range(0, n, 2), *range(n - 1, 0, -2)]


def ring_share(n, at):
    me = lax.axis_index("rows")
    place = lax.rem(lax.select(lax.rem(me, 2) == 0, me // 2, n - 1 - me // 2) + at, n)
    return lax.select(place < n // 2, 2 * place, 2 * (n - 1 - place) + 1)


def far_kernel(parts, n, soft_ref, inverse_ref, scaled2_ref, back_ref, mass_ref, scaled_ref, crawl_ref, *refs):
    part_refs, (first, second, third, *piece_refs, flat) = refs[:parts], refs[parts:]
    first[...] = column_form(-inverse_ref[...])
    second[...] = column_form(-scaled_ref[...])
    third[...] = column_form(-sum(p[...] for p in part_refs))
    if not piece_refs:
        return
    width = flat.shape[1]
    start = ring_share(n, n // 2) * width
    flat[...] = jnp.zeros_like(flat)

    def body(block, _):
        rows = pl.ds(pl.multiple_of(block * TALL, TALL), TALL)
        a, b, c = first[rows, :], second[rows, :], third[rows, :]
        pieces = []
        for lane in range(0, width, LANES):
            span = pl.ds(pl.multiple_of(start + lane, LANES), LANES)
            factor = a * scaled2_ref[:, span] + b + (c * mass_ref[:, span] - back_ref[:, span])
            pieces.append((soft_ref[rows, span] * factor).astype(jnp.bfloat16))
        grad = jnp.concatenate(pieces, axis=1)
        flat[...] += lax.dot_general(crawl_ref[rows, :], grad, (((0,), (0,)), ((), ())), preferred_element_type=F32)
        return _

    lax.fori_loop(0, soft_ref.shape[0] // TALL, body, 0)
    half = width // 2
    for k, piece in enumerate(piece_refs):
        piece[...] = jnp.transpose(flat[:, k * half:(k + 1) * half])


def gradient_kernel(n, places, soft_ref, first, second, third, scaled2_ref, back_ref, mass_ref, crawl_ref, bench_ref, *refs):
    keep_ref, send_ref, *piece_refs, flat, whole, total = refs
    flat[...] = jnp.zeros_like(flat)

    def body(block, _):
        rows = pl.ds(pl.multiple_of(block * TALL, TALL), TALL)
        a, b, c = first[rows, :], second[rows, :], third[rows, :]
        x = crawl_ref[rows, :]
        acc = jnp.zeros((TALL, LANES), F32)
        for at in range(0, soft_ref.shape[1], WIDE):
            pieces = []
            for lane in range(at, at + WIDE, LANES):
                span = slice(lane, lane + LANES)
                factor = a * scaled2_ref[:, span] + b + (c * mass_ref[:, span] - back_ref[:, span])
                pieces.append((soft_ref[rows, span] * factor).astype(jnp.bfloat16))
            grad = jnp.concatenate(pieces, axis=1)
            acc += jnp.dot(grad, bench_ref[at:at + WIDE, :], preferred_element_type=F32)
            flat[:, at:at + WIDE] += lax.dot_general(x, grad, (((0,), (0,)), ((), ())), preferred_element_type=F32)
        total[rows, :] = acc
        return _

    lax.fori_loop(0, soft_ref.shape[0] // TALL, body, 0)
    me = lax.axis_index("cols")
    quarter = total.shape[0] // 4
    for k, (ref, low) in enumerate(((keep_ref, 0), (send_ref, 0), (keep_ref, quarter), (send_ref, quarter))):
        start = pl.multiple_of(lax.bitwise_xor(me, k) * quarter, quarter)
        ref[low:low + quarter, :] = total[pl.ds(start, quarter), :]
    whole[...] = jnp.transpose(flat[...])
    height = piece_refs[0].shape[0]
    for k, piece in enumerate(piece_refs):
        start = ring_share(n, places[k // 2]) * 2 * height + k % 2 * height
        piece[...] = whole[pl.ds(pl.multiple_of(start, height), height), :]


def placing_kernel(n, *refs):
    (own_ref, beside_ref, pair_ref, *pieces), (crawl_out, bench_out, sems) = refs[:-3], refs[-3:]
    me = lax.axis_index("cols")
    quarter = own_ref.shape[0]
    moves = []
    for k, piece in ((0, own_ref), (2, beside_ref), (1, pair_ref.at[:quarter]), (3, pair_ref.at[quarter:])):
        start = pl.multiple_of(lax.bitwise_xor(me, k) * quarter, quarter)
        moves.append((piece, crawl_out.at[pl.ds(start, quarter)]))
    height = pieces[0].shape[0]
    for at, piece in enumerate(pieces):
        start = pl.multiple_of(ring_share(n, at // 2) * 2 * height + at % 2 * height, height)
        moves.append((piece, bench_out.at[pl.ds(start, height)]))
    copies = [pltpu.make_async_copy(source, target, sems.at[k]) for k, (source, target) in enumerate(moves)]
    for copy in copies:
        copy.start()
    for copy in copies:
        copy.wait()


def call(kernel, args, outs, scratch, aliases=None, held=()):
    ins = len(args)

    def body(*refs):
        kernel(*refs[:ins], *refs[ins + len(held):])

    return pl.pallas_call(
        body,
        in_specs=[pl.BlockSpec(memory_space=pltpu.VMEM)] * (ins + len(held)),
        out_specs=[pl.BlockSpec(memory_space=pltpu.VMEM)] * len(outs),
        out_shape=outs,
        scratch_shapes=[pltpu.VMEM(shape, F32) for shape in scratch],
        input_output_aliases=aliases or {},
        compiler_params=pltpu.CompilerParams(vmem_limit_bytes=20 * 2**20),
    )(*args, *held)


def shaped(*shape):
    return jax.ShapeDtypeStruct(shape, F32)


def resident(*shape):
    return pltpu.VMEM(shape, F32)


def kept(x):
    return pltpu.with_memory_space_constraint(x, pltpu.VMEM)


def exchange(x, axis, stride, size):
    n = lax.axis_size(axis)
    return [x] + [lax.ppermute(x, axis, [(i, i ^ (k * stride)) for i in range(n)]) for k in range(1, size)]


def spread(x, axis, first, join):
    n = lax.axis_size(axis)
    stride, size = 1, min(first, n)
    while True:
        parts = exchange(x, axis, stride, size)
        stride *= size
        if stride == n:
            return parts
        x = join(parts)
        size = min(4, n // stride)


def ring_all_reduce(pieces, n):
    order = ring_order(n)
    up = [(order[p], order[(p + 1) % n]) for p in range(n)]
    down = [(b, a) for a, b in up]
    far = n // 2
    mine = [[pieces[2 * at], pieces[2 * at + 1]] for at in range(n)]

    def ahead(x):
        return lax.ppermute(x, "rows", up)

    def behind(x):
        return lax.ppermute(x, "rows", down)

    rise, fall = [ahead(mine[far][0]), None], [None, behind(mine[far][1])]
    for step in range(far - 1, 0, -1):
        rise = [ahead(m if r is None else m + r) for m, r in zip(mine[step], rise)]
        fall = [behind(m if f is None else m + f) for m, f in zip(mine[-step], fall)]
    own = [m + r + f for m, r, f in zip(mine[0], rise, fall)]
    found = {0: own}
    rise = fall = own
    for step in range(1, far):
        rise, fall = [ahead(r) for r in rise], [behind(f) for f in fall]
        found[n - step], found[step] = rise, fall
    found[far] = [ahead(rise[0]), behind(fall[1])]
    return [half for at in range(n) for half in found[at]]


def quarter_all_reduce(keep, send):
    quarter = keep.shape[0] // 2
    keep = keep + exchange(send, "cols", 1, 2)[1]
    own = keep[:quarter] + exchange(keep[quarter:], "cols", 2, 2)[1]
    beside = exchange(own, "cols", 2, 2)[1]
    return own, beside, exchange(jnp.concatenate([own, beside]), "cols", 1, 2)[1]


def per_device(crawl, bench, start_duals, row_cotangent, col_cotangent):
    rows, columns = crawl.shape[0], bench.shape[0]
    shift = (start_duals * KAPPA).reshape(1, columns)
    row_cotangent = row_cotangent.reshape(1, rows)
    col_cotangent = col_cotangent.reshape(1, columns)
    row, column, tall = shaped(1, rows), shaped(1, columns), (rows, LANES)
    tile_shape = resident(rows, columns)

    def over_cols(x, join=sum):
        return spread(x, "cols", 4, join)

    def over_rows(x, join=sum):
        return spread(x, "rows", 2, join)

    tile, top, local = call(row_level_kernel, [crawl, bench, shift], [tile_shape, row, row], [tall, tall])
    parts = over_cols(local, log_sum)
    level, local = call(
        functools.partial(column_level_kernel, len(parts)),
        [kept(tile), top, *parts, crawl, bench, shift], [row, column], [tall])
    parts = over_rows(local, log_sum)
    soft, mass, local = call(
        functools.partial(soft_kernel, len(parts)),
        [kept(tile), top, level, *parts, crawl, bench, shift], [tile_shape, column, row],
        [tall, tall, (1, columns)], aliases={0: 0})
    parts = over_cols(local)
    inverse, local = call(functools.partial(second_column_kernel, len(parts)), [kept(soft), *parts], [row, column], [tall], held=[bench, crawl])
    parts = over_rows(local)
    scaled2, local = call(
        functools.partial(second_row_kernel, len(parts)),
        [kept(soft), inverse, col_cotangent, *parts], [column, row], [tall], held=[bench, crawl])
    parts = over_cols(local)
    scaled, local = call(
        functools.partial(first_column_kernel, len(parts)),
        [kept(soft), inverse, row_cotangent, *parts], [row, column], [tall], held=[bench, crawl])
    parts = over_rows(local)
    back, local = call(functools.partial(first_row_kernel, len(parts)), [kept(soft), *parts], [column, row], [tall], held=[bench, crawl])
    parts = over_cols(local)
    n = lax.axis_size("rows")
    width = bench.shape[1]
    share = columns // n
    piece = shaped(share // 2, width)
    ahead = share % (2 * LANES) == 0
    *factors, = call(
        functools.partial(far_kernel, len(parts), n),
        [kept(soft), inverse, scaled2, back, mass, scaled, crawl, *parts],
        [shaped(*tall)] * 3 + [piece] * (2 * ahead), [(LANES, share)], held=[bench])
    factors, far = factors[:3], factors[3:]
    places = [at for at in range(n) if at != n // 2 or not ahead]
    keep, send, *pieces = call(
        functools.partial(gradient_kernel, n, places),
        [kept(soft), *factors, scaled2, back, mass, crawl, bench],
        [shaped(rows // 2, width)] * 2 + [piece] * (2 * len(places)), [(LANES, columns), (columns, LANES), tall])
    if ahead:
        pieces[n:n] = far
    pieces = ring_all_reduce(pieces, n)
    quarters = quarter_all_reduce(keep, send)
    crawl_grad, bench_grad = pl.pallas_call(
        functools.partial(placing_kernel, n),
        in_specs=[pl.BlockSpec(memory_space=pltpu.VMEM)] * (3 + len(pieces)),
        out_specs=[pl.BlockSpec(memory_space=pl.ANY)] * 2,
        out_shape=[shaped(rows, width), shaped(columns, width)],
        scratch_shapes=[pltpu.SemaphoreType.DMA((4 + len(pieces),))],
    )(*quarters, *pieces)
    return (crawl_grad, bench_grad)


def solution(mesh):
    placed = (P("rows", None), P("cols", None), P("cols"), P("rows"), P("cols"))
    return jax.shard_map(
        per_device,
        mesh=mesh,
        in_specs=placed,
        out_specs=(P("rows", None), P("cols", None)),
        check_vma=False,
    )
```

```python
import functools
import math

import jax
import jax.numpy as jnp
from jax import lax
from jax.experimental import pallas as pl
from jax.experimental.pallas import tpu as pltpu
from jax.sharding import PartitionSpec as P

EPSILON = 0.05
KAPPA = math.log2(math.e) / EPSILON
LOWEST = -90.0
LANES = 128
WIDE = 512
TALL = 256
LIMIT = 20 * 2**20
F32 = jnp.float32


def transposed_dot(a, b):
    return lax.dot_general(a, b, (((1,), (1,)), ((), ())), preferred_element_type=F32)


def column_form(row):
    return jnp.transpose(jnp.broadcast_to(row, (LANES, row.shape[1])))


def row_form(partial):
    return jnp.sum(jnp.transpose(partial), axis=0, keepdims=True)


def log_sum(parts):
    top = functools.reduce(jnp.maximum, parts)
    return top + jnp.log2(sum(jnp.exp2(p - top) for p in parts))


def row_sums(tile_ref, weights_ref, partial_ref):
    height = 64

    def body(block, _):
        rows = pl.ds(pl.multiple_of(block * height, height), height)
        acc = jnp.zeros((height, LANES), F32)
        for at in range(0, tile_ref.shape[1], LANES):
            acc += tile_ref[rows, at:at + LANES] * weights_ref[:, at:at + LANES]
        partial_ref[rows, :] = acc
        return _

    lax.fori_loop(0, tile_ref.shape[0] // height, body, 0)
    return row_form(partial_ref[...])


def column_sums(tile_ref, weights_ref, out_ref):
    starts = range(0, tile_ref.shape[1], LANES)

    def body(block, accs):
        for half in range(2):
            rows = pl.ds(pl.multiple_of(block * 16 + half * 8, 8), 8)
            weights = weights_ref[rows, :]
            accs = tuple(acc + tile_ref[rows, at:at + LANES] * weights for acc, at in zip(accs, starts))
        return accs

    accs = lax.fori_loop(0, tile_ref.shape[0] // 16, body, tuple(jnp.zeros((8, LANES), F32) for _ in starts))
    for acc, at in zip(accs, starts):
        out_ref[:, at:at + LANES] = jnp.sum(acc, axis=0, keepdims=True)


def exponent_block(crawl_ref, bench_ref, shift_ref, rows, columns):
    scores = transposed_dot(crawl_ref[rows, :], bench_ref[columns, :])
    return scores * KAPPA + shift_ref[:, columns]


def row_level_kernel(crawl_hbm, bench_hbm, duals_hbm, tile_ref, top_ref, level_ref, crawl_ref, bench_ref, shift_ref,
                     top_scratch, sum_scratch, sems):
    height = 64
    chunks = 4
    part = bench_ref.shape[0] // chunks
    copies = [pltpu.make_async_copy(crawl_hbm, crawl_ref, sems.at[chunks]),
              pltpu.make_async_copy(duals_hbm, shift_ref, sems.at[chunks + 1])]
    fetches = [
        pltpu.make_async_copy(bench_hbm.at[k * part:(k + 1) * part], bench_ref.at[k * part:(k + 1) * part], sems.at[k])
        for k in range(chunks)]
    for copy in (*copies, *fetches):
        copy.start()
    for copy in copies:
        copy.wait()
    shift_ref[...] = shift_ref[...] * KAPPA

    def fill(block, _, fetches=()):
        rows = pl.ds(pl.multiple_of(block * TALL, TALL), TALL)
        top = jnp.full((TALL, LANES), -jnp.inf, F32)
        for at in range(0, tile_ref.shape[1], WIDE):
            for k, fetch in enumerate(fetches):
                if at <= k * part < at + WIDE:
                    fetch.wait()
            exponent = exponent_block(crawl_ref, bench_ref, shift_ref, rows, pl.ds(at, WIDE))
            tile_ref[rows, at:at + WIDE] = exponent
            for lane in range(0, WIDE, LANES):
                top = jnp.maximum(top, exponent[:, lane:lane + LANES])
        top_scratch[rows, :] = top
        return _

    fill(0, 0, fetches)
    lax.fori_loop(1, tile_ref.shape[0] // TALL, fill, 0)

    def power(block, _):
        rows = pl.ds(pl.multiple_of(block * height, height), height)
        top = jnp.broadcast_to(jnp.max(top_scratch[rows, :], axis=1, keepdims=True), (height, LANES))
        acc = jnp.zeros((height, LANES), F32)
        for at in range(0, tile_ref.shape[1], LANES):
            value = jnp.exp2(tile_ref[rows, at:at + LANES] - top)
            tile_ref[rows, at:at + LANES] = value
            acc += value
        top_scratch[rows, :] = top
        sum_scratch[rows, :] = acc
        return _

    lax.fori_loop(0, tile_ref.shape[0] // height, power, 0)
    top = jnp.transpose(top_scratch[...])[0:1, :]
    top_ref[...] = top
    level_ref[...] = top + jnp.log2(row_form(sum_scratch[...]))


def column_level_kernel(parts, tile_ref, top_ref, *refs):
    part_refs, (crawl_ref, bench_ref, shift_ref, level_ref, out_ref, weights) = refs[:parts], refs[parts:]
    level = log_sum([p[...] for p in part_refs])
    level_ref[...] = level
    weights[...] = column_form(jnp.exp2(top_ref[...] - level))
    column_sums(tile_ref, weights, out_ref)
    out_ref[...] = jnp.log2(out_ref[...])

    @pl.when(jnp.min(out_ref[...]) < LOWEST)
    def _():
        weights[...] = column_form(level)
        blocks = tile_ref.shape[0] // TALL

        def column_block(column, _):
            columns = pl.ds(pl.multiple_of(column * WIDE, WIDE), WIDE)

            def logs(block):
                rows = pl.ds(pl.multiple_of(block * TALL, TALL), TALL)
                return exponent_block(crawl_ref, bench_ref, shift_ref, rows, columns) - weights[rows, 0:1]

            top = lax.fori_loop(
                0, blocks, lambda b, t: jnp.maximum(t, jnp.max(logs(b), axis=0, keepdims=True)),
                jnp.full((1, WIDE), -jnp.inf, F32))
            total = lax.fori_loop(
                0, blocks, lambda b, t: t + jnp.sum(jnp.exp2(logs(b) - top), axis=0, keepdims=True),
                jnp.zeros((1, WIDE), F32))
            out_ref[:, columns] = top + jnp.log2(total)
            return _

        lax.fori_loop(0, tile_ref.shape[1] // WIDE, column_block, 0)


def soft_kernel(parts, tile_ref, top_ref, level_ref, *refs):
    part_refs = refs[:parts]
    crawl_ref, bench_ref, shift_ref, soft_ref, mass_ref, sums_ref, partial, weights, scale = refs[parts:]
    logs = log_sum([p[...] for p in part_refs])
    mass_ref[...] = jnp.exp2(logs)
    lowest = jnp.min(logs)
    height = 64

    @pl.when(lowest >= LOWEST)
    def _():
        weights[...] = column_form(jnp.exp2(top_ref[...] - level_ref[...]))
        scale[...] = jnp.exp2(-logs)

        def body(block, _):
            rows = pl.ds(pl.multiple_of(block * height, height), height)
            weight = weights[rows, :]
            acc = jnp.zeros((height, LANES), F32)
            for at in range(0, tile_ref.shape[1], LANES):
                value = tile_ref[rows, at:at + LANES] * weight * scale[:, at:at + LANES]
                soft_ref[rows, at:at + LANES] = value
                acc += value
            partial[rows, :] = acc
            return _

        lax.fori_loop(0, tile_ref.shape[0] // height, body, 0)

    @pl.when(lowest < LOWEST)
    def _():
        weights[...] = column_form(level_ref[...])
        scale[...] = logs
        partial[...] = jnp.zeros_like(partial)

        def body(block, _):
            rows = pl.ds(pl.multiple_of(block * TALL, TALL), TALL)
            level = weights[rows, 0:1]

            def column_block(column, _):
                columns = pl.ds(pl.multiple_of(column * WIDE, WIDE), WIDE)
                exponent = exponent_block(crawl_ref, bench_ref, shift_ref, rows, columns)
                value = jnp.exp2(exponent - level - scale[:, columns])
                soft_ref[rows, columns] = value
                partial[rows, :] += sum(value[:, lane:lane + LANES] for lane in range(0, WIDE, LANES))
                return _

            return lax.fori_loop(0, tile_ref.shape[1] // WIDE, column_block, _)

        lax.fori_loop(0, tile_ref.shape[0] // TALL, body, 0)

    sums_ref[...] = row_form(partial[...])


def second_column_kernel(parts, soft_ref, *refs):
    part_refs, (inverse_ref, out_ref, weights) = refs[:parts], refs[parts:]
    inverse = 1.0 / sum(p[...] for p in part_refs)
    inverse_ref[...] = inverse
    weights[...] = column_form(inverse)
    column_sums(soft_ref, weights, out_ref)


def second_row_kernel(parts, soft_ref, inverse_ref, cotangent_ref, *refs):
    part_refs, (scaled_ref, out_ref, partial) = refs[:parts], refs[parts:]
    scaled_ref[...] = cotangent_ref[...] / sum(p[...] for p in part_refs)
    out_ref[...] = row_sums(soft_ref, scaled_ref, partial) * inverse_ref[...]


def first_column_kernel(parts, soft_ref, inverse_ref, cotangent_ref, *refs):
    part_refs, (scaled_ref, out_ref, weights) = refs[:parts], refs[parts:]
    scaled = (cotangent_ref[...] - sum(p[...] for p in part_refs)) * inverse_ref[...]
    scaled_ref[...] = scaled
    weights[...] = column_form(-scaled)
    column_sums(soft_ref, weights, out_ref)


def first_row_kernel(parts, soft_ref, *refs):
    part_refs, (back_ref, out_ref, partial) = refs[:parts], refs[parts:]
    back_ref[...] = sum(p[...] for p in part_refs)
    out_ref[...] = -row_sums(soft_ref, back_ref, partial)


def ring_order(n):
    return [*range(0, n, 2), *range(n - 1, 0, -2)]


def ring_share(n, at):
    me = lax.axis_index("rows")
    place = lax.rem(lax.select(lax.rem(me, 2) == 0, me // 2, n - 1 - me // 2) + at, n)
    return lax.select(place < n // 2, 2 * place, 2 * (n - 1 - place) + 1)


def far_kernel(parts, n, soft_ref, inverse_ref, scaled2_ref, back_ref, mass_ref, scaled_ref, crawl_ref, *refs):
    part_refs, (first, second, third, *piece_refs, flat) = refs[:parts], refs[parts:]
    first[...] = column_form(-inverse_ref[...])
    second[...] = column_form(-scaled_ref[...])
    third[...] = column_form(-sum(p[...] for p in part_refs))
    if not piece_refs:
        return
    width = flat.shape[1]
    start = ring_share(n, n // 2) * width
    flat[...] = jnp.zeros_like(flat)

    def body(block, _):
        rows = pl.ds(pl.multiple_of(block * TALL, TALL), TALL)
        a, b, c = first[rows, :], second[rows, :], third[rows, :]
        pieces = []
        for lane in range(0, width, LANES):
            span = pl.ds(pl.multiple_of(start + lane, LANES), LANES)
            factor = a * scaled2_ref[:, span] + b + (c * mass_ref[:, span] - back_ref[:, span])
            pieces.append((soft_ref[rows, span] * factor).astype(jnp.bfloat16))
        grad = jnp.concatenate(pieces, axis=1)
        flat[...] += lax.dot_general(crawl_ref[rows, :], grad, (((0,), (0,)), ((), ())), preferred_element_type=F32)
        return _

    lax.fori_loop(0, soft_ref.shape[0] // TALL, body, 0)
    half = width // 2
    for k, piece in enumerate(piece_refs):
        piece[...] = jnp.transpose(flat[:, k * half:(k + 1) * half])


def gradient_kernel(n, places, soft_ref, first, second, third, scaled2_ref, back_ref, mass_ref, crawl_ref, bench_ref, *refs):
    keep_ref, send_ref, *piece_refs, flat, whole, total = refs
    flat[...] = jnp.zeros_like(flat)

    def body(block, _):
        rows = pl.ds(pl.multiple_of(block * TALL, TALL), TALL)
        a, b, c = first[rows, :], second[rows, :], third[rows, :]
        x = crawl_ref[rows, :]
        acc = jnp.zeros((TALL, LANES), F32)
        for at in range(0, soft_ref.shape[1], WIDE):
            pieces = []
            for lane in range(at, at + WIDE, LANES):
                span = slice(lane, lane + LANES)
                factor = a * scaled2_ref[:, span] + b + (c * mass_ref[:, span] - back_ref[:, span])
                pieces.append((soft_ref[rows, span] * factor).astype(jnp.bfloat16))
            grad = jnp.concatenate(pieces, axis=1)
            acc += jnp.dot(grad, bench_ref[at:at + WIDE, :], preferred_element_type=F32)
            flat[:, at:at + WIDE] += lax.dot_general(x, grad, (((0,), (0,)), ((), ())), preferred_element_type=F32)
        total[rows, :] = acc
        return _

    lax.fori_loop(0, soft_ref.shape[0] // TALL, body, 0)
    me = lax.axis_index("cols")
    quarter = total.shape[0] // 4
    for k, (ref, low) in enumerate(((keep_ref, 0), (send_ref, 0), (keep_ref, quarter), (send_ref, quarter))):
        start = pl.multiple_of(lax.bitwise_xor(me, k) * quarter, quarter)
        ref[low:low + quarter, :] = total[pl.ds(start, quarter), :]
    whole[...] = jnp.transpose(flat[...])
    height = piece_refs[0].shape[0]
    for k, piece in enumerate(piece_refs):
        start = ring_share(n, places[k // 2]) * 2 * height + k % 2 * height
        piece[...] = whole[pl.ds(pl.multiple_of(start, height), height), :]


def placing_kernel(n, *refs):
    (own_ref, beside_ref, pair_ref, *pieces), (crawl_out, bench_out, sems) = refs[:-3], refs[-3:]
    me = lax.axis_index("cols")
    quarter = own_ref.shape[0]
    moves = []
    for k, piece in ((0, own_ref), (2, beside_ref), (1, pair_ref.at[:quarter]), (3, pair_ref.at[quarter:])):
        start = pl.multiple_of(lax.bitwise_xor(me, k) * quarter, quarter)
        moves.append((piece, crawl_out.at[pl.ds(start, quarter)]))
    height = pieces[0].shape[0]
    for at, piece in enumerate(pieces):
        start = pl.multiple_of(ring_share(n, at // 2) * 2 * height + at % 2 * height, height)
        moves.append((piece, bench_out.at[pl.ds(start, height)]))
    copies = [pltpu.make_async_copy(source, target, sems.at[k]) for k, (source, target) in enumerate(moves)]
    for copy in copies:
        copy.start()
    for copy in copies:
        copy.wait()


def call(kernel, args, outs, scratch, aliases=None):
    return pl.pallas_call(
        kernel,
        in_specs=[pl.BlockSpec(memory_space=pltpu.VMEM)] * len(args),
        out_specs=[pl.BlockSpec(memory_space=pltpu.VMEM)] * len(outs),
        out_shape=outs,
        scratch_shapes=[pltpu.VMEM(shape, F32) for shape in scratch],
        input_output_aliases=aliases or {},
        compiler_params=pltpu.CompilerParams(vmem_limit_bytes=LIMIT),
    )(*args)


def shaped(*shape, kind=F32):
    return jax.ShapeDtypeStruct(shape, kind)


def resident(*shape, kind=F32):
    return pltpu.VMEM(shape, kind)


def kept(x):
    return pltpu.with_memory_space_constraint(x, pltpu.VMEM)


def exchange(x, axis, stride, size):
    n = lax.axis_size(axis)
    return [x] + [lax.ppermute(x, axis, [(i, i ^ (k * stride)) for i in range(n)]) for k in range(1, size)]


def spread(x, axis, first, join):
    n = lax.axis_size(axis)
    stride, size = 1, min(first, n)
    while True:
        parts = exchange(x, axis, stride, size)
        stride *= size
        if stride == n:
            return parts
        x = join(parts)
        size = min(4, n // stride)


def ring_all_reduce(pieces, n):
    order = ring_order(n)
    up = [(order[p], order[(p + 1) % n]) for p in range(n)]
    down = [(b, a) for a, b in up]
    far = n // 2
    mine = [[pieces[2 * at], pieces[2 * at + 1]] for at in range(n)]

    def ahead(x):
        return lax.ppermute(x, "rows", up)

    def behind(x):
        return lax.ppermute(x, "rows", down)

    rise, fall = [ahead(mine[far][0]), None], [None, behind(mine[far][1])]
    for step in range(far - 1, 0, -1):
        rise = [ahead(m if r is None else m + r) for m, r in zip(mine[step], rise)]
        fall = [behind(m if f is None else m + f) for m, f in zip(mine[-step], fall)]
    own = [m + r + f for m, r, f in zip(mine[0], rise, fall)]
    found = {0: own}
    rise = fall = own
    for step in range(1, far):
        rise, fall = [ahead(r) for r in rise], [behind(f) for f in fall]
        found[n - step], found[step] = rise, fall
    found[far] = [ahead(rise[0]), behind(fall[1])]
    return [half for at in range(n) for half in found[at]]


def quarter_all_reduce(keep, send):
    quarter = keep.shape[0] // 2
    keep = keep + exchange(send, "cols", 1, 2)[1]
    own = keep[:quarter] + exchange(keep[quarter:], "cols", 2, 2)[1]
    beside = exchange(own, "cols", 2, 2)[1]
    return own, beside, exchange(jnp.concatenate([own, beside]), "cols", 1, 2)[1]


def per_device(crawl, bench, start_duals, row_cotangent, col_cotangent):
    rows, columns = crawl.shape[0], bench.shape[0]
    row_cotangent = row_cotangent.reshape(1, rows)
    col_cotangent = col_cotangent.reshape(1, columns)
    row, column, tall = shaped(1, rows), shaped(1, columns), (rows, LANES)
    tile_shape = resident(rows, columns)

    def over_cols(x, join=sum):
        return spread(x, "cols", 4, join)

    def over_rows(x, join=sum):
        return spread(x, "rows", 4, join)

    tile, top, local, crawl, bench, shift = pl.pallas_call(
        row_level_kernel,
        in_specs=[pl.BlockSpec(memory_space=pltpu.HBM)] * 3,
        out_specs=[pl.BlockSpec(memory_space=pltpu.VMEM)] * 6,
        out_shape=[tile_shape, row, row, resident(*crawl.shape, kind=crawl.dtype), resident(*bench.shape, kind=bench.dtype),
                   resident(1, columns)],
        scratch_shapes=[pltpu.VMEM(tall, F32)] * 2 + [pltpu.SemaphoreType.DMA((6,))],
        compiler_params=pltpu.CompilerParams(vmem_limit_bytes=LIMIT),
    )(*(pltpu.with_memory_space_constraint(x, pltpu.HBM) for x in (crawl, bench, start_duals.reshape(1, columns))))
    crawl, bench, shift = kept(crawl), kept(bench), kept(shift)
    parts = over_cols(local, log_sum)
    level, local = call(
        functools.partial(column_level_kernel, len(parts)),
        [kept(tile), top, *parts, crawl, bench, shift], [row, column], [tall])
    parts = over_rows(local, log_sum)
    soft, mass, local = call(
        functools.partial(soft_kernel, len(parts)),
        [kept(tile), top, level, *parts, crawl, bench, shift], [tile_shape, column, row],
        [tall, tall, (1, columns)], aliases={0: 0})
    parts = over_cols(local)
    inverse, local = call(functools.partial(second_column_kernel, len(parts)), [kept(soft), *parts], [row, column], [tall])
    parts = over_rows(local)
    scaled2, local = call(
        functools.partial(second_row_kernel, len(parts)),
        [kept(soft), inverse, col_cotangent, *parts], [column, row], [tall])
    parts = over_cols(local)
    scaled, local = call(
        functools.partial(first_column_kernel, len(parts)),
        [kept(soft), inverse, row_cotangent, *parts], [row, column], [tall])
    parts = over_rows(local)
    back, local = call(functools.partial(first_row_kernel, len(parts)), [kept(soft), *parts], [column, row], [tall])
    parts = over_cols(local)
    n = lax.axis_size("rows")
    width = bench.shape[1]
    share = columns // n
    piece = shaped(share // 2, width)
    ahead = share % (2 * LANES) == 0
    *factors, = call(
        functools.partial(far_kernel, len(parts), n),
        [kept(soft), inverse, scaled2, back, mass, scaled, crawl, *parts],
        [shaped(*tall)] * 3 + [piece] * (2 * ahead), [(LANES, share)])
    factors, far = factors[:3], factors[3:]
    places = [at for at in range(n) if at != n // 2 or not ahead]
    keep, send, *pieces = call(
        functools.partial(gradient_kernel, n, places),
        [kept(soft), *factors, scaled2, back, mass, crawl, bench],
        [shaped(rows // 2, width)] * 2 + [piece] * (2 * len(places)), [(LANES, columns), (columns, LANES), tall])
    if ahead:
        pieces[n:n] = far
    pieces = ring_all_reduce(pieces, n)
    quarters = quarter_all_reduce(keep, send)
    crawl_grad, bench_grad = pl.pallas_call(
        functools.partial(placing_kernel, n),
        in_specs=[pl.BlockSpec(memory_space=pltpu.VMEM)] * (3 + len(pieces)),
        out_specs=[pl.BlockSpec(memory_space=pl.ANY)] * 2,
        out_shape=[shaped(rows, width), shaped(columns, width)],
        scratch_shapes=[pltpu.SemaphoreType.DMA((4 + len(pieces),))],
        compiler_params=pltpu.CompilerParams(vmem_limit_bytes=LIMIT),
    )(*map(kept, (*quarters, *pieces)))
    return (crawl_grad, bench_grad)


def solution(mesh):
    placed = (P("rows", None), P("cols", None), P("cols"), P("rows"), P("cols"))
    return jax.shard_map(
        per_device,
        mesh=mesh,
        in_specs=placed,
        out_specs=(P("rows", None), P("cols", None)),
        check_vma=False,
    )
```

```python
import functools
import math

import jax
import jax.numpy as jnp
from jax import lax
from jax.experimental import pallas as pl
from jax.experimental.pallas import tpu as pltpu
from jax.sharding import PartitionSpec as P

EPSILON = 0.05
KAPPA = math.log2(math.e) / EPSILON
LOWEST = -90.0
LANES = 128
WIDE = 512
TALL = 256
LIMIT = 20 * 2**20
F32 = jnp.float32


def transposed_dot(a, b):
    return lax.dot_general(a, b, (((1,), (1,)), ((), ())), preferred_element_type=F32)


def column_form(row):
    return jnp.transpose(jnp.broadcast_to(row, (LANES, row.shape[1])))


def row_form(partial):
    return jnp.sum(jnp.transpose(partial), axis=0, keepdims=True)


def log_sum(parts):
    top = functools.reduce(jnp.maximum, parts)
    return top + jnp.log2(sum(jnp.exp2(p - top) for p in parts))


def row_sums(tile_ref, weights_ref, partial_ref):
    height = 64

    def body(block, _):
        rows = pl.ds(pl.multiple_of(block * height, height), height)
        acc = jnp.zeros((height, LANES), F32)
        for at in range(0, tile_ref.shape[1], LANES):
            acc += tile_ref[rows, at:at + LANES] * weights_ref[:, at:at + LANES]
        partial_ref[rows, :] = acc
        return _

    lax.fori_loop(0, tile_ref.shape[0] // height, body, 0)
    return row_form(partial_ref[...])


def column_sums(tile_ref, weights_ref, out_ref):
    starts = range(0, tile_ref.shape[1], LANES)

    def body(block, accs):
        for half in range(2):
            rows = pl.ds(pl.multiple_of(block * 16 + half * 8, 8), 8)
            weights = weights_ref[rows, :]
            accs = tuple(acc + tile_ref[rows, at:at + LANES] * weights for acc, at in zip(accs, starts))
        return accs

    accs = lax.fori_loop(0, tile_ref.shape[0] // 16, body, tuple(jnp.zeros((8, LANES), F32) for _ in starts))
    for acc, at in zip(accs, starts):
        out_ref[:, at:at + LANES] = jnp.sum(acc, axis=0, keepdims=True)


def exponent_block(crawl_ref, bench_ref, shift_ref, rows, columns):
    scores = transposed_dot(crawl_ref[rows, :], bench_ref[columns, :])
    return scores * KAPPA + shift_ref[:, columns]


def row_level_kernel(crawl_hbm, bench_hbm, duals_hbm, tile_ref, top_ref, level_ref, crawl_ref, bench_ref, shift_ref,
                     top_scratch, sum_scratch, sems):
    height = 64
    chunks = 4
    part = bench_ref.shape[0] // chunks
    copies = [pltpu.make_async_copy(crawl_hbm, crawl_ref, sems.at[chunks]),
              pltpu.make_async_copy(duals_hbm, shift_ref, sems.at[chunks + 1])]
    fetches = [
        pltpu.make_async_copy(bench_hbm.at[k * part:(k + 1) * part], bench_ref.at[k * part:(k + 1) * part], sems.at[k])
        for k in range(chunks)]
    for copy in (*copies, *fetches):
        copy.start()
    for copy in copies:
        copy.wait()
    shift_ref[...] = shift_ref[...] * KAPPA

    def fill(block, _, fetches=()):
        rows = pl.ds(pl.multiple_of(block * TALL, TALL), TALL)
        top = jnp.full((TALL, LANES), -jnp.inf, F32)
        for at in range(0, tile_ref.shape[1], WIDE):
            for k, fetch in enumerate(fetches):
                if at <= k * part < at + WIDE:
                    fetch.wait()
            exponent = exponent_block(crawl_ref, bench_ref, shift_ref, rows, pl.ds(at, WIDE))
            tile_ref[rows, at:at + WIDE] = exponent
            for lane in range(0, WIDE, LANES):
                top = jnp.maximum(top, exponent[:, lane:lane + LANES])
        top_scratch[rows, :] = top
        return _

    fill(0, 0, fetches)
    lax.fori_loop(1, tile_ref.shape[0] // TALL, fill, 0)

    def power(block, _):
        rows = pl.ds(pl.multiple_of(block * height, height), height)
        top = jnp.broadcast_to(jnp.max(top_scratch[rows, :], axis=1, keepdims=True), (height, LANES))
        acc = jnp.zeros((height, LANES), F32)
        for at in range(0, tile_ref.shape[1], LANES):
            value = jnp.exp2(tile_ref[rows, at:at + LANES] - top)
            tile_ref[rows, at:at + LANES] = value
            acc += value
        top_scratch[rows, :] = top
        sum_scratch[rows, :] = acc
        return _

    lax.fori_loop(0, tile_ref.shape[0] // height, power, 0)
    top = jnp.transpose(top_scratch[...])[0:1, :]
    top_ref[...] = top
    level_ref[...] = top + jnp.log2(row_form(sum_scratch[...]))


def column_level_kernel(parts, tile_ref, top_ref, *refs):
    part_refs, (crawl_ref, bench_ref, shift_ref, level_ref, out_ref, weights) = refs[:parts], refs[parts:]
    level = log_sum([p[...] for p in part_refs])
    level_ref[...] = level
    weights[...] = column_form(jnp.exp2(top_ref[...] - level))
    column_sums(tile_ref, weights, out_ref)
    out_ref[...] = jnp.log2(out_ref[...])

    @pl.when(jnp.min(out_ref[...]) < LOWEST)
    def _():
        weights[...] = column_form(level)
        blocks = tile_ref.shape[0] // TALL

        def column_block(column, _):
            columns = pl.ds(pl.multiple_of(column * WIDE, WIDE), WIDE)

            def logs(block):
                rows = pl.ds(pl.multiple_of(block * TALL, TALL), TALL)
                return exponent_block(crawl_ref, bench_ref, shift_ref, rows, columns) - weights[rows, 0:1]

            top = lax.fori_loop(
                0, blocks, lambda b, t: jnp.maximum(t, jnp.max(logs(b), axis=0, keepdims=True)),
                jnp.full((1, WIDE), -jnp.inf, F32))
            total = lax.fori_loop(
                0, blocks, lambda b, t: t + jnp.sum(jnp.exp2(logs(b) - top), axis=0, keepdims=True),
                jnp.zeros((1, WIDE), F32))
            out_ref[:, columns] = top + jnp.log2(total)
            return _

        lax.fori_loop(0, tile_ref.shape[1] // WIDE, column_block, 0)


def soft_kernel(parts, tile_ref, top_ref, level_ref, *refs):
    part_refs = refs[:parts]
    crawl_ref, bench_ref, shift_ref, soft_ref, mass_ref, sums_ref, partial, weights, scale = refs[parts:]
    logs = log_sum([p[...] for p in part_refs])
    mass_ref[...] = jnp.exp2(logs)
    lowest = jnp.min(logs)
    height = 64

    @pl.when(lowest >= LOWEST)
    def _():
        weights[...] = column_form(jnp.exp2(top_ref[...] - level_ref[...]))
        scale[...] = jnp.exp2(-logs)

        def body(block, _):
            rows = pl.ds(pl.multiple_of(block * height, height), height)
            weight = weights[rows, :]
            acc = jnp.zeros((height, LANES), F32)
            for at in range(0, tile_ref.shape[1], LANES):
                value = tile_ref[rows, at:at + LANES] * weight * scale[:, at:at + LANES]
                soft_ref[rows, at:at + LANES] = value
                acc += value
            partial[rows, :] = acc
            return _

        lax.fori_loop(0, tile_ref.shape[0] // height, body, 0)

    @pl.when(lowest < LOWEST)
    def _():
        weights[...] = column_form(level_ref[...])
        scale[...] = logs
        partial[...] = jnp.zeros_like(partial)

        def body(block, _):
            rows = pl.ds(pl.multiple_of(block * TALL, TALL), TALL)
            level = weights[rows, 0:1]

            def column_block(column, _):
                columns = pl.ds(pl.multiple_of(column * WIDE, WIDE), WIDE)
                exponent = exponent_block(crawl_ref, bench_ref, shift_ref, rows, columns)
                value = jnp.exp2(exponent - level - scale[:, columns])
                soft_ref[rows, columns] = value
                partial[rows, :] += sum(value[:, lane:lane + LANES] for lane in range(0, WIDE, LANES))
                return _

            return lax.fori_loop(0, tile_ref.shape[1] // WIDE, column_block, _)

        lax.fori_loop(0, tile_ref.shape[0] // TALL, body, 0)

    sums_ref[...] = row_form(partial[...])


def second_column_kernel(parts, soft_ref, *refs):
    part_refs, (inverse_ref, out_ref, weights) = refs[:parts], refs[parts:]
    inverse = 1.0 / sum(p[...] for p in part_refs)
    inverse_ref[...] = inverse
    weights[...] = column_form(inverse)
    column_sums(soft_ref, weights, out_ref)


def second_row_kernel(parts, soft_ref, inverse_ref, cotangent_ref, *refs):
    part_refs, (scaled_ref, out_ref, partial) = refs[:parts], refs[parts:]
    scaled_ref[...] = cotangent_ref[...] / sum(p[...] for p in part_refs)
    out_ref[...] = row_sums(soft_ref, scaled_ref, partial) * inverse_ref[...]


def first_column_kernel(parts, soft_ref, inverse_ref, cotangent_ref, *refs):
    part_refs, (scaled_ref, out_ref, weights) = refs[:parts], refs[parts:]
    scaled = (cotangent_ref[...] - sum(p[...] for p in part_refs)) * inverse_ref[...]
    scaled_ref[...] = scaled
    weights[...] = column_form(-scaled)
    column_sums(soft_ref, weights, out_ref)


def first_row_kernel(parts, soft_ref, *refs):
    part_refs, (back_ref, out_ref, partial) = refs[:parts], refs[parts:]
    back_ref[...] = sum(p[...] for p in part_refs)
    out_ref[...] = -row_sums(soft_ref, back_ref, partial)


def ring_order(n):
    return [*range(0, n, 2), *range(n - 1, 0, -2)]


def ring_share(n, at):
    me = lax.axis_index("rows")
    place = lax.rem(lax.select(lax.rem(me, 2) == 0, me // 2, n - 1 - me // 2) + at, n)
    return lax.select(place < n // 2, 2 * place, 2 * (n - 1 - place) + 1)


def far_kernel(parts, n, soft_ref, inverse_ref, scaled2_ref, back_ref, mass_ref, scaled_ref, crawl_ref, *refs):
    part_refs, (first, second, third, *piece_refs, flat) = refs[:parts], refs[parts:]
    first[...] = column_form(-inverse_ref[...])
    second[...] = column_form(-scaled_ref[...])
    third[...] = column_form(-sum(p[...] for p in part_refs))
    if not piece_refs:
        return
    width = flat.shape[1]
    start = ring_share(n, n // 2) * width
    flat[...] = jnp.zeros_like(flat)

    def body(block, _):
        rows = pl.ds(pl.multiple_of(block * TALL, TALL), TALL)
        a, b, c = first[rows, :], second[rows, :], third[rows, :]
        pieces = []
        for lane in range(0, width, LANES):
            span = pl.ds(pl.multiple_of(start + lane, LANES), LANES)
            factor = a * scaled2_ref[:, span] + b + (c * mass_ref[:, span] - back_ref[:, span])
            pieces.append((soft_ref[rows, span] * factor).astype(jnp.bfloat16))
        grad = jnp.concatenate(pieces, axis=1)
        flat[...] += lax.dot_general(crawl_ref[rows, :], grad, (((0,), (0,)), ((), ())), preferred_element_type=F32)
        return _

    lax.fori_loop(0, soft_ref.shape[0] // TALL, body, 0)
    half = width // 2
    for k, piece in enumerate(piece_refs):
        piece[...] = jnp.transpose(flat[:, k * half:(k + 1) * half])


def gradient_kernel(n, places, soft_ref, first, second, third, scaled2_ref, back_ref, mass_ref, crawl_ref, bench_ref, *refs):
    keep_ref, send_ref, *piece_refs, flat, whole, total = refs
    flat[...] = jnp.zeros_like(flat)

    def body(block, _):
        rows = pl.ds(pl.multiple_of(block * TALL, TALL), TALL)
        a, b, c = first[rows, :], second[rows, :], third[rows, :]
        x = crawl_ref[rows, :]
        acc = jnp.zeros((TALL, LANES), F32)
        for at in range(0, soft_ref.shape[1], WIDE):
            pieces = []
            for lane in range(at, at + WIDE, LANES):
                span = slice(lane, lane + LANES)
                factor = a * scaled2_ref[:, span] + b + (c * mass_ref[:, span] - back_ref[:, span])
                pieces.append((soft_ref[rows, span] * factor).astype(jnp.bfloat16))
            grad = jnp.concatenate(pieces, axis=1)
            acc += jnp.dot(grad, bench_ref[at:at + WIDE, :], preferred_element_type=F32)
            flat[:, at:at + WIDE] += lax.dot_general(x, grad, (((0,), (0,)), ((), ())), preferred_element_type=F32)
        total[rows, :] = acc
        return _

    lax.fori_loop(0, soft_ref.shape[0] // TALL, body, 0)
    me = lax.axis_index("cols")
    quarter = total.shape[0] // 4
    for k, (ref, low) in enumerate(((keep_ref, 0), (send_ref, 0), (keep_ref, quarter), (send_ref, quarter))):
        start = pl.multiple_of(lax.bitwise_xor(me, k) * quarter, quarter)
        ref[low:low + quarter, :] = total[pl.ds(start, quarter), :]
    whole[...] = jnp.transpose(flat[...])
    height = piece_refs[0].shape[0]
    for k, piece in enumerate(piece_refs):
        start = ring_share(n, places[k // 2]) * 2 * height + k % 2 * height
        piece[...] = whole[pl.ds(pl.multiple_of(start, height), height), :]


def placing_kernel(n, *refs):
    (own_ref, beside_ref, pair_ref, *pieces), (crawl_out, bench_out, sems) = refs[:-3], refs[-3:]
    me = lax.axis_index("cols")
    quarter = own_ref.shape[0]
    moves = []
    for k, piece in ((0, own_ref), (2, beside_ref), (1, pair_ref.at[:quarter]), (3, pair_ref.at[quarter:])):
        start = pl.multiple_of(lax.bitwise_xor(me, k) * quarter, quarter)
        moves.append((piece, crawl_out.at[pl.ds(start, quarter)]))
    height = pieces[0].shape[0]
    for at, piece in enumerate(pieces):
        start = pl.multiple_of(ring_share(n, at // 2) * 2 * height + at % 2 * height, height)
        moves.append((piece, bench_out.at[pl.ds(start, height)]))
    copies = [pltpu.make_async_copy(source, target, sems.at[k]) for k, (source, target) in enumerate(moves)]
    for copy in copies:
        copy.start()
    for copy in copies:
        copy.wait()


def call(kernel, args, outs, scratch, aliases=None):
    return pl.pallas_call(
        kernel,
        in_specs=[pl.BlockSpec(memory_space=pltpu.VMEM)] * len(args),
        out_specs=[pl.BlockSpec(memory_space=pltpu.VMEM)] * len(outs),
        out_shape=outs,
        scratch_shapes=[pltpu.VMEM(shape, F32) for shape in scratch],
        input_output_aliases=aliases or {},
        compiler_params=pltpu.CompilerParams(vmem_limit_bytes=LIMIT),
    )(*args)


def shaped(*shape, kind=F32):
    return jax.ShapeDtypeStruct(shape, kind)


def resident(*shape, kind=F32):
    return pltpu.VMEM(shape, kind)


def kept(x):
    return pltpu.with_memory_space_constraint(x, pltpu.VMEM)


def exchange(x, axis, stride, size):
    n = lax.axis_size(axis)
    return [x] + [lax.ppermute(x, axis, [(i, i ^ (k * stride)) for i in range(n)]) for k in range(1, size)]


def spread(x, axis, first, join):
    n = lax.axis_size(axis)
    stride, size = 1, min(first, n)
    while True:
        parts = exchange(x, axis, stride, size)
        stride *= size
        if stride == n:
            return parts
        x = join(parts)
        size = min(4, n // stride)


def ring_all_reduce(pieces, n):
    order = ring_order(n)
    up = [(order[p], order[(p + 1) % n]) for p in range(n)]
    down = [(b, a) for a, b in up]
    far = n // 2
    mine = [[pieces[2 * at], pieces[2 * at + 1]] for at in range(n)]

    def ahead(x):
        return lax.ppermute(x, "rows", up)

    def behind(x):
        return lax.ppermute(x, "rows", down)

    rise, fall = [ahead(mine[far][0]), None], [None, behind(mine[far][1])]
    for step in range(far - 1, 0, -1):
        rise = [ahead(m if r is None else m + r) for m, r in zip(mine[step], rise)]
        fall = [behind(m if f is None else m + f) for m, f in zip(mine[-step], fall)]
    own = [m + r + f for m, r, f in zip(mine[0], rise, fall)]
    found = {0: own}
    rise = fall = own
    for step in range(1, far):
        rise, fall = [ahead(r) for r in rise], [behind(f) for f in fall]
        found[n - step], found[step] = rise, fall
    found[far] = [ahead(rise[0]), behind(fall[1])]
    return [half for at in range(n) for half in found[at]]


def quarter_all_reduce(keep, send):
    quarter = keep.shape[0] // 2
    keep = keep + exchange(send, "cols", 1, 2)[1]
    own = keep[:quarter] + exchange(keep[quarter:], "cols", 2, 2)[1]
    beside = exchange(own, "cols", 2, 2)[1]
    return own, beside, exchange(jnp.concatenate([own, beside]), "cols", 1, 2)[1]


def per_device(crawl, bench, start_duals, row_cotangent, col_cotangent):
    rows, columns = crawl.shape[0], bench.shape[0]
    row_cotangent = row_cotangent.reshape(1, rows)
    col_cotangent = col_cotangent.reshape(1, columns)
    row, column, tall = shaped(1, rows), shaped(1, columns), (rows, LANES)
    tile_shape = resident(rows, columns)

    def over_cols(x, join=sum):
        return spread(x, "cols", 4, join)

    def over_rows(x, join=sum):
        if lax.axis_size("rows") > 8:
            return spread(x, "rows", 4, join)
        n = lax.axis_size("rows")
        copies = jnp.broadcast_to(x.reshape(1, -1, LANES), (n, columns // LANES, LANES))
        return [join(list(lax.all_to_all(copies, "rows", 0, 0))).reshape(1, columns)]

    tile, top, local, crawl, bench, shift = pl.pallas_call(
        row_level_kernel,
        in_specs=[pl.BlockSpec(memory_space=pltpu.HBM)] * 3,
        out_specs=[pl.BlockSpec(memory_space=pltpu.VMEM)] * 6,
        out_shape=[tile_shape, row, row, resident(*crawl.shape, kind=crawl.dtype), resident(*bench.shape, kind=bench.dtype),
                   resident(1, columns)],
        scratch_shapes=[pltpu.VMEM(tall, F32)] * 2 + [pltpu.SemaphoreType.DMA((6,))],
        compiler_params=pltpu.CompilerParams(vmem_limit_bytes=LIMIT),
    )(*(pltpu.with_memory_space_constraint(x, pltpu.HBM) for x in (crawl, bench, start_duals.reshape(1, columns))))
    crawl, bench, shift = kept(crawl), kept(bench), kept(shift)
    parts = over_cols(local, log_sum)
    level, local = call(
        functools.partial(column_level_kernel, len(parts)),
        [kept(tile), top, *parts, crawl, bench, shift], [row, column], [tall])
    parts = over_rows(local, log_sum)
    soft, mass, local = call(
        functools.partial(soft_kernel, len(parts)),
        [kept(tile), top, level, *parts, crawl, bench, shift], [tile_shape, column, row],
        [tall, tall, (1, columns)], aliases={0: 0})
    parts = over_cols(local)
    inverse, local = call(functools.partial(second_column_kernel, len(parts)), [kept(soft), *parts], [row, column], [tall])
    parts = over_rows(local)
    scaled2, local = call(
        functools.partial(second_row_kernel, len(parts)),
        [kept(soft), inverse, col_cotangent, *parts], [column, row], [tall])
    parts = over_cols(local)
    scaled, local = call(
        functools.partial(first_column_kernel, len(parts)),
        [kept(soft), inverse, row_cotangent, *parts], [row, column], [tall])
    parts = over_rows(local)
    back, local = call(functools.partial(first_row_kernel, len(parts)), [kept(soft), *parts], [column, row], [tall])
    parts = over_cols(local)
    n = lax.axis_size("rows")
    width = bench.shape[1]
    share = columns // n
    piece = shaped(share // 2, width)
    ahead = share % (2 * LANES) == 0
    *factors, = call(
        functools.partial(far_kernel, len(parts), n),
        [kept(soft), inverse, scaled2, back, mass, scaled, crawl, *parts],
        [shaped(*tall)] * 3 + [piece] * (2 * ahead), [(LANES, share)])
    factors, far = factors[:3], factors[3:]
    places = [at for at in range(n) if at != n // 2 or not ahead]
    keep, send, *pieces = call(
        functools.partial(gradient_kernel, n, places),
        [kept(soft), *factors, scaled2, back, mass, crawl, bench],
        [shaped(rows // 2, width)] * 2 + [piece] * (2 * len(places)), [(LANES, columns), (columns, LANES), tall])
    if ahead:
        pieces[n:n] = far
    pieces = ring_all_reduce(pieces, n)
    quarters = quarter_all_reduce(keep, send)
    crawl_grad, bench_grad = pl.pallas_call(
        functools.partial(placing_kernel, n),
        in_specs=[pl.BlockSpec(memory_space=pltpu.VMEM)] * (3 + len(pieces)),
        out_specs=[pl.BlockSpec(memory_space=pl.ANY)] * 2,
        out_shape=[shaped(rows, width), shaped(columns, width)],
        scratch_shapes=[pltpu.SemaphoreType.DMA((4 + len(pieces),))],
        compiler_params=pltpu.CompilerParams(vmem_limit_bytes=LIMIT),
    )(*map(kept, (*quarters, *pieces)))
    return (crawl_grad, bench_grad)


def solution(mesh):
    placed = (P("rows", None), P("cols", None), P("cols"), P("rows"), P("cols"))
    return jax.shard_map(
        per_device,
        mesh=mesh,
        in_specs=placed,
        out_specs=(P("rows", None), P("cols", None)),
        check_vma=False,
    )
```

```python
import functools
import math

import jax
import jax.numpy as jnp
from jax import lax
from jax.experimental import pallas as pl
from jax.experimental.pallas import tpu as pltpu
from jax.sharding import PartitionSpec as P

EPSILON = 0.05
KAPPA = math.log2(math.e) / EPSILON
LOWEST = -90.0
LANES = 128
WIDE = 512
TALL = 256
LIMIT = 8 * 2**20
F32 = jnp.float32


def transposed_dot(a, b):
    return lax.dot_general(a, b, (((1,), (1,)), ((), ())), preferred_element_type=F32)


def column_form(row):
    return jnp.transpose(jnp.broadcast_to(row, (LANES, row.shape[1])))


def row_form(partial):
    return jnp.sum(jnp.transpose(partial), axis=0, keepdims=True)


def log_sum(parts):
    top = functools.reduce(jnp.maximum, parts)
    return top + jnp.log2(sum(jnp.exp2(p - top) for p in parts))


def row_sums(tile_ref, weights_ref, partial_ref):
    height = 64

    def body(block, _):
        rows = pl.ds(pl.multiple_of(block * height, height), height)
        acc = jnp.zeros((height, LANES), F32)
        for at in range(0, tile_ref.shape[1], LANES):
            acc += tile_ref[rows, at:at + LANES] * weights_ref[:, at:at + LANES]
        partial_ref[rows, :] = acc
        return _

    lax.fori_loop(0, tile_ref.shape[0] // height, body, 0)
    return row_form(partial_ref[...])


def column_sums(tile_ref, weights_ref, out_ref, scale_ref=None):
    starts = range(0, tile_ref.shape[1], LANES)

    def body(block, accs):
        for half in range(2):
            rows = pl.ds(pl.multiple_of(block * 16 + half * 8, 8), 8)
            weights = weights_ref[rows, :]
            accs = tuple(acc + tile_ref[rows, at:at + LANES] * weights for acc, at in zip(accs, starts))
        return accs

    accs = lax.fori_loop(0, tile_ref.shape[0] // 16, body, tuple(jnp.zeros((8, LANES), F32) for _ in starts))
    for acc, at in zip(accs, starts):
        total = jnp.sum(acc, axis=0, keepdims=True)
        out_ref[:, at:at + LANES] = total if scale_ref is None else total * scale_ref[:, at:at + LANES]


def exponent_block(crawl_ref, bench_ref, shift_ref, rows, columns):
    scores = transposed_dot(crawl_ref[rows, :], bench_ref[columns, :])
    return scores * KAPPA + shift_ref[:, columns]


def row_level_kernel(crawl_hbm, bench_hbm, duals_hbm, tile_ref, top_ref, level_ref, crawl_ref, bench_ref, shift_ref,
                     top_scratch, sum_scratch, sems):
    height = 64
    chunks = 4
    part = bench_ref.shape[0] // chunks
    copies = [pltpu.make_async_copy(crawl_hbm, crawl_ref, sems.at[chunks]),
              pltpu.make_async_copy(duals_hbm, shift_ref, sems.at[chunks + 1])]
    fetches = [
        pltpu.make_async_copy(bench_hbm.at[k * part:(k + 1) * part], bench_ref.at[k * part:(k + 1) * part], sems.at[k])
        for k in range(chunks)]
    for copy in (*copies, *fetches):
        copy.start()
    for copy in copies:
        copy.wait()
    shift_ref[...] = shift_ref[...] * KAPPA

    def fill(block, _, fetches=()):
        rows = pl.ds(pl.multiple_of(block * TALL, TALL), TALL)
        top = jnp.full((TALL, LANES), -jnp.inf, F32)
        for at in range(0, tile_ref.shape[1], WIDE):
            for k, fetch in enumerate(fetches):
                if at <= k * part < at + WIDE:
                    fetch.wait()
            exponent = exponent_block(crawl_ref, bench_ref, shift_ref, rows, pl.ds(at, WIDE))
            tile_ref[rows, at:at + WIDE] = exponent
            for lane in range(0, WIDE, LANES):
                top = jnp.maximum(top, exponent[:, lane:lane + LANES])
        top_scratch[rows, :] = top
        return _

    fill(0, 0, fetches)
    lax.fori_loop(1, tile_ref.shape[0] // TALL, fill, 0)

    def power(block, _):
        rows = pl.ds(pl.multiple_of(block * height, height), height)
        top = jnp.broadcast_to(jnp.max(top_scratch[rows, :], axis=1, keepdims=True), (height, LANES))
        acc = jnp.zeros((height, LANES), F32)
        for at in range(0, tile_ref.shape[1], LANES):
            value = jnp.exp2(tile_ref[rows, at:at + LANES] - top)
            tile_ref[rows, at:at + LANES] = value
            acc += value
        top_scratch[rows, :] = top
        sum_scratch[rows, :] = acc
        return _

    lax.fori_loop(0, tile_ref.shape[0] // height, power, 0)
    top = jnp.transpose(top_scratch[...])[0:1, :]
    top_ref[...] = top
    level_ref[...] = top + jnp.log2(row_form(sum_scratch[...]))


def column_level_kernel(parts, tile_ref, top_ref, *refs):
    part_refs, (crawl_ref, bench_ref, shift_ref, level_ref, out_ref, weights) = refs[:parts], refs[parts:]
    level = log_sum([p[...] for p in part_refs])
    level_ref[...] = level
    weights[...] = column_form(jnp.exp2(top_ref[...] - level))
    column_sums(tile_ref, weights, out_ref)
    out_ref[...] = jnp.log2(out_ref[...])

    @pl.when(jnp.min(out_ref[...]) < LOWEST)
    def _():
        weights[...] = column_form(level)
        blocks = tile_ref.shape[0] // TALL

        def column_block(column, _):
            columns = pl.ds(pl.multiple_of(column * WIDE, WIDE), WIDE)

            def logs(block):
                rows = pl.ds(pl.multiple_of(block * TALL, TALL), TALL)
                return exponent_block(crawl_ref, bench_ref, shift_ref, rows, columns) - weights[rows, 0:1]

            top = lax.fori_loop(
                0, blocks, lambda b, t: jnp.maximum(t, jnp.max(logs(b), axis=0, keepdims=True)),
                jnp.full((1, WIDE), -jnp.inf, F32))
            total = lax.fori_loop(
                0, blocks, lambda b, t: t + jnp.sum(jnp.exp2(logs(b) - top), axis=0, keepdims=True),
                jnp.zeros((1, WIDE), F32))
            out_ref[:, columns] = top + jnp.log2(total)
            return _

        lax.fori_loop(0, tile_ref.shape[1] // WIDE, column_block, 0)


def soft_kernel(parts, tile_ref, top_ref, level_ref, *refs):
    part_refs = refs[:parts]
    crawl_ref, bench_ref, shift_ref, soft_ref, left_ref, right_ref, mass_ref, sums_ref, partial, weights = refs[parts:]
    logs = log_sum([p[...] for p in part_refs])
    lowest = jnp.min(logs)

    @pl.when(lowest >= LOWEST)
    def _():
        left = jnp.exp2(top_ref[...] - level_ref[...])
        left_ref[...] = left
        right_ref[...] = jnp.exp2(-logs)
        mass_ref[...] = jnp.ones_like(logs)
        sums_ref[...] = row_sums(tile_ref, right_ref, partial) * left

    @pl.when(lowest < LOWEST)
    def _():
        left_ref[...] = jnp.ones_like(left_ref)
        mass_ref[...] = jnp.exp2(logs)
        right_ref[...] = logs
        weights[...] = column_form(level_ref[...])
        partial[...] = jnp.zeros_like(partial)

        def body(block, _):
            rows = pl.ds(pl.multiple_of(block * TALL, TALL), TALL)
            level = weights[rows, 0:1]

            def column_block(column, _):
                columns = pl.ds(pl.multiple_of(column * WIDE, WIDE), WIDE)
                exponent = exponent_block(crawl_ref, bench_ref, shift_ref, rows, columns)
                value = jnp.exp2(exponent - level - right_ref[:, columns])
                soft_ref[rows, columns] = value
                partial[rows, :] += sum(value[:, lane:lane + LANES] for lane in range(0, WIDE, LANES))
                return _

            return lax.fori_loop(0, tile_ref.shape[1] // WIDE, column_block, _)

        lax.fori_loop(0, tile_ref.shape[0] // TALL, body, 0)
        right_ref[...] = jnp.ones_like(right_ref)
        sums_ref[...] = row_form(partial[...])


def second_column_kernel(parts, soft_ref, left_ref, right_ref, *refs):
    part_refs, (inverse_ref, out_ref, weights) = refs[:parts], refs[parts:]
    inverse = left_ref[...] / sum(p[...] for p in part_refs)
    inverse_ref[...] = inverse
    weights[...] = column_form(inverse)
    column_sums(soft_ref, weights, out_ref, right_ref)


def second_row_kernel(parts, soft_ref, inverse_ref, right_ref, cotangent_ref, *refs):
    part_refs, (scaled_ref, out_ref, partial) = refs[:parts], refs[parts:]
    scaled_ref[...] = cotangent_ref[...] / sum(p[...] for p in part_refs) * right_ref[...]
    out_ref[...] = row_sums(soft_ref, scaled_ref, partial) * inverse_ref[...]


def first_column_kernel(parts, soft_ref, inverse_ref, right_ref, cotangent_ref, *refs):
    part_refs, (scaled_ref, out_ref, weights) = refs[:parts], refs[parts:]
    scaled = (cotangent_ref[...] - sum(p[...] for p in part_refs)) * inverse_ref[...]
    scaled_ref[...] = scaled
    weights[...] = column_form(-scaled)
    column_sums(soft_ref, weights, out_ref, right_ref)


def first_row_kernel(parts, soft_ref, left_ref, right_ref, *refs):
    part_refs, (back_ref, out_ref, partial) = refs[:parts], refs[parts:]
    back_ref[...] = sum(p[...] for p in part_refs) * right_ref[...]
    out_ref[...] = -row_sums(soft_ref, back_ref, partial) * left_ref[...]


def ring_order(n):
    return [*range(0, n, 2), *range(n - 1, 0, -2)]


def ring_share(n, at):
    me = lax.axis_index("rows")
    place = lax.rem(lax.select(lax.rem(me, 2) == 0, me // 2, n - 1 - me // 2) + at, n)
    return lax.select(place < n // 2, 2 * place, 2 * (n - 1 - place) + 1)


def early_kernel(soft_ref, inverse_ref, scaled_ref, left_ref, scaled2_ref, right_ref, back_ref, mass_ref, *refs):
    first_ref, early_ref, *row_refs = refs
    height = 64
    for row_ref, row in zip(row_refs, (inverse_ref, scaled_ref, left_ref)):
        row_ref[...] = column_form(-row[...])

    def body(block, _):
        rows = pl.ds(pl.multiple_of(block * height, height), height)
        a, b, c = (ref[rows, :] for ref in row_refs)
        for at in range(0, soft_ref.shape[1], LANES):
            span = slice(at, at + LANES)
            factor = a * scaled2_ref[:, span] + b * right_ref[:, span] + c * back_ref[:, span]
            early_ref[rows, span] = soft_ref[rows, span] * factor
        return _

    lax.fori_loop(0, soft_ref.shape[0] // height, body, 0)
    mass = mass_ref[...]

    @pl.when(jnp.max(jnp.abs(mass - 1.0)) > 0.0)
    def _():
        def scale(block, _):
            rows = pl.ds(pl.multiple_of(block * 8, 8), 8)
            first_ref[rows, :] = soft_ref[rows, :] * mass_ref[...]
            return _

        lax.fori_loop(0, soft_ref.shape[0] // 8, scale, 0)


def score_grad(early, first, last):
    return (early + first * last).astype(jnp.bfloat16)


def far_kernel(parts, n, first_ref, early_ref, left_ref, crawl_ref, *refs):
    part_refs, (last_ref, *piece_refs, flat) = refs[:parts], refs[parts:]
    last_ref[...] = column_form(-left_ref[...] * sum(p[...] for p in part_refs))
    if not piece_refs:
        return
    width = flat.shape[1]
    start = ring_share(n, n // 2) * width
    flat[...] = jnp.zeros_like(flat)

    def body(block, _):
        rows = pl.ds(pl.multiple_of(block * TALL, TALL), TALL)
        last = last_ref[rows, :]
        pieces = []
        for lane in range(0, width, LANES):
            span = pl.ds(pl.multiple_of(start + lane, LANES), LANES)
            pieces.append(score_grad(early_ref[rows, span], first_ref[rows, span], last))
        grad = jnp.concatenate(pieces, axis=1)
        flat[...] += lax.dot_general(crawl_ref[rows, :], grad, (((0,), (0,)), ((), ())), preferred_element_type=F32)
        return _

    lax.fori_loop(0, first_ref.shape[0] // TALL, body, 0)
    half = width // 2
    for k, piece in enumerate(piece_refs):
        piece[...] = jnp.transpose(flat[:, k * half:(k + 1) * half])


def gradient_kernel(n, places, first_ref, early_ref, last_ref, crawl_ref, bench_ref, *refs):
    keep_ref, send_ref, *piece_refs, flat, whole, total = refs
    flat[...] = jnp.zeros_like(flat)

    def body(block, _):
        rows = pl.ds(pl.multiple_of(block * TALL, TALL), TALL)
        last = last_ref[rows, :]
        x = crawl_ref[rows, :]
        acc = jnp.zeros((TALL, LANES), F32)
        for at in range(0, first_ref.shape[1], WIDE):
            pieces = []
            for lane in range(at, at + WIDE, LANES):
                span = slice(lane, lane + LANES)
                pieces.append(score_grad(early_ref[rows, span], first_ref[rows, span], last))
            grad = jnp.concatenate(pieces, axis=1)
            acc += jnp.dot(grad, bench_ref[at:at + WIDE, :], preferred_element_type=F32)
            flat[:, at:at + WIDE] += lax.dot_general(x, grad, (((0,), (0,)), ((), ())), preferred_element_type=F32)
        total[rows, :] = acc
        return _

    lax.fori_loop(0, first_ref.shape[0] // TALL, body, 0)
    me = lax.axis_index("cols")
    quarter = total.shape[0] // 4
    for k, (ref, low) in enumerate(((keep_ref, 0), (send_ref, 0), (keep_ref, quarter), (send_ref, quarter))):
        start = pl.multiple_of(lax.bitwise_xor(me, k) * quarter, quarter)
        ref[low:low + quarter, :] = total[pl.ds(start, quarter), :]
    whole[...] = jnp.transpose(flat[...])
    height = piece_refs[0].shape[0]
    for k, piece in enumerate(piece_refs):
        start = ring_share(n, places[k // 2]) * 2 * height + k % 2 * height
        piece[...] = whole[pl.ds(pl.multiple_of(start, height), height), :]


def placing_kernel(n, *refs):
    (own_ref, beside_ref, pair_ref, *pieces), (crawl_out, bench_out, sems) = refs[:-3], refs[-3:]
    me = lax.axis_index("cols")
    quarter = own_ref.shape[0]
    moves = []
    for k, piece in ((0, own_ref), (2, beside_ref), (1, pair_ref.at[:quarter]), (3, pair_ref.at[quarter:])):
        start = pl.multiple_of(lax.bitwise_xor(me, k) * quarter, quarter)
        moves.append((piece, crawl_out.at[pl.ds(start, quarter)]))
    height = pieces[0].shape[0]
    for at, piece in enumerate(pieces):
        start = pl.multiple_of(ring_share(n, at // 2) * 2 * height + at % 2 * height, height)
        moves.append((piece, bench_out.at[pl.ds(start, height)]))
    copies = [pltpu.make_async_copy(source, target, sems.at[k]) for k, (source, target) in enumerate(moves)]
    for copy in copies:
        copy.start()
    for copy in copies:
        copy.wait()


def call(kernel, args, outs, scratch, aliases=None):
    return pl.pallas_call(
        kernel,
        in_specs=[pl.BlockSpec(memory_space=pltpu.VMEM)] * len(args),
        out_specs=[pl.BlockSpec(memory_space=pltpu.VMEM)] * len(outs),
        out_shape=outs,
        scratch_shapes=[pltpu.VMEM(shape, F32) for shape in scratch],
        input_output_aliases=aliases or {},
        compiler_params=pltpu.CompilerParams(vmem_limit_bytes=LIMIT),
    )(*args)


def shaped(*shape, kind=F32):
    return jax.ShapeDtypeStruct(shape, kind)


def resident(*shape, kind=F32):
    return pltpu.VMEM(shape, kind)


def kept(x):
    return pltpu.with_memory_space_constraint(x, pltpu.VMEM)


def exchange(x, axis, stride, size):
    n = lax.axis_size(axis)
    return [x] + [lax.ppermute(x, axis, [(i, i ^ (k * stride)) for i in range(n)]) for k in range(1, size)]


def spread(x, axis, first, join):
    n = lax.axis_size(axis)
    stride, size = 1, min(first, n)
    while True:
        parts = exchange(x, axis, stride, size)
        stride *= size
        if stride == n:
            return parts
        x = join(parts)
        size = min(4, n // stride)


def ring_all_reduce(pieces, n):
    order = ring_order(n)
    up = [(order[p], order[(p + 1) % n]) for p in range(n)]
    down = [(b, a) for a, b in up]
    far = n // 2
    mine = [[pieces[2 * at], pieces[2 * at + 1]] for at in range(n)]

    def ahead(x):
        return lax.ppermute(x, "rows", up)

    def behind(x):
        return lax.ppermute(x, "rows", down)

    rise, fall = [ahead(mine[far][0]), None], [None, behind(mine[far][1])]
    for step in range(far - 1, 0, -1):
        rise = [ahead(m if r is None else m + r) for m, r in zip(mine[step], rise)]
        fall = [behind(m if f is None else m + f) for m, f in zip(mine[-step], fall)]
    own = [m + r + f for m, r, f in zip(mine[0], rise, fall)]
    found = {0: own}
    rise = fall = own
    for step in range(1, far):
        rise, fall = [ahead(r) for r in rise], [behind(f) for f in fall]
        found[n - step], found[step] = rise, fall
    found[far] = [ahead(rise[0]), behind(fall[1])]
    return [half for at in range(n) for half in found[at]]


def quarter_all_reduce(keep, send):
    quarter = keep.shape[0] // 2
    keep = keep + exchange(send, "cols", 1, 2)[1]
    own = keep[:quarter] + exchange(keep[quarter:], "cols", 2, 2)[1]
    beside = exchange(own, "cols", 2, 2)[1]
    return own, beside, exchange(jnp.concatenate([own, beside]), "cols", 1, 2)[1]


def per_device(crawl, bench, start_duals, row_cotangent, col_cotangent):
    rows, columns = crawl.shape[0], bench.shape[0]
    row_cotangent = row_cotangent.reshape(1, rows)
    col_cotangent = col_cotangent.reshape(1, columns)
    row, column, tall = shaped(1, rows), shaped(1, columns), (rows, LANES)
    tile_shape = resident(rows, columns)

    def over_cols(x, join=sum):
        return spread(x, "cols", 4, join)

    def over_rows(x, join=sum):
        n = lax.axis_size("rows")
        if n > 8:
            return spread(x, "rows", 4, join)
        copies = jnp.broadcast_to(x.reshape(1, -1, LANES), (n, columns // LANES, LANES))
        return [join(list(lax.all_to_all(copies, "rows", 0, 0))).reshape(1, columns)]

    tile, top, local, crawl, bench, shift = pl.pallas_call(
        row_level_kernel,
        in_specs=[pl.BlockSpec(memory_space=pltpu.HBM)] * 3,
        out_specs=[pl.BlockSpec(memory_space=pltpu.VMEM)] * 6,
        out_shape=[tile_shape, row, row, resident(*crawl.shape, kind=crawl.dtype), resident(*bench.shape, kind=bench.dtype),
                   resident(1, columns)],
        scratch_shapes=[pltpu.VMEM(tall, F32)] * 2 + [pltpu.SemaphoreType.DMA((6,))],
        compiler_params=pltpu.CompilerParams(vmem_limit_bytes=LIMIT),
    )(*(pltpu.with_memory_space_constraint(x, pltpu.HBM) for x in (crawl, bench, start_duals.reshape(1, columns))))
    crawl, bench, shift = kept(crawl), kept(bench), kept(shift)
    parts = over_cols(local, log_sum)
    level, local = call(
        functools.partial(column_level_kernel, len(parts)),
        [kept(tile), top, *parts, crawl, bench, shift], [row, column], [tall])
    parts = over_rows(local, log_sum)
    soft, left, right, mass, local = call(
        functools.partial(soft_kernel, len(parts)),
        [kept(tile), top, level, *parts, crawl, bench, shift], [tile_shape, row, column, column, row],
        [tall, tall], aliases={0: 0})
    soft = kept(soft)
    parts = over_cols(local)
    inverse, local = call(
        functools.partial(second_column_kernel, len(parts)), [soft, left, right, *parts], [row, column], [tall])
    parts = over_rows(local)
    scaled2, local = call(
        functools.partial(second_row_kernel, len(parts)),
        [soft, inverse, right, col_cotangent, *parts], [column, row], [tall])
    parts = over_cols(local)
    scaled, local = call(
        functools.partial(first_column_kernel, len(parts)),
        [soft, inverse, right, row_cotangent, *parts], [row, column], [tall])
    parts = over_rows(local)
    back, local = call(
        functools.partial(first_row_kernel, len(parts)), [soft, left, right, *parts], [column, row], [tall])
    parts = over_cols(local)
    n = lax.axis_size("rows")
    width = bench.shape[1]
    share = columns // n
    piece = shaped(share // 2, width)
    ahead = share % (2 * LANES) == 0
    first, early = call(
        early_kernel, [soft, inverse, scaled, left, scaled2, right, back, mass],
        [tile_shape, tile_shape], [tall] * 3, aliases={0: 0})
    first, early = kept(first), kept(early)
    last, *far = call(
        functools.partial(far_kernel, len(parts), n), [first, early, left, crawl, *parts],
        [shaped(*tall)] + [piece] * (2 * ahead), [(LANES, share)])
    places = [at for at in range(n) if at != n // 2 or not ahead]
    keep, send, *pieces = call(
        functools.partial(gradient_kernel, n, places),
        [first, early, last, crawl, bench],
        [shaped(rows // 2, width)] * 2 + [piece] * (2 * len(places)), [(LANES, columns), (columns, LANES), tall])
    if ahead:
        pieces[n:n] = far
    pieces = ring_all_reduce(pieces, n)
    quarters = quarter_all_reduce(keep, send)
    crawl_grad, bench_grad = pl.pallas_call(
        functools.partial(placing_kernel, n),
        in_specs=[pl.BlockSpec(memory_space=pltpu.VMEM)] * (3 + len(pieces)),
        out_specs=[pl.BlockSpec(memory_space=pl.ANY)] * 2,
        out_shape=[shaped(rows, width), shaped(columns, width)],
        scratch_shapes=[pltpu.SemaphoreType.DMA((4 + len(pieces),))],
        compiler_params=pltpu.CompilerParams(vmem_limit_bytes=LIMIT),
    )(*map(kept, (*quarters, *pieces)))
    return (crawl_grad, bench_grad)


def solution(mesh):
    placed = (P("rows", None), P("cols", None), P("cols"), P("rows"), P("cols"))
    return jax.shard_map(
        per_device,
        mesh=mesh,
        in_specs=placed,
        out_specs=(P("rows", None), P("cols", None)),
        check_vma=False,
    )
```

```python
import functools
import math

import jax
import jax.numpy as jnp
from jax import lax
from jax.experimental import pallas as pl
from jax.experimental.pallas import tpu as pltpu
from jax.sharding import PartitionSpec as P

EPSILON = 0.05
KAPPA = math.log2(math.e) / EPSILON
LOWEST = -90.0
LANES = 128
WIDE = 512
TALL = 256
LIMIT = 8 * 2**20
F32 = jnp.float32


def transposed_dot(a, b):
    return lax.dot_general(a, b, (((1,), (1,)), ((), ())), preferred_element_type=F32)


def column_form(row):
    return jnp.transpose(jnp.broadcast_to(row, (LANES, row.shape[1])))


def row_form(partial):
    return jnp.sum(jnp.transpose(partial), axis=0, keepdims=True)


def transposed_product(a, b):
    return lax.dot_general(a, b, (((0,), (0,)), ((), ())), preferred_element_type=F32)


def log_sum(parts):
    top = functools.reduce(jnp.maximum, parts)
    return top + jnp.log2(sum(jnp.exp2(p - top) for p in parts))


def row_sums(tile_ref, weights_ref, partial_ref):
    height = 64

    def body(block, _):
        rows = pl.ds(pl.multiple_of(block * height, height), height)
        acc = jnp.zeros((height, LANES), F32)
        for at in range(0, tile_ref.shape[1], LANES):
            acc += tile_ref[rows, at:at + LANES] * weights_ref[:, at:at + LANES]
        partial_ref[rows, :] = acc
        return _

    lax.fori_loop(0, tile_ref.shape[0] // height, body, 0)
    return row_form(partial_ref[...])


def column_sums(tile_ref, weights_ref, out_ref, scale_ref=None):
    starts = range(0, tile_ref.shape[1], LANES)

    def body(block, accs):
        for half in range(2):
            rows = pl.ds(pl.multiple_of(block * 16 + half * 8, 8), 8)
            weights = weights_ref[rows, :]
            accs = tuple(acc + tile_ref[rows, at:at + LANES] * weights for acc, at in zip(accs, starts))
        return accs

    accs = lax.fori_loop(0, tile_ref.shape[0] // 16, body, tuple(jnp.zeros((8, LANES), F32) for _ in starts))
    for acc, at in zip(accs, starts):
        total = jnp.sum(acc, axis=0, keepdims=True)
        out_ref[:, at:at + LANES] = total if scale_ref is None else total * scale_ref[:, at:at + LANES]


def exponent_block(crawl_ref, bench_ref, shift_ref, rows, columns):
    scores = transposed_dot(crawl_ref[rows, :], bench_ref[columns, :])
    return scores * KAPPA + shift_ref[:, columns]


def row_level_kernel(crawl_hbm, bench_hbm, duals_hbm, tile_ref, top_ref, level_ref, crawl_ref, bench_ref, shift_ref,
                     top_scratch, sum_scratch, sems):
    chunks = 4
    part = bench_ref.shape[0] // chunks
    copies = [pltpu.make_async_copy(crawl_hbm, crawl_ref, sems.at[chunks]),
              pltpu.make_async_copy(duals_hbm, shift_ref, sems.at[chunks + 1])]
    fetches = [
        pltpu.make_async_copy(bench_hbm.at[k * part:(k + 1) * part], bench_ref.at[k * part:(k + 1) * part], sems.at[k])
        for k in range(chunks)]
    for copy in (*copies, *fetches):
        copy.start()
    for copy in copies:
        copy.wait()
    shift_ref[...] = shift_ref[...] * KAPPA

    highest = jnp.max(shift_ref[...])

    def tops(block, _, fetches=()):
        rows = pl.ds(pl.multiple_of(block * TALL, TALL), TALL)
        top = jnp.full((TALL, LANES), -jnp.inf, F32)
        for at in range(0, tile_ref.shape[1], WIDE):
            for k, fetch in enumerate(fetches):
                if at <= k * part < at + WIDE:
                    fetch.wait()
            scores = transposed_dot(crawl_ref[rows, :], bench_ref[at:at + WIDE, :])
            for lane in range(0, WIDE, LANES):
                top = jnp.maximum(top, scores[:, lane:lane + LANES])
        top = jnp.max(top, axis=1, keepdims=True) * KAPPA + highest
        top_scratch[rows, :] = jnp.broadcast_to(top, (TALL, LANES))
        return _

    tops(0, 0, fetches)
    lax.fori_loop(1, tile_ref.shape[0] // TALL, tops, 0)

    def powers(block, _):
        rows = pl.ds(pl.multiple_of(block * TALL, TALL), TALL)
        top = top_scratch[rows, :]
        acc = jnp.zeros((TALL, LANES), F32)
        for at in range(0, tile_ref.shape[1], WIDE):
            scores = transposed_dot(crawl_ref[rows, :], bench_ref[at:at + WIDE, :])
            values = []
            for lane in range(0, WIDE, LANES):
                span = slice(at + lane, at + lane + LANES)
                value = jnp.exp2(scores[:, lane:lane + LANES] * KAPPA + (shift_ref[:, span] - top))
                tile_ref[rows, span] = value
                values.append(value)
            acc += sum(values)
        sum_scratch[rows, :] = acc
        return _

    lax.fori_loop(0, tile_ref.shape[0] // TALL, powers, 0)
    top = jnp.transpose(top_scratch[...])[0:1, :]
    top_ref[...] = top
    level_ref[...] = top + jnp.log2(row_form(sum_scratch[...]))


def column_level_kernel(parts, tile_ref, top_ref, *refs):
    part_refs, (crawl_ref, bench_ref, shift_ref, level_ref, out_ref, weights) = refs[:parts], refs[parts:]
    level = log_sum([p[...] for p in part_refs])
    level_ref[...] = level
    weights[...] = column_form(jnp.exp2(top_ref[...] - level))
    column_sums(tile_ref, weights, out_ref)
    out_ref[...] = jnp.log2(out_ref[...])

    @pl.when(jnp.min(out_ref[...]) < LOWEST)
    def _():
        weights[...] = column_form(level)
        blocks = tile_ref.shape[0] // TALL

        def column_block(column, _):
            columns = pl.ds(pl.multiple_of(column * WIDE, WIDE), WIDE)

            def logs(block):
                rows = pl.ds(pl.multiple_of(block * TALL, TALL), TALL)
                return exponent_block(crawl_ref, bench_ref, shift_ref, rows, columns) - weights[rows, 0:1]

            top = lax.fori_loop(
                0, blocks, lambda b, t: jnp.maximum(t, jnp.max(logs(b), axis=0, keepdims=True)),
                jnp.full((1, WIDE), -jnp.inf, F32))
            total = lax.fori_loop(
                0, blocks, lambda b, t: t + jnp.sum(jnp.exp2(logs(b) - top), axis=0, keepdims=True),
                jnp.zeros((1, WIDE), F32))
            out_ref[:, columns] = top + jnp.log2(total)
            return _

        lax.fori_loop(0, tile_ref.shape[1] // WIDE, column_block, 0)


def soft_kernel(parts, tile_ref, top_ref, level_ref, *refs):
    part_refs = refs[:parts]
    crawl_ref, bench_ref, shift_ref, soft_ref, left_ref, right_ref, mass_ref, sums_ref, partial, weights = refs[parts:]
    logs = log_sum([p[...] for p in part_refs])
    lowest = jnp.min(logs)

    @pl.when(lowest >= LOWEST)
    def _():
        left = jnp.exp2(top_ref[...] - level_ref[...])
        left_ref[...] = left
        right_ref[...] = jnp.exp2(-logs)
        mass_ref[...] = jnp.ones_like(logs)
        sums_ref[...] = row_sums(tile_ref, right_ref, partial) * left

    @pl.when(lowest < LOWEST)
    def _():
        left_ref[...] = jnp.ones_like(left_ref)
        mass_ref[...] = jnp.exp2(logs)
        right_ref[...] = logs
        weights[...] = column_form(level_ref[...])
        partial[...] = jnp.zeros_like(partial)

        def body(block, _):
            rows = pl.ds(pl.multiple_of(block * TALL, TALL), TALL)
            level = weights[rows, 0:1]

            def column_block(column, _):
                columns = pl.ds(pl.multiple_of(column * WIDE, WIDE), WIDE)
                exponent = exponent_block(crawl_ref, bench_ref, shift_ref, rows, columns)
                value = jnp.exp2(exponent - level - right_ref[:, columns])
                soft_ref[rows, columns] = value
                partial[rows, :] += sum(value[:, lane:lane + LANES] for lane in range(0, WIDE, LANES))
                return _

            return lax.fori_loop(0, tile_ref.shape[1] // WIDE, column_block, _)

        lax.fori_loop(0, tile_ref.shape[0] // TALL, body, 0)
        right_ref[...] = jnp.ones_like(right_ref)
        sums_ref[...] = row_form(partial[...])


def second_column_kernel(parts, soft_ref, left_ref, right_ref, *refs):
    part_refs, (inverse_ref, out_ref, weights) = refs[:parts], refs[parts:]
    inverse = left_ref[...] / sum(p[...] for p in part_refs)
    inverse_ref[...] = inverse
    weights[...] = column_form(inverse)
    column_sums(soft_ref, weights, out_ref, right_ref)


def second_row_kernel(parts, soft_ref, inverse_ref, right_ref, cotangent_ref, *refs):
    part_refs, (scaled_ref, out_ref, partial) = refs[:parts], refs[parts:]
    scaled_ref[...] = cotangent_ref[...] / sum(p[...] for p in part_refs) * right_ref[...]
    out_ref[...] = row_sums(soft_ref, scaled_ref, partial) * inverse_ref[...]


def first_column_kernel(parts, soft_ref, inverse_ref, right_ref, cotangent_ref, *refs):
    part_refs, (scaled_ref, out_ref, weights) = refs[:parts], refs[parts:]
    scaled = (cotangent_ref[...] - sum(p[...] for p in part_refs)) * inverse_ref[...]
    scaled_ref[...] = scaled
    weights[...] = column_form(-scaled)
    column_sums(soft_ref, weights, out_ref, right_ref)


def first_row_kernel(parts, soft_ref, left_ref, right_ref, *refs):
    part_refs, (back_ref, out_ref, partial) = refs[:parts], refs[parts:]
    back_ref[...] = sum(p[...] for p in part_refs) * right_ref[...]
    out_ref[...] = -row_sums(soft_ref, back_ref, partial) * left_ref[...]


def ring_order(n):
    return [*range(0, n, 2), *range(n - 1, 0, -2)]


def ring_share(n, at):
    me = lax.axis_index("rows")
    place = lax.rem(lax.select(lax.rem(me, 2) == 0, me // 2, n - 1 - me // 2) + at, n)
    return lax.select(place < n // 2, 2 * place, 2 * (n - 1 - place) + 1)


def early_kernel(soft_ref, inverse_ref, scaled_ref, left_ref, scaled2_ref, right_ref, back_ref, mass_ref, *refs):
    first_ref, early_ref, *row_refs = refs
    height = 64
    for row_ref, row in zip(row_refs, (inverse_ref, scaled_ref, left_ref)):
        row_ref[...] = column_form(-row[...])

    def body(block, _):
        rows = pl.ds(pl.multiple_of(block * height, height), height)
        a, b, c = (ref[rows, :] for ref in row_refs)
        for at in range(0, soft_ref.shape[1], LANES):
            span = slice(at, at + LANES)
            factor = a * scaled2_ref[:, span] + b * right_ref[:, span] + c * back_ref[:, span]
            early_ref[rows, span] = soft_ref[rows, span] * factor
        return _

    lax.fori_loop(0, soft_ref.shape[0] // height, body, 0)
    mass = mass_ref[...]

    @pl.when(jnp.max(jnp.abs(mass - 1.0)) > 0.0)
    def _():
        def scale(block, _):
            rows = pl.ds(pl.multiple_of(block * 8, 8), 8)
            first_ref[rows, :] = soft_ref[rows, :] * mass_ref[...]
            return _

        lax.fori_loop(0, soft_ref.shape[0] // 8, scale, 0)


def score_grad(early, first, last):
    return (early + first * last).astype(jnp.bfloat16)


def far_kernel(parts, n, places, first_ref, early_ref, left_ref, crawl_ref, *refs):
    part_refs, (last_ref, *piece_refs, flat) = refs[:parts], refs[parts:]
    last_ref[...] = column_form(-left_ref[...] * sum(p[...] for p in part_refs))
    if not places:
        return
    width = flat.shape[1] // len(places)
    starts = [ring_share(n, at) * width for at in places]
    flat[...] = jnp.zeros_like(flat)

    def body(block, _):
        rows = pl.ds(pl.multiple_of(block * TALL, TALL), TALL)
        last = last_ref[rows, :]
        for k, start in enumerate(starts):
            pieces = []
            for lane in range(0, width, LANES):
                span = pl.ds(pl.multiple_of(start + lane, LANES), LANES)
                pieces.append(score_grad(early_ref[rows, span], first_ref[rows, span], last))
            flat[:, k * width:(k + 1) * width] += transposed_product(crawl_ref[rows, :], jnp.concatenate(pieces, axis=1))
        return _

    lax.fori_loop(0, first_ref.shape[0] // TALL, body, 0)
    height = width // 2
    for k, piece in enumerate(piece_refs):
        piece[...] = jnp.transpose(flat[:, k * height:(k + 1) * height])


def gradient_kernel(n, places, first_ref, early_ref, last_ref, crawl_ref, bench_ref, *refs):
    in_order = len(places) < n
    if in_order:
        (near, far), refs = refs[:2], refs[2:]
        refs[2][...], refs[3][...] = near[...], far[...]
        refs = refs[:2] + refs[4:]
    keep_ref, send_ref, *piece_refs, flat, whole, total = refs
    flat[...] = jnp.zeros_like(flat)
    columns = first_ref.shape[1]
    width = columns // n if in_order else WIDE
    starts = [ring_share(n, at) * width if in_order else at * width for at in range(columns // width)]

    def body(block, _):
        rows = pl.ds(pl.multiple_of(block * TALL, TALL), TALL)
        last = last_ref[rows, :]
        acc = jnp.zeros((TALL, LANES), F32)
        for k, start in enumerate(starts):
            pieces = []
            for lane in range(0, width, LANES):
                span = pl.ds(pl.multiple_of(start + lane, LANES), LANES)
                pieces.append(score_grad(early_ref[rows, span], first_ref[rows, span], last))
            grad = jnp.concatenate(pieces, axis=1)
            acc += jnp.dot(grad, bench_ref[pl.ds(pl.multiple_of(start, width), width), :], preferred_element_type=F32)
            if k in places or not in_order:
                flat[:, k * width:(k + 1) * width] += transposed_product(crawl_ref[rows, :], grad)
        total[rows, :] = acc
        return _

    lax.fori_loop(0, first_ref.shape[0] // TALL, body, 0)
    me = lax.axis_index("cols")
    quarter = total.shape[0] // 4
    for k, (ref, low) in enumerate(((keep_ref, 0), (send_ref, 0), (keep_ref, quarter), (send_ref, quarter))):
        start = pl.multiple_of(lax.bitwise_xor(me, k) * quarter, quarter)
        ref[low:low + quarter, :] = total[pl.ds(start, quarter), :]
    height = piece_refs[0].shape[0]
    if not in_order:
        whole[...] = jnp.transpose(flat[...])
    for k, piece in enumerate(piece_refs):
        at = places[k // 2]
        if in_order:
            low = at * width + k % 2 * height
            piece[...] = jnp.transpose(flat[:, low:low + height])
        else:
            start = ring_share(n, at) * 2 * height + k % 2 * height
            piece[...] = whole[pl.ds(pl.multiple_of(start, height), height), :]


def placing_kernel(n, *refs):
    (own_ref, beside_ref, pair_ref, *pieces), (crawl_out, bench_out, sems) = refs[:-3], refs[-3:]
    me = lax.axis_index("cols")
    quarter = own_ref.shape[0]
    moves = []
    for k, piece in ((0, own_ref), (2, beside_ref), (1, pair_ref.at[:quarter]), (3, pair_ref.at[quarter:])):
        start = pl.multiple_of(lax.bitwise_xor(me, k) * quarter, quarter)
        moves.append((piece, crawl_out.at[pl.ds(start, quarter)]))
    height = pieces[0].shape[0]
    for at, piece in enumerate(pieces):
        start = pl.multiple_of(ring_share(n, at // 2) * 2 * height + at % 2 * height, height)
        moves.append((piece, bench_out.at[pl.ds(start, height)]))
    copies = [pltpu.make_async_copy(source, target, sems.at[k]) for k, (source, target) in enumerate(moves)]
    for copy in copies:
        copy.start()
    for copy in copies:
        copy.wait()


def call(kernel, args, outs, scratch, aliases=None):
    return pl.pallas_call(
        kernel,
        in_specs=[pl.BlockSpec(memory_space=pltpu.VMEM)] * len(args),
        out_specs=[pl.BlockSpec(memory_space=pltpu.VMEM)] * len(outs),
        out_shape=outs,
        scratch_shapes=[pltpu.VMEM(shape, F32) for shape in scratch],
        input_output_aliases=aliases or {},
        compiler_params=pltpu.CompilerParams(vmem_limit_bytes=LIMIT),
    )(*args)


def shaped(*shape, kind=F32):
    return jax.ShapeDtypeStruct(shape, kind)


def resident(*shape, kind=F32):
    return pltpu.VMEM(shape, kind)


def kept(x):
    return pltpu.with_memory_space_constraint(x, pltpu.VMEM)


def exchange(x, axis, stride, size):
    n = lax.axis_size(axis)
    return [x] + [lax.ppermute(x, axis, [(i, i ^ (k * stride)) for i in range(n)]) for k in range(1, size)]


def spread(x, axis, first, join):
    n = lax.axis_size(axis)
    stride, size = 1, min(first, n)
    while True:
        parts = exchange(x, axis, stride, size)
        stride *= size
        if stride == n:
            return parts
        x = join(parts)
        size = min(4, n // stride)


def ring_all_reduce(pieces, n):
    order = ring_order(n)
    up = [(order[p], order[(p + 1) % n]) for p in range(n)]
    down = [(b, a) for a, b in up]
    far = n // 2
    mine = [[pieces[2 * at], pieces[2 * at + 1]] for at in range(n)]

    def ahead(x):
        return lax.ppermute(x, "rows", up)

    def behind(x):
        return lax.ppermute(x, "rows", down)

    rise, fall = [ahead(mine[far][0]), None], [None, behind(mine[far][1])]
    for step in range(far - 1, 0, -1):
        rise = [ahead(m if r is None else m + r) for m, r in zip(mine[step], rise)]
        fall = [behind(m if f is None else m + f) for m, f in zip(mine[-step], fall)]
    own = [m + r + f for m, r, f in zip(mine[0], rise, fall)]
    found = {0: own}
    rise = fall = own
    for step in range(1, far):
        rise, fall = [ahead(r) for r in rise], [behind(f) for f in fall]
        found[n - step], found[step] = rise, fall
    found[far] = [ahead(rise[0]), behind(fall[1])]
    return [half for at in range(n) for half in found[at]]


def quarter_all_reduce(keep, send):
    quarter = keep.shape[0] // 2
    keep = keep + exchange(send, "cols", 1, 2)[1]
    own = keep[:quarter] + exchange(keep[quarter:], "cols", 2, 2)[1]
    beside = exchange(own, "cols", 2, 2)[1]
    return own, beside, exchange(jnp.concatenate([own, beside]), "cols", 1, 2)[1]


def per_device(crawl, bench, start_duals, row_cotangent, col_cotangent):
    rows, columns = crawl.shape[0], bench.shape[0]
    row_cotangent = row_cotangent.reshape(1, rows)
    col_cotangent = col_cotangent.reshape(1, columns)
    row, column, tall = shaped(1, rows), shaped(1, columns), (rows, LANES)
    tile_shape = resident(rows, columns)

    def over_cols(x, join=sum):
        return spread(x, "cols", 4, join)

    def over_rows(x, join=sum):
        n = lax.axis_size("rows")
        if n > 8:
            return spread(x, "rows", 4, join)
        copies = jnp.broadcast_to(x.reshape(1, -1, LANES), (n, columns // LANES, LANES))
        return [join(list(lax.all_to_all(copies, "rows", 0, 0))).reshape(1, columns)]

    tile, top, local, crawl, bench, shift = pl.pallas_call(
        row_level_kernel,
        in_specs=[pl.BlockSpec(memory_space=pltpu.HBM)] * 3,
        out_specs=[pl.BlockSpec(memory_space=pltpu.VMEM)] * 6,
        out_shape=[tile_shape, row, row, resident(*crawl.shape, kind=crawl.dtype), resident(*bench.shape, kind=bench.dtype),
                   resident(1, columns)],
        scratch_shapes=[pltpu.VMEM(tall, F32)] * 2 + [pltpu.SemaphoreType.DMA((6,))],
        compiler_params=pltpu.CompilerParams(vmem_limit_bytes=LIMIT),
    )(*(pltpu.with_memory_space_constraint(x, pltpu.HBM) for x in (crawl, bench, start_duals.reshape(1, columns))))
    crawl, bench, shift = kept(crawl), kept(bench), kept(shift)
    parts = over_cols(local, log_sum)
    level, local = call(
        functools.partial(column_level_kernel, len(parts)),
        [kept(tile), top, *parts, crawl, bench, shift], [row, column], [tall])
    parts = over_rows(local, log_sum)
    soft, left, right, mass, local = call(
        functools.partial(soft_kernel, len(parts)),
        [kept(tile), top, level, *parts, crawl, bench, shift], [tile_shape, row, column, column, row],
        [tall, tall], aliases={0: 0})
    soft = kept(soft)
    parts = over_cols(local)
    inverse, local = call(
        functools.partial(second_column_kernel, len(parts)), [soft, left, right, *parts], [row, column], [tall])
    parts = over_rows(local)
    scaled2, local = call(
        functools.partial(second_row_kernel, len(parts)),
        [soft, inverse, right, col_cotangent, *parts], [column, row], [tall])
    parts = over_cols(local)
    scaled, local = call(
        functools.partial(first_column_kernel, len(parts)),
        [soft, inverse, right, row_cotangent, *parts], [row, column], [tall])
    parts = over_rows(local)
    back, local = call(
        functools.partial(first_row_kernel, len(parts)), [soft, left, right, *parts], [column, row], [tall])
    parts = over_cols(local)
    n = lax.axis_size("rows")
    width = bench.shape[1]
    share = columns // n
    piece = shaped(share // 2, width)
    first, early = call(
        early_kernel, [soft, inverse, scaled, left, scaled2, right, back, mass],
        [tile_shape, tile_shape], [tall] * 3, aliases={0: 0})
    first, early = kept(first), kept(early)
    ahead = [n // 2 - 1, n // 2, n // 2 + 1] if n >= 4 and share % (2 * LANES) == 0 else []
    last, *far = call(
        functools.partial(far_kernel, len(parts), n, ahead), [first, early, left, crawl, *parts],
        [shaped(*tall)] + [piece] * (2 * len(ahead)), [(LANES, share * max(1, len(ahead)))])
    places = [at for at in range(n) if at not in ahead]
    first_added = [far[0], far[5]] if ahead else []
    keep, send, *pieces = call(
        functools.partial(gradient_kernel, n, places),
        [first, early, last, crawl, bench, *first_added],
        [shaped(rows // 2, width)] * 2 + [piece] * (len(first_added) + 2 * len(places)),
        [(LANES, columns), (LANES, LANES) if ahead else (columns, LANES), tall])
    if ahead:
        far[0], far[5], *pieces = pieces
        pieces[2 * ahead[0]:2 * ahead[0]] = far
    pieces = ring_all_reduce(pieces, n)
    quarters = quarter_all_reduce(keep, send)
    crawl_grad, bench_grad = pl.pallas_call(
        functools.partial(placing_kernel, n),
        in_specs=[pl.BlockSpec(memory_space=pltpu.VMEM)] * (3 + len(pieces)),
        out_specs=[pl.BlockSpec(memory_space=pl.ANY)] * 2,
        out_shape=[shaped(rows, width), shaped(columns, width)],
        scratch_shapes=[pltpu.SemaphoreType.DMA((4 + len(pieces),))],
        compiler_params=pltpu.CompilerParams(vmem_limit_bytes=LIMIT),
    )(*map(kept, (*quarters, *pieces)))
    return (crawl_grad, bench_grad)


def solution(mesh):
    placed = (P("rows", None), P("cols", None), P("cols"), P("rows"), P("cols"))
    return jax.shard_map(
        per_device,
        mesh=mesh,
        in_specs=placed,
        out_specs=(P("rows", None), P("cols", None)),
        check_vma=False,
    )
```

```python
import functools
import math

import jax
import jax.numpy as jnp
from jax import lax
from jax.experimental import pallas as pl
from jax.experimental.pallas import tpu as pltpu
from jax.sharding import PartitionSpec as P

EPSILON = 0.05
KAPPA = math.log2(math.e) / EPSILON
LOWEST = -64.0
LANES = 128
WIDE = 512
TALL = 256
LIMIT = 8 * 2**20
F32 = jnp.float32


def transposed_dot(a, b):
    return lax.dot_general(a, b, (((1,), (1,)), ((), ())), preferred_element_type=F32)


def column_form(row):
    return jnp.transpose(jnp.broadcast_to(row, (LANES, row.shape[1])))


def row_form(partial):
    return jnp.sum(jnp.transpose(partial), axis=0, keepdims=True)


def log_sum(parts):
    top = functools.reduce(jnp.maximum, parts)
    return top + jnp.log2(sum(jnp.exp2(p - top) for p in parts))


def row_sums(tile_ref, weights_ref, partial_ref):
    height = 64

    def body(block, _):
        rows = pl.ds(pl.multiple_of(block * height, height), height)
        acc = jnp.zeros((height, LANES), F32)
        for at in range(0, tile_ref.shape[1], LANES):
            acc += tile_ref[rows, at:at + LANES] * weights_ref[:, at:at + LANES]
        partial_ref[rows, :] = acc
        return _

    lax.fori_loop(0, tile_ref.shape[0] // height, body, 0)
    return row_form(partial_ref[...])


def column_sums(tile_ref, weights_ref, out_ref, scale_ref=None):
    starts = range(0, tile_ref.shape[1], LANES)

    def body(block, accs):
        for half in range(2):
            rows = pl.ds(pl.multiple_of(block * 16 + half * 8, 8), 8)
            weights = weights_ref[rows, :]
            accs = tuple(acc + tile_ref[rows, at:at + LANES] * weights for acc, at in zip(accs, starts))
        return accs

    accs = lax.fori_loop(0, tile_ref.shape[0] // 16, body, tuple(jnp.zeros((8, LANES), F32) for _ in starts))
    for acc, at in zip(accs, starts):
        total = jnp.sum(acc, axis=0, keepdims=True)
        out_ref[:, at:at + LANES] = total if scale_ref is None else total * scale_ref[:, at:at + LANES]


def exponent_block(crawl_ref, bench_ref, shift_ref, rows, columns):
    scores = transposed_dot(crawl_ref[rows, :], bench_ref[columns, :])
    return scores * KAPPA + shift_ref[:, columns]


def row_level_kernel(crawl_hbm, bench_hbm, duals_hbm, tile_ref, top_ref, level_ref, crawl_ref, bench_ref, shift_ref,
                     top_scratch, sum_scratch, sems):
    height = 64
    chunks = 4
    part = bench_ref.shape[0] // chunks
    copies = [pltpu.make_async_copy(crawl_hbm, crawl_ref, sems.at[chunks]),
              pltpu.make_async_copy(duals_hbm, shift_ref, sems.at[chunks + 1])]
    fetches = [
        pltpu.make_async_copy(bench_hbm.at[k * part:(k + 1) * part], bench_ref.at[k * part:(k + 1) * part], sems.at[k])
        for k in range(chunks)]
    for copy in (*copies, *fetches):
        copy.start()
    for copy in copies:
        copy.wait()
    shift_ref[...] = shift_ref[...] * KAPPA

    def fill(block, _, fetches=()):
        rows = pl.ds(pl.multiple_of(block * TALL, TALL), TALL)
        top = jnp.full((TALL, LANES), -jnp.inf, F32)
        for at in range(0, tile_ref.shape[1], WIDE):
            for k, fetch in enumerate(fetches):
                if at <= k * part < at + WIDE:
                    fetch.wait()
            exponent = exponent_block(crawl_ref, bench_ref, shift_ref, rows, pl.ds(at, WIDE))
            tile_ref[rows, at:at + WIDE] = exponent
            for lane in range(0, WIDE, LANES):
                top = jnp.maximum(top, exponent[:, lane:lane + LANES])
        top_scratch[rows, :] = top
        return _

    fill(0, 0, fetches)
    lax.fori_loop(1, tile_ref.shape[0] // TALL, fill, 0)

    def power(block, _):
        rows = pl.ds(pl.multiple_of(block * height, height), height)
        top = jnp.broadcast_to(jnp.max(top_scratch[rows, :], axis=1, keepdims=True), (height, LANES))
        acc = jnp.zeros((height, LANES), F32)
        for at in range(0, tile_ref.shape[1], LANES):
            value = jnp.exp2(tile_ref[rows, at:at + LANES] - top)
            tile_ref[rows, at:at + LANES] = value
            acc += value
        top_scratch[rows, :] = top
        sum_scratch[rows, :] = acc
        return _

    lax.fori_loop(0, tile_ref.shape[0] // height, power, 0)
    top = jnp.transpose(top_scratch[...])[0:1, :]
    top_ref[...] = top
    level_ref[...] = top + jnp.log2(row_form(sum_scratch[...]))


def column_level_kernel(parts, tile_ref, top_ref, *refs):
    part_refs, (crawl_ref, bench_ref, shift_ref, level_ref, out_ref, weights) = refs[:parts], refs[parts:]
    level = log_sum([p[...] for p in part_refs])
    level_ref[...] = level
    weights[...] = column_form(jnp.exp2(top_ref[...] - level))
    column_sums(tile_ref, weights, out_ref)
    out_ref[...] = jnp.log2(out_ref[...])

    @pl.when(jnp.min(out_ref[...]) < LOWEST)
    def _():
        weights[...] = column_form(level)
        blocks = tile_ref.shape[0] // TALL

        def column_block(column, _):
            columns = pl.ds(pl.multiple_of(column * WIDE, WIDE), WIDE)

            def logs(block):
                rows = pl.ds(pl.multiple_of(block * TALL, TALL), TALL)
                return exponent_block(crawl_ref, bench_ref, shift_ref, rows, columns) - weights[rows, 0:1]

            top = lax.fori_loop(
                0, blocks, lambda b, t: jnp.maximum(t, jnp.max(logs(b), axis=0, keepdims=True)),
                jnp.full((1, WIDE), -jnp.inf, F32))
            total = lax.fori_loop(
                0, blocks, lambda b, t: t + jnp.sum(jnp.exp2(logs(b) - top), axis=0, keepdims=True),
                jnp.zeros((1, WIDE), F32))
            out_ref[:, columns] = top + jnp.log2(total)
            return _

        lax.fori_loop(0, tile_ref.shape[1] // WIDE, column_block, 0)


def soft_kernel(parts, tile_ref, top_ref, level_ref, *refs):
    part_refs = refs[:parts]
    crawl_ref, bench_ref, shift_ref, soft_ref, left_ref, right_ref, mass_ref, sums_ref, partial, weights = refs[parts:]
    logs = log_sum([p[...] for p in part_refs])
    lowest = jnp.min(logs)

    @pl.when(lowest >= LOWEST)
    def _():
        left = jnp.exp2(top_ref[...] - level_ref[...])
        left_ref[...] = left
        right_ref[...] = jnp.exp2(-logs)
        mass_ref[...] = jnp.ones_like(logs)
        sums_ref[...] = row_sums(tile_ref, right_ref, partial) * left

    @pl.when(lowest < LOWEST)
    def _():
        left_ref[...] = jnp.ones_like(left_ref)
        mass_ref[...] = jnp.exp2(logs)
        right_ref[...] = logs
        weights[...] = column_form(level_ref[...])
        partial[...] = jnp.zeros_like(partial)

        def body(block, _):
            rows = pl.ds(pl.multiple_of(block * TALL, TALL), TALL)
            level = weights[rows, 0:1]

            def column_block(column, _):
                columns = pl.ds(pl.multiple_of(column * WIDE, WIDE), WIDE)
                exponent = exponent_block(crawl_ref, bench_ref, shift_ref, rows, columns)
                value = jnp.exp2(exponent - level - right_ref[:, columns])
                soft_ref[rows, columns] = value
                partial[rows, :] += sum(value[:, lane:lane + LANES] for lane in range(0, WIDE, LANES))
                return _

            return lax.fori_loop(0, tile_ref.shape[1] // WIDE, column_block, _)

        lax.fori_loop(0, tile_ref.shape[0] // TALL, body, 0)
        right_ref[...] = jnp.ones_like(right_ref)
        sums_ref[...] = row_form(partial[...])


def second_column_kernel(parts, soft_ref, left_ref, right_ref, *refs):
    part_refs, (inverse_ref, out_ref, weights) = refs[:parts], refs[parts:]
    inverse = left_ref[...] / sum(p[...] for p in part_refs)
    inverse_ref[...] = inverse
    weights[...] = column_form(inverse)
    column_sums(soft_ref, weights, out_ref, right_ref)


def second_row_kernel(parts, soft_ref, inverse_ref, right_ref, cotangent_ref, *refs):
    part_refs, (scaled_ref, out_ref, partial) = refs[:parts], refs[parts:]
    scaled_ref[...] = cotangent_ref[...] / sum(p[...] for p in part_refs) * right_ref[...]
    out_ref[...] = row_sums(soft_ref, scaled_ref, partial) * inverse_ref[...]


def first_column_kernel(parts, soft_ref, inverse_ref, right_ref, cotangent_ref, *refs):
    part_refs, (scaled_ref, out_ref, weights) = refs[:parts], refs[parts:]
    scaled = (cotangent_ref[...] - sum(p[...] for p in part_refs)) * inverse_ref[...]
    scaled_ref[...] = scaled
    weights[...] = column_form(-scaled)
    column_sums(soft_ref, weights, out_ref, right_ref)


def first_row_kernel(parts, soft_ref, left_ref, right_ref, *refs):
    part_refs, (back_ref, out_ref, partial) = refs[:parts], refs[parts:]
    back_ref[...] = sum(p[...] for p in part_refs) * right_ref[...]
    out_ref[...] = -row_sums(soft_ref, back_ref, partial) * left_ref[...]


def ring_order(n):
    return [*range(0, n, 2), *range(n - 1, 0, -2)]


def ring_share(n, at):
    me = lax.axis_index("rows")
    place = lax.rem(lax.select(lax.rem(me, 2) == 0, me // 2, n - 1 - me // 2) + at, n)
    return lax.select(place < n // 2, 2 * place, 2 * (n - 1 - place) + 1)


def thirds(x):
    parts = []
    for _ in range(3):
        parts.append(x.astype(jnp.bfloat16).astype(F32))
        x = x - parts[-1]
    return parts


def early_kernel(soft_ref, inverse_ref, scaled_ref, left_ref, scaled2_ref, right_ref, back_ref, mass_ref, *refs):
    first_ref, early_ref, row_parts, column_parts = refs
    row_parts[...] = jnp.zeros_like(row_parts)
    column_parts[...] = jnp.zeros_like(column_parts)
    at = 0
    for row, column in ((inverse_ref, scaled2_ref), (scaled_ref, right_ref), (left_ref, back_ref)):
        r, c = thirds(-row[...]), thirds(column[...])
        for i, j in ((0, 0), (0, 1), (1, 0), (1, 1), (0, 2), (2, 0)):
            row_parts[at:at + 1, :] = r[i]
            column_parts[at:at + 1, :] = c[j]
            at += 1

    def body(block, _):
        rows = pl.ds(pl.multiple_of(block * TALL, TALL), TALL)
        r = row_parts[:, rows].astype(jnp.bfloat16)
        for at in range(0, soft_ref.shape[1], WIDE):
            span = slice(at, at + WIDE)
            factor = lax.dot_general(
                r, column_parts[:, span].astype(jnp.bfloat16), (((0,), (0,)), ((), ())), preferred_element_type=F32)
            early_ref[rows, span] = soft_ref[rows, span] * factor
        return _

    lax.fori_loop(0, soft_ref.shape[0] // TALL, body, 0)
    mass = mass_ref[...]

    @pl.when(jnp.max(jnp.abs(mass - 1.0)) > 0.0)
    def _():
        def scale(block, _):
            rows = pl.ds(pl.multiple_of(block * 8, 8), 8)
            first_ref[rows, :] = soft_ref[rows, :] * mass_ref[...]
            return _

        lax.fori_loop(0, soft_ref.shape[0] // 8, scale, 0)


def score_grad(early, first, last):
    return (early + first * last).astype(jnp.bfloat16)


def far_kernel(parts, n, first_ref, early_ref, left_ref, crawl_ref, *refs):
    part_refs, (last_ref, *piece_refs, flat) = refs[:parts], refs[parts:]
    last_ref[...] = column_form(-left_ref[...] * sum(p[...] for p in part_refs))
    if not piece_refs:
        return
    width = flat.shape[1]
    start = ring_share(n, n // 2) * width
    flat[...] = jnp.zeros_like(flat)

    def body(block, _):
        rows = pl.ds(pl.multiple_of(block * TALL, TALL), TALL)
        last = last_ref[rows, :]
        pieces = []
        for lane in range(0, width, LANES):
            span = pl.ds(pl.multiple_of(start + lane, LANES), LANES)
            pieces.append(score_grad(early_ref[rows, span], first_ref[rows, span], last))
        grad = jnp.concatenate(pieces, axis=1)
        flat[...] += lax.dot_general(crawl_ref[rows, :], grad, (((0,), (0,)), ((), ())), preferred_element_type=F32)
        return _

    lax.fori_loop(0, first_ref.shape[0] // TALL, body, 0)
    half = width // 2
    for k, piece in enumerate(piece_refs):
        piece[...] = jnp.transpose(flat[:, k * half:(k + 1) * half])


def gradient_kernel(n, places, first_ref, early_ref, last_ref, crawl_ref, bench_ref, *refs):
    keep_ref, send_ref, *piece_refs, flat, whole, total = refs
    flat[...] = jnp.zeros_like(flat)

    def body(block, _):
        rows = pl.ds(pl.multiple_of(block * TALL, TALL), TALL)
        last = last_ref[rows, :]
        x = crawl_ref[rows, :]
        acc = jnp.zeros((TALL, LANES), F32)
        for at in range(0, first_ref.shape[1], WIDE):
            pieces = []
            for lane in range(at, at + WIDE, LANES):
                span = slice(lane, lane + LANES)
                pieces.append(score_grad(early_ref[rows, span], first_ref[rows, span], last))
            grad = jnp.concatenate(pieces, axis=1)
            acc += jnp.dot(grad, bench_ref[at:at + WIDE, :], preferred_element_type=F32)
            flat[:, at:at + WIDE] += lax.dot_general(x, grad, (((0,), (0,)), ((), ())), preferred_element_type=F32)
        total[rows, :] = acc
        return _

    lax.fori_loop(0, first_ref.shape[0] // TALL, body, 0)
    me = lax.axis_index("cols")
    quarter = total.shape[0] // 4
    for k, (ref, low) in enumerate(((keep_ref, 0), (send_ref, 0), (keep_ref, quarter), (send_ref, quarter))):
        start = pl.multiple_of(lax.bitwise_xor(me, k) * quarter, quarter)
        ref[low:low + quarter, :] = total[pl.ds(start, quarter), :]
    whole[...] = jnp.transpose(flat[...])
    height = piece_refs[0].shape[0]
    for k, piece in enumerate(piece_refs):
        start = ring_share(n, places[k // 2]) * 2 * height + k % 2 * height
        piece[...] = whole[pl.ds(pl.multiple_of(start, height), height), :]


def placing_kernel(n, *refs):
    (own_ref, beside_ref, pair_ref, *pieces), (crawl_out, bench_out, sems) = refs[:-3], refs[-3:]
    me = lax.axis_index("cols")
    quarter = own_ref.shape[0]
    moves = []
    for k, piece in ((0, own_ref), (2, beside_ref), (1, pair_ref.at[:quarter]), (3, pair_ref.at[quarter:])):
        start = pl.multiple_of(lax.bitwise_xor(me, k) * quarter, quarter)
        moves.append((piece, crawl_out.at[pl.ds(start, quarter)]))
    height = pieces[0].shape[0]
    for at, piece in enumerate(pieces):
        start = pl.multiple_of(ring_share(n, at // 2) * 2 * height + at % 2 * height, height)
        moves.append((piece, bench_out.at[pl.ds(start, height)]))
    copies = [pltpu.make_async_copy(source, target, sems.at[k]) for k, (source, target) in enumerate(moves)]
    for copy in copies:
        copy.start()
    for copy in copies:
        copy.wait()


def call(kernel, args, outs, scratch, aliases=None):
    return pl.pallas_call(
        kernel,
        in_specs=[pl.BlockSpec(memory_space=pltpu.VMEM)] * len(args),
        out_specs=[pl.BlockSpec(memory_space=pltpu.VMEM)] * len(outs),
        out_shape=outs,
        scratch_shapes=[pltpu.VMEM(shape, F32) for shape in scratch],
        input_output_aliases=aliases or {},
        compiler_params=pltpu.CompilerParams(vmem_limit_bytes=LIMIT),
    )(*args)


def shaped(*shape, kind=F32):
    return jax.ShapeDtypeStruct(shape, kind)


def resident(*shape, kind=F32):
    return pltpu.VMEM(shape, kind)


def kept(x):
    return pltpu.with_memory_space_constraint(x, pltpu.VMEM)


def exchange(x, axis, stride, size):
    n = lax.axis_size(axis)
    return [x] + [lax.ppermute(x, axis, [(i, i ^ (k * stride)) for i in range(n)]) for k in range(1, size)]


def spread(x, axis, first, join):
    n = lax.axis_size(axis)
    stride, size = 1, min(first, n)
    while True:
        parts = exchange(x, axis, stride, size)
        stride *= size
        if stride == n:
            return parts
        x = join(parts)
        size = min(4, n // stride)


def ring_all_reduce(pieces, n):
    order = ring_order(n)
    up = [(order[p], order[(p + 1) % n]) for p in range(n)]
    down = [(b, a) for a, b in up]
    far = n // 2
    mine = [[pieces[2 * at], pieces[2 * at + 1]] for at in range(n)]

    def ahead(x):
        return lax.ppermute(x, "rows", up)

    def behind(x):
        return lax.ppermute(x, "rows", down)

    rise, fall = [ahead(mine[far][0]), None], [None, behind(mine[far][1])]
    for step in range(far - 1, 0, -1):
        rise = [ahead(m if r is None else m + r) for m, r in zip(mine[step], rise)]
        fall = [behind(m if f is None else m + f) for m, f in zip(mine[-step], fall)]
    own = [m + r + f for m, r, f in zip(mine[0], rise, fall)]
    found = {0: own}
    rise = fall = own
    for step in range(1, far):
        rise, fall = [ahead(r) for r in rise], [behind(f) for f in fall]
        found[n - step], found[step] = rise, fall
    found[far] = [ahead(rise[0]), behind(fall[1])]
    return [half for at in range(n) for half in found[at]]


def quarter_all_reduce(keep, send):
    quarter = keep.shape[0] // 2
    keep = keep + exchange(send, "cols", 1, 2)[1]
    own = keep[:quarter] + exchange(keep[quarter:], "cols", 2, 2)[1]
    beside = exchange(own, "cols", 2, 2)[1]
    return own, beside, exchange(jnp.concatenate([own, beside]), "cols", 1, 2)[1]


def per_device(crawl, bench, start_duals, row_cotangent, col_cotangent):
    rows, columns = crawl.shape[0], bench.shape[0]
    row_cotangent = row_cotangent.reshape(1, rows)
    col_cotangent = col_cotangent.reshape(1, columns)
    row, column, tall = shaped(1, rows), shaped(1, columns), (rows, LANES)
    tile_shape = resident(rows, columns)

    def over_cols(x, join=sum):
        return spread(x, "cols", 4, join)

    def over_rows(x, join=sum):
        n = lax.axis_size("rows")
        if n > 8:
            return spread(x, "rows", 4, join)
        copies = jnp.broadcast_to(x.reshape(1, -1, LANES), (n, columns // LANES, LANES))
        return [join(list(lax.all_to_all(copies, "rows", 0, 0))).reshape(1, columns)]

    tile, top, local, crawl, bench, shift = pl.pallas_call(
        row_level_kernel,
        in_specs=[pl.BlockSpec(memory_space=pltpu.HBM)] * 3,
        out_specs=[pl.BlockSpec(memory_space=pltpu.VMEM)] * 6,
        out_shape=[tile_shape, row, row, resident(*crawl.shape, kind=crawl.dtype), resident(*bench.shape, kind=bench.dtype),
                   resident(1, columns)],
        scratch_shapes=[pltpu.VMEM(tall, F32)] * 2 + [pltpu.SemaphoreType.DMA((6,))],
        compiler_params=pltpu.CompilerParams(vmem_limit_bytes=LIMIT),
    )(*(pltpu.with_memory_space_constraint(x, pltpu.HBM) for x in (crawl, bench, start_duals.reshape(1, columns))))
    crawl, bench, shift = kept(crawl), kept(bench), kept(shift)
    parts = over_cols(local, log_sum)
    level, local = call(
        functools.partial(column_level_kernel, len(parts)),
        [kept(tile), top, *parts, crawl, bench, shift], [row, column], [tall])
    parts = over_rows(local, log_sum)
    soft, left, right, mass, local = call(
        functools.partial(soft_kernel, len(parts)),
        [kept(tile), top, level, *parts, crawl, bench, shift], [tile_shape, row, column, column, row],
        [tall, tall], aliases={0: 0})
    soft = kept(soft)
    parts = over_cols(local)
    inverse, local = call(
        functools.partial(second_column_kernel, len(parts)), [soft, left, right, *parts], [row, column], [tall])
    parts = over_rows(local)
    scaled2, local = call(
        functools.partial(second_row_kernel, len(parts)),
        [soft, inverse, right, col_cotangent, *parts], [column, row], [tall])
    parts = over_cols(local)
    scaled, local = call(
        functools.partial(first_column_kernel, len(parts)),
        [soft, inverse, right, row_cotangent, *parts], [row, column], [tall])
    parts = over_rows(local)
    back, local = call(
        functools.partial(first_row_kernel, len(parts)), [soft, left, right, *parts], [column, row], [tall])
    parts = over_cols(local)
    n = lax.axis_size("rows")
    width = bench.shape[1]
    share = columns // n
    piece = shaped(share // 2, width)
    ahead = share % (2 * LANES) == 0
    first, early = call(
        early_kernel, [soft, inverse, scaled, left, scaled2, right, back, mass],
        [tile_shape, tile_shape], [(32, rows), (32, columns)], aliases={0: 0})
    first, early = kept(first), kept(early)
    last, *far = call(
        functools.partial(far_kernel, len(parts), n), [first, early, left, crawl, *parts],
        [shaped(*tall)] + [piece] * (2 * ahead), [(LANES, share)])
    places = [at for at in range(n) if at != n // 2 or not ahead]
    keep, send, *pieces = call(
        functools.partial(gradient_kernel, n, places),
        [first, early, last, crawl, bench],
        [shaped(rows // 2, width)] * 2 + [piece] * (2 * len(places)), [(LANES, columns), (columns, LANES), tall])
    if ahead:
        pieces[n:n] = far
    pieces = ring_all_reduce(pieces, n)
    quarters = quarter_all_reduce(keep, send)
    crawl_grad, bench_grad = pl.pallas_call(
        functools.partial(placing_kernel, n),
        in_specs=[pl.BlockSpec(memory_space=pltpu.VMEM)] * (3 + len(pieces)),
        out_specs=[pl.BlockSpec(memory_space=pl.ANY)] * 2,
        out_shape=[shaped(rows, width), shaped(columns, width)],
        scratch_shapes=[pltpu.SemaphoreType.DMA((4 + len(pieces),))],
        compiler_params=pltpu.CompilerParams(vmem_limit_bytes=LIMIT),
    )(*map(kept, (*quarters, *pieces)))
    return (crawl_grad, bench_grad)


def solution(mesh):
    placed = (P("rows", None), P("cols", None), P("cols"), P("rows"), P("cols"))
    return jax.shard_map(
        per_device,
        mesh=mesh,
        in_specs=placed,
        out_specs=(P("rows", None), P("cols", None)),
        check_vma=False,
    )
```

```python
import functools
import math

import jax
import jax.numpy as jnp
from jax import lax
from jax.experimental import pallas as pl
from jax.experimental.pallas import tpu as pltpu
from jax.sharding import PartitionSpec as P

EPSILON = 0.05
KAPPA = math.log2(math.e) / EPSILON
LOWEST = -64.0
LANES = 128
WIDE = 512
TALL = 512
LIMIT = 8 * 2**20
F32 = jnp.float32


def transposed_dot(a, b):
    return lax.dot_general(a, b, (((1,), (1,)), ((), ())), preferred_element_type=F32)


def column_form(row):
    return jnp.transpose(jnp.broadcast_to(row, (LANES, row.shape[1])))


def row_form(partial):
    return jnp.sum(jnp.transpose(partial), axis=0, keepdims=True)


def log_sum(parts):
    top = functools.reduce(jnp.maximum, parts)
    return top + jnp.log2(sum(jnp.exp2(p - top) for p in parts))


def row_sums(tile_ref, weights_ref, partial_ref):
    height = 64

    def body(block, _):
        rows = pl.ds(pl.multiple_of(block * height, height), height)
        acc = jnp.zeros((height, LANES), F32)
        for at in range(0, tile_ref.shape[1], LANES):
            acc += tile_ref[rows, at:at + LANES] * weights_ref[:, at:at + LANES]
        partial_ref[rows, :] = acc
        return _

    lax.fori_loop(0, tile_ref.shape[0] // height, body, 0)
    return row_form(partial_ref[...])


def column_sums(tile_ref, weights_ref, out_ref, scale_ref=None):
    starts = range(0, tile_ref.shape[1], LANES)

    def body(block, accs):
        for half in range(2):
            rows = pl.ds(pl.multiple_of(block * 16 + half * 8, 8), 8)
            weights = weights_ref[rows, :]
            accs = tuple(acc + tile_ref[rows, at:at + LANES] * weights for acc, at in zip(accs, starts))
        return accs

    accs = lax.fori_loop(0, tile_ref.shape[0] // 16, body, tuple(jnp.zeros((8, LANES), F32) for _ in starts))
    for acc, at in zip(accs, starts):
        total = jnp.sum(acc, axis=0, keepdims=True)
        out_ref[:, at:at + LANES] = total if scale_ref is None else total * scale_ref[:, at:at + LANES]


def exponent_block(crawl_ref, bench_ref, shift_ref, rows, columns):
    scores = transposed_dot(crawl_ref[rows, :], bench_ref[columns, :])
    return scores * KAPPA + shift_ref[:, columns]


def row_level_kernel(crawl_hbm, bench_hbm, duals_hbm, tile_ref, top_ref, level_ref, crawl_ref, bench_ref, shift_ref,
                     top_scratch, sum_scratch, sems):
    height = 64
    chunks = 4
    part = bench_ref.shape[0] // chunks
    copies = [pltpu.make_async_copy(crawl_hbm, crawl_ref, sems.at[chunks]),
              pltpu.make_async_copy(duals_hbm, shift_ref, sems.at[chunks + 1])]
    fetches = [
        pltpu.make_async_copy(bench_hbm.at[k * part:(k + 1) * part], bench_ref.at[k * part:(k + 1) * part], sems.at[k])
        for k in range(chunks)]
    for copy in (*copies, *fetches):
        copy.start()
    for copy in copies:
        copy.wait()
    shift_ref[...] = shift_ref[...] * KAPPA

    def fill(block, _, fetches=()):
        rows = pl.ds(pl.multiple_of(block * TALL, TALL), TALL)
        top = jnp.full((TALL, LANES), -jnp.inf, F32)
        for at in range(0, tile_ref.shape[1], WIDE):
            for k, fetch in enumerate(fetches):
                if at <= k * part < at + WIDE:
                    fetch.wait()
            exponent = exponent_block(crawl_ref, bench_ref, shift_ref, rows, pl.ds(at, WIDE))
            tile_ref[rows, at:at + WIDE] = exponent
            for lane in range(0, WIDE, LANES):
                top = jnp.maximum(top, exponent[:, lane:lane + LANES])
        top_scratch[rows, :] = top
        return _

    fill(0, 0, fetches)
    lax.fori_loop(1, tile_ref.shape[0] // TALL, fill, 0)

    def power(block, _):
        rows = pl.ds(pl.multiple_of(block * height, height), height)
        top = jnp.broadcast_to(jnp.max(top_scratch[rows, :], axis=1, keepdims=True), (height, LANES))
        acc = jnp.zeros((height, LANES), F32)
        for at in range(0, tile_ref.shape[1], LANES):
            value = jnp.exp2(tile_ref[rows, at:at + LANES] - top)
            tile_ref[rows, at:at + LANES] = value
            acc += value
        top_scratch[rows, :] = top
        sum_scratch[rows, :] = acc
        return _

    lax.fori_loop(0, tile_ref.shape[0] // height, power, 0)
    top = jnp.transpose(top_scratch[...])[0:1, :]
    top_ref[...] = top
    level_ref[...] = top + jnp.log2(row_form(sum_scratch[...]))


def column_level_kernel(parts, tile_ref, top_ref, *refs):
    part_refs, (crawl_ref, bench_ref, shift_ref, level_ref, out_ref, weights) = refs[:parts], refs[parts:]
    level = log_sum([p[...] for p in part_refs])
    level_ref[...] = level
    weights[...] = column_form(jnp.exp2(top_ref[...] - level))
    column_sums(tile_ref, weights, out_ref)
    out_ref[...] = jnp.log2(out_ref[...])

    @pl.when(jnp.min(out_ref[...]) < LOWEST)
    def _():
        weights[...] = column_form(level)
        blocks = tile_ref.shape[0] // TALL

        def column_block(column, _):
            columns = pl.ds(pl.multiple_of(column * WIDE, WIDE), WIDE)

            def logs(block):
                rows = pl.ds(pl.multiple_of(block * TALL, TALL), TALL)
                return exponent_block(crawl_ref, bench_ref, shift_ref, rows, columns) - weights[rows, 0:1]

            top = lax.fori_loop(
                0, blocks, lambda b, t: jnp.maximum(t, jnp.max(logs(b), axis=0, keepdims=True)),
                jnp.full((1, WIDE), -jnp.inf, F32))
            total = lax.fori_loop(
                0, blocks, lambda b, t: t + jnp.sum(jnp.exp2(logs(b) - top), axis=0, keepdims=True),
                jnp.zeros((1, WIDE), F32))
            out_ref[:, columns] = top + jnp.log2(total)
            return _

        lax.fori_loop(0, tile_ref.shape[1] // WIDE, column_block, 0)


def soft_kernel(parts, tile_ref, top_ref, level_ref, *refs):
    part_refs = refs[:parts]
    crawl_ref, bench_ref, shift_ref, soft_ref, left_ref, right_ref, mass_ref, sums_ref, partial, weights = refs[parts:]
    logs = log_sum([p[...] for p in part_refs])
    lowest = jnp.min(logs)

    @pl.when(lowest >= LOWEST)
    def _():
        left = jnp.exp2(top_ref[...] - level_ref[...])
        left_ref[...] = left
        right_ref[...] = jnp.exp2(-logs)
        mass_ref[...] = jnp.ones_like(logs)
        sums_ref[...] = row_sums(tile_ref, right_ref, partial) * left

    @pl.when(lowest < LOWEST)
    def _():
        left_ref[...] = jnp.ones_like(left_ref)
        mass_ref[...] = jnp.exp2(logs)
        right_ref[...] = logs
        weights[...] = column_form(level_ref[...])
        partial[...] = jnp.zeros_like(partial)

        def body(block, _):
            rows = pl.ds(pl.multiple_of(block * TALL, TALL), TALL)
            level = weights[rows, 0:1]

            def column_block(column, _):
                columns = pl.ds(pl.multiple_of(column * WIDE, WIDE), WIDE)
                exponent = exponent_block(crawl_ref, bench_ref, shift_ref, rows, columns)
                value = jnp.exp2(exponent - level - right_ref[:, columns])
                soft_ref[rows, columns] = value
                partial[rows, :] += sum(value[:, lane:lane + LANES] for lane in range(0, WIDE, LANES))
                return _

            return lax.fori_loop(0, tile_ref.shape[1] // WIDE, column_block, _)

        lax.fori_loop(0, tile_ref.shape[0] // TALL, body, 0)
        right_ref[...] = jnp.ones_like(right_ref)
        sums_ref[...] = row_form(partial[...])


def second_column_kernel(parts, soft_ref, left_ref, right_ref, *refs):
    part_refs, (inverse_ref, out_ref, weights) = refs[:parts], refs[parts:]
    inverse = left_ref[...] / sum(p[...] for p in part_refs)
    inverse_ref[...] = inverse
    weights[...] = column_form(inverse)
    column_sums(soft_ref, weights, out_ref, right_ref)


def second_row_kernel(parts, soft_ref, inverse_ref, right_ref, cotangent_ref, *refs):
    part_refs, (scaled_ref, out_ref, partial) = refs[:parts], refs[parts:]
    scaled_ref[...] = cotangent_ref[...] / sum(p[...] for p in part_refs) * right_ref[...]
    out_ref[...] = row_sums(soft_ref, scaled_ref, partial) * inverse_ref[...]


def first_column_kernel(parts, soft_ref, inverse_ref, right_ref, cotangent_ref, *refs):
    part_refs, (scaled_ref, out_ref, weights) = refs[:parts], refs[parts:]
    scaled = (cotangent_ref[...] - sum(p[...] for p in part_refs)) * inverse_ref[...]
    scaled_ref[...] = scaled
    weights[...] = column_form(-scaled)
    column_sums(soft_ref, weights, out_ref, right_ref)


def first_row_kernel(parts, soft_ref, left_ref, right_ref, *refs):
    part_refs, (back_ref, out_ref, partial) = refs[:parts], refs[parts:]
    back_ref[...] = sum(p[...] for p in part_refs) * right_ref[...]
    out_ref[...] = -row_sums(soft_ref, back_ref, partial) * left_ref[...]


def ring_order(n):
    return [*range(0, n, 2), *range(n - 1, 0, -2)]


def ring_share(n, at):
    me = lax.axis_index("rows")
    place = lax.rem(lax.select(lax.rem(me, 2) == 0, me // 2, n - 1 - me // 2) + at, n)
    return lax.select(place < n // 2, 2 * place, 2 * (n - 1 - place) + 1)


def thirds(x):
    parts = []
    for _ in range(3):
        parts.append(x.astype(jnp.bfloat16).astype(F32))
        x = x - parts[-1]
    return parts


def early_kernel(soft_ref, inverse_ref, scaled_ref, left_ref, scaled2_ref, right_ref, back_ref, mass_ref, *refs):
    first_ref, early_ref, row_parts, column_parts = refs
    row_parts[...] = jnp.zeros_like(row_parts)
    column_parts[...] = jnp.zeros_like(column_parts)
    at = 0
    for row, column in ((inverse_ref, scaled2_ref), (scaled_ref, right_ref), (left_ref, back_ref)):
        r, c = thirds(-row[...]), thirds(column[...])
        for i, j in ((0, 0), (0, 1), (1, 0), (1, 1), (0, 2), (2, 0)):
            row_parts[at:at + 1, :] = r[i]
            column_parts[at:at + 1, :] = c[j]
            at += 1

    def body(block, _):
        rows = pl.ds(pl.multiple_of(block * TALL, TALL), TALL)
        r = row_parts[:, rows].astype(jnp.bfloat16)
        for at in range(0, soft_ref.shape[1], WIDE):
            span = slice(at, at + WIDE)
            factor = lax.dot_general(
                r, column_parts[:, span].astype(jnp.bfloat16), (((0,), (0,)), ((), ())), preferred_element_type=F32)
            early_ref[rows, span] = soft_ref[rows, span] * factor
        return _

    lax.fori_loop(0, soft_ref.shape[0] // TALL, body, 0)
    mass = mass_ref[...]

    @pl.when(jnp.max(jnp.abs(mass - 1.0)) > 0.0)
    def _():
        def scale(block, _):
            rows = pl.ds(pl.multiple_of(block * 8, 8), 8)
            first_ref[rows, :] = soft_ref[rows, :] * mass_ref[...]
            return _

        lax.fori_loop(0, soft_ref.shape[0] // 8, scale, 0)


def score_grad(early, first, last):
    return (early + first * last).astype(jnp.bfloat16)


def far_kernel(parts, n, first_ref, early_ref, left_ref, crawl_ref, *refs):
    part_refs, (last_ref, *piece_refs, flat) = refs[:parts], refs[parts:]
    last_ref[...] = column_form(-left_ref[...] * sum(p[...] for p in part_refs))
    if not piece_refs:
        return
    width = flat.shape[1]
    start = ring_share(n, n // 2) * width
    flat[...] = jnp.zeros_like(flat)

    def body(block, _):
        rows = pl.ds(pl.multiple_of(block * TALL, TALL), TALL)
        last = last_ref[rows, :]
        pieces = []
        for lane in range(0, width, LANES):
            span = pl.ds(pl.multiple_of(start + lane, LANES), LANES)
            pieces.append(score_grad(early_ref[rows, span], first_ref[rows, span], last))
        grad = jnp.concatenate(pieces, axis=1)
        flat[...] += lax.dot_general(crawl_ref[rows, :], grad, (((0,), (0,)), ((), ())), preferred_element_type=F32)
        return _

    lax.fori_loop(0, first_ref.shape[0] // TALL, body, 0)
    half = width // 2
    for k, piece in enumerate(piece_refs):
        piece[...] = jnp.transpose(flat[:, k * half:(k + 1) * half])


def gradient_kernel(n, places, first_ref, early_ref, last_ref, crawl_ref, bench_ref, *refs):
    keep_ref, send_ref, *piece_refs, flat, whole, total = refs
    flat[...] = jnp.zeros_like(flat)

    def body(block, _):
        rows = pl.ds(pl.multiple_of(block * TALL, TALL), TALL)
        last = last_ref[rows, :]
        x = crawl_ref[rows, :]
        acc = jnp.zeros((TALL, LANES), F32)
        for at in range(0, first_ref.shape[1], WIDE):
            pieces = []
            for lane in range(at, at + WIDE, LANES):
                span = slice(lane, lane + LANES)
                pieces.append(score_grad(early_ref[rows, span], first_ref[rows, span], last))
            grad = jnp.concatenate(pieces, axis=1)
            acc += jnp.dot(grad, bench_ref[at:at + WIDE, :], preferred_element_type=F32)
            flat[:, at:at + WIDE] += lax.dot_general(x, grad, (((0,), (0,)), ((), ())), preferred_element_type=F32)
        total[rows, :] = acc
        return _

    lax.fori_loop(0, first_ref.shape[0] // TALL, body, 0)
    me = lax.axis_index("cols")
    quarter = total.shape[0] // 4
    for k, (ref, low) in enumerate(((keep_ref, 0), (send_ref, 0), (keep_ref, quarter), (send_ref, quarter))):
        start = pl.multiple_of(lax.bitwise_xor(me, k) * quarter, quarter)
        ref[low:low + quarter, :] = total[pl.ds(start, quarter), :]
    whole[...] = jnp.transpose(flat[...])
    height = piece_refs[0].shape[0]
    for k, piece in enumerate(piece_refs):
        start = ring_share(n, places[k // 2]) * 2 * height + k % 2 * height
        piece[...] = whole[pl.ds(pl.multiple_of(start, height), height), :]


def placing_kernel(n, *refs):
    (own_ref, beside_ref, pair_ref, *pieces), (crawl_out, bench_out, sems) = refs[:-3], refs[-3:]
    me = lax.axis_index("cols")
    quarter = own_ref.shape[0]
    moves = []
    for k, piece in ((0, own_ref), (2, beside_ref), (1, pair_ref.at[:quarter]), (3, pair_ref.at[quarter:])):
        start = pl.multiple_of(lax.bitwise_xor(me, k) * quarter, quarter)
        moves.append((piece, crawl_out.at[pl.ds(start, quarter)]))
    height = pieces[0].shape[0]
    for at, piece in enumerate(pieces):
        start = pl.multiple_of(ring_share(n, at // 2) * 2 * height + at % 2 * height, height)
        moves.append((piece, bench_out.at[pl.ds(start, height)]))
    copies = [pltpu.make_async_copy(source, target, sems.at[k]) for k, (source, target) in enumerate(moves)]
    for copy in copies:
        copy.start()
    for copy in copies:
        copy.wait()


def call(kernel, args, outs, scratch, aliases=None):
    return pl.pallas_call(
        kernel,
        in_specs=[pl.BlockSpec(memory_space=pltpu.VMEM)] * len(args),
        out_specs=[pl.BlockSpec(memory_space=pltpu.VMEM)] * len(outs),
        out_shape=outs,
        scratch_shapes=[pltpu.VMEM(shape, F32) for shape in scratch],
        input_output_aliases=aliases or {},
        compiler_params=pltpu.CompilerParams(vmem_limit_bytes=LIMIT),
    )(*args)


def shaped(*shape, kind=F32):
    return jax.ShapeDtypeStruct(shape, kind)


def resident(*shape, kind=F32):
    return pltpu.VMEM(shape, kind)


def kept(x):
    return pltpu.with_memory_space_constraint(x, pltpu.VMEM)


def exchange(x, axis, stride, size):
    n = lax.axis_size(axis)
    return [x] + [lax.ppermute(x, axis, [(i, i ^ (k * stride)) for i in range(n)]) for k in range(1, size)]


def spread(x, axis, first, join):
    n = lax.axis_size(axis)
    stride, size = 1, min(first, n)
    while True:
        parts = exchange(x, axis, stride, size)
        stride *= size
        if stride == n:
            return parts
        x = join(parts)
        size = min(4, n // stride)


def ring_all_reduce(pieces, n):
    order = ring_order(n)
    up = [(order[p], order[(p + 1) % n]) for p in range(n)]
    down = [(b, a) for a, b in up]
    far = n // 2
    mine = [[pieces[2 * at], pieces[2 * at + 1]] for at in range(n)]

    def ahead(x):
        return lax.ppermute(x, "rows", up)

    def behind(x):
        return lax.ppermute(x, "rows", down)

    rise, fall = [ahead(mine[far][0]), None], [None, behind(mine[far][1])]
    for step in range(far - 1, 0, -1):
        rise = [ahead(m if r is None else m + r) for m, r in zip(mine[step], rise)]
        fall = [behind(m if f is None else m + f) for m, f in zip(mine[-step], fall)]
    own = [m + r + f for m, r, f in zip(mine[0], rise, fall)]
    found = {0: own}
    rise = fall = own
    for step in range(1, far):
        rise, fall = [ahead(r) for r in rise], [behind(f) for f in fall]
        found[n - step], found[step] = rise, fall
    found[far] = [ahead(rise[0]), behind(fall[1])]
    return [half for at in range(n) for half in found[at]]


def quarter_all_reduce(keep, send):
    quarter = keep.shape[0] // 2
    keep = keep + exchange(send, "cols", 1, 2)[1]
    own = keep[:quarter] + exchange(keep[quarter:], "cols", 2, 2)[1]
    beside = exchange(own, "cols", 2, 2)[1]
    return own, beside, exchange(jnp.concatenate([own, beside]), "cols", 1, 2)[1]


def per_device(crawl, bench, start_duals, row_cotangent, col_cotangent):
    rows, columns = crawl.shape[0], bench.shape[0]
    row_cotangent = row_cotangent.reshape(1, rows)
    col_cotangent = col_cotangent.reshape(1, columns)
    row, column, tall = shaped(1, rows), shaped(1, columns), (rows, LANES)
    tile_shape = resident(rows, columns)

    def over_cols(x, join=sum):
        return spread(x, "cols", 4, join)

    def over_rows(x, join=sum):
        n = lax.axis_size("rows")
        if n > 8:
            return spread(x, "rows", 4, join)
        copies = jnp.broadcast_to(x.reshape(1, -1, LANES), (n, columns // LANES, LANES))
        return [join(list(lax.all_to_all(copies, "rows", 0, 0))).reshape(1, columns)]

    tile, top, local, crawl, bench, shift = pl.pallas_call(
        row_level_kernel,
        in_specs=[pl.BlockSpec(memory_space=pltpu.HBM)] * 3,
        out_specs=[pl.BlockSpec(memory_space=pltpu.VMEM)] * 6,
        out_shape=[tile_shape, row, row, resident(*crawl.shape, kind=crawl.dtype), resident(*bench.shape, kind=bench.dtype),
                   resident(1, columns)],
        scratch_shapes=[pltpu.VMEM(tall, F32)] * 2 + [pltpu.SemaphoreType.DMA((6,))],
        compiler_params=pltpu.CompilerParams(vmem_limit_bytes=LIMIT),
    )(*(pltpu.with_memory_space_constraint(x, pltpu.HBM) for x in (crawl, bench, start_duals.reshape(1, columns))))
    crawl, bench, shift = kept(crawl), kept(bench), kept(shift)
    parts = over_cols(local, log_sum)
    level, local = call(
        functools.partial(column_level_kernel, len(parts)),
        [kept(tile), top, *parts, crawl, bench, shift], [row, column], [tall])
    parts = over_rows(local, log_sum)
    soft, left, right, mass, local = call(
        functools.partial(soft_kernel, len(parts)),
        [kept(tile), top, level, *parts, crawl, bench, shift], [tile_shape, row, column, column, row],
        [tall, tall], aliases={0: 0})
    soft = kept(soft)
    parts = over_cols(local)
    inverse, local = call(
        functools.partial(second_column_kernel, len(parts)), [soft, left, right, *parts], [row, column], [tall])
    parts = over_rows(local)
    scaled2, local = call(
        functools.partial(second_row_kernel, len(parts)),
        [soft, inverse, right, col_cotangent, *parts], [column, row], [tall])
    parts = over_cols(local)
    scaled, local = call(
        functools.partial(first_column_kernel, len(parts)),
        [soft, inverse, right, row_cotangent, *parts], [row, column], [tall])
    parts = over_rows(local)
    back, local = call(
        functools.partial(first_row_kernel, len(parts)), [soft, left, right, *parts], [column, row], [tall])
    parts = over_cols(local)
    n = lax.axis_size("rows")
    width = bench.shape[1]
    share = columns // n
    piece = shaped(share // 2, width)
    ahead = share % (2 * LANES) == 0
    first, early = call(
        early_kernel, [soft, inverse, scaled, left, scaled2, right, back, mass],
        [tile_shape, tile_shape], [(32, rows), (32, columns)], aliases={0: 0})
    first, early = kept(first), kept(early)
    last, *far = call(
        functools.partial(far_kernel, len(parts), n), [first, early, left, crawl, *parts],
        [shaped(*tall)] + [piece] * (2 * ahead), [(LANES, share)])
    places = [at for at in range(n) if at != n // 2 or not ahead]
    keep, send, *pieces = call(
        functools.partial(gradient_kernel, n, places),
        [first, early, last, crawl, bench],
        [shaped(rows // 2, width)] * 2 + [piece] * (2 * len(places)), [(LANES, columns), (columns, LANES), tall])
    if ahead:
        pieces[n:n] = far
    pieces = ring_all_reduce(pieces, n)
    quarters = quarter_all_reduce(keep, send)
    crawl_grad, bench_grad = pl.pallas_call(
        functools.partial(placing_kernel, n),
        in_specs=[pl.BlockSpec(memory_space=pltpu.VMEM)] * (3 + len(pieces)),
        out_specs=[pl.BlockSpec(memory_space=pl.ANY)] * 2,
        out_shape=[shaped(rows, width), shaped(columns, width)],
        scratch_shapes=[pltpu.SemaphoreType.DMA((4 + len(pieces),))],
        compiler_params=pltpu.CompilerParams(vmem_limit_bytes=LIMIT),
    )(*map(kept, (*quarters, *pieces)))
    return (crawl_grad, bench_grad)


def solution(mesh):
    placed = (P("rows", None), P("cols", None), P("cols"), P("rows"), P("cols"))
    return jax.shard_map(
        per_device,
        mesh=mesh,
        in_specs=placed,
        out_specs=(P("rows", None), P("cols", None)),
        check_vma=False,
    )
```

```python
import functools
import math

import jax
import jax.numpy as jnp
from jax import lax
from jax.experimental import pallas as pl
from jax.experimental.pallas import tpu as pltpu
from jax.sharding import PartitionSpec as P

EPSILON = 0.05
KAPPA = math.log2(math.e) / EPSILON
LOWEST = -64.0
LANES = 128
WIDE = 512
TALL = 1024
LIMIT = 8 * 2**20
F32 = jnp.float32


def transposed_dot(a, b):
    return lax.dot_general(a, b, (((1,), (1,)), ((), ())), preferred_element_type=F32)


def column_form(row):
    return jnp.transpose(jnp.broadcast_to(row, (LANES, row.shape[1])))


def row_form(partial):
    return jnp.sum(jnp.transpose(partial), axis=0, keepdims=True)


def log_sum(parts):
    top = functools.reduce(jnp.maximum, parts)
    return top + jnp.log2(sum(jnp.exp2(p - top) for p in parts))


def row_sums(tile_ref, weights_ref, partial_ref):
    height = 64

    def body(block, _):
        rows = pl.ds(pl.multiple_of(block * height, height), height)
        acc = jnp.zeros((height, LANES), F32)
        for at in range(0, tile_ref.shape[1], LANES):
            acc += tile_ref[rows, at:at + LANES] * weights_ref[:, at:at + LANES]
        partial_ref[rows, :] = acc
        return _

    lax.fori_loop(0, tile_ref.shape[0] // height, body, 0)
    return row_form(partial_ref[...])


def column_sums(tile_ref, weights_ref, out_ref, scale_ref=None):
    starts = range(0, tile_ref.shape[1], LANES)

    def body(block, accs):
        for half in range(2):
            rows = pl.ds(pl.multiple_of(block * 16 + half * 8, 8), 8)
            weights = weights_ref[rows, :]
            accs = tuple(acc + tile_ref[rows, at:at + LANES] * weights for acc, at in zip(accs, starts))
        return accs

    accs = lax.fori_loop(0, tile_ref.shape[0] // 16, body, tuple(jnp.zeros((8, LANES), F32) for _ in starts))
    for acc, at in zip(accs, starts):
        total = jnp.sum(acc, axis=0, keepdims=True)
        out_ref[:, at:at + LANES] = total if scale_ref is None else total * scale_ref[:, at:at + LANES]


def exponent_block(crawl_ref, bench_ref, shift_ref, rows, columns):
    scores = transposed_dot(crawl_ref[rows, :], bench_ref[columns, :])
    return scores * KAPPA + shift_ref[:, columns]


def row_level_kernel(crawl_hbm, bench_hbm, duals_hbm, tile_ref, top_ref, level_ref, crawl_ref, bench_ref, shift_ref,
                     top_scratch, sum_scratch, sems):
    height = 64
    chunks = 4
    part = bench_ref.shape[0] // chunks
    copies = [pltpu.make_async_copy(crawl_hbm, crawl_ref, sems.at[chunks]),
              pltpu.make_async_copy(duals_hbm, shift_ref, sems.at[chunks + 1])]
    fetches = [
        pltpu.make_async_copy(bench_hbm.at[k * part:(k + 1) * part], bench_ref.at[k * part:(k + 1) * part], sems.at[k])
        for k in range(chunks)]
    for copy in (*copies, *fetches):
        copy.start()
    for copy in copies:
        copy.wait()
    shift_ref[...] = shift_ref[...] * KAPPA

    def fill(block, _, fetches=()):
        rows = pl.ds(pl.multiple_of(block * TALL, TALL), TALL)
        top = jnp.full((TALL, LANES), -jnp.inf, F32)
        for at in range(0, tile_ref.shape[1], WIDE):
            for k, fetch in enumerate(fetches):
                if at <= k * part < at + WIDE:
                    fetch.wait()
            exponent = exponent_block(crawl_ref, bench_ref, shift_ref, rows, pl.ds(at, WIDE))
            tile_ref[rows, at:at + WIDE] = exponent
            for lane in range(0, WIDE, LANES):
                top = jnp.maximum(top, exponent[:, lane:lane + LANES])
        top_scratch[rows, :] = top
        return _

    fill(0, 0, fetches)
    lax.fori_loop(1, tile_ref.shape[0] // TALL, fill, 0)

    def power(block, _):
        rows = pl.ds(pl.multiple_of(block * height, height), height)
        top = jnp.broadcast_to(jnp.max(top_scratch[rows, :], axis=1, keepdims=True), (height, LANES))
        acc = jnp.zeros((height, LANES), F32)
        for at in range(0, tile_ref.shape[1], LANES):
            value = jnp.exp2(tile_ref[rows, at:at + LANES] - top)
            tile_ref[rows, at:at + LANES] = value
            acc += value
        top_scratch[rows, :] = top
        sum_scratch[rows, :] = acc
        return _

    lax.fori_loop(0, tile_ref.shape[0] // height, power, 0)
    top = jnp.transpose(top_scratch[...])[0:1, :]
    top_ref[...] = top
    level_ref[...] = top + jnp.log2(row_form(sum_scratch[...]))


def column_level_kernel(parts, tile_ref, top_ref, *refs):
    part_refs, (crawl_ref, bench_ref, shift_ref, level_ref, out_ref, weights) = refs[:parts], refs[parts:]
    level = log_sum([p[...] for p in part_refs])
    level_ref[...] = level
    weights[...] = column_form(jnp.exp2(top_ref[...] - level))
    column_sums(tile_ref, weights, out_ref)
    out_ref[...] = jnp.log2(out_ref[...])

    @pl.when(jnp.min(out_ref[...]) < LOWEST)
    def _():
        weights[...] = column_form(level)
        blocks = tile_ref.shape[0] // TALL

        def column_block(column, _):
            columns = pl.ds(pl.multiple_of(column * WIDE, WIDE), WIDE)

            def logs(block):
                rows = pl.ds(pl.multiple_of(block * TALL, TALL), TALL)
                return exponent_block(crawl_ref, bench_ref, shift_ref, rows, columns) - weights[rows, 0:1]

            top = lax.fori_loop(
                0, blocks, lambda b, t: jnp.maximum(t, jnp.max(logs(b), axis=0, keepdims=True)),
                jnp.full((1, WIDE), -jnp.inf, F32))
            total = lax.fori_loop(
                0, blocks, lambda b, t: t + jnp.sum(jnp.exp2(logs(b) - top), axis=0, keepdims=True),
                jnp.zeros((1, WIDE), F32))
            out_ref[:, columns] = top + jnp.log2(total)
            return _

        lax.fori_loop(0, tile_ref.shape[1] // WIDE, column_block, 0)


def soft_kernel(parts, tile_ref, top_ref, level_ref, *refs):
    part_refs = refs[:parts]
    crawl_ref, bench_ref, shift_ref, soft_ref, left_ref, right_ref, mass_ref, sums_ref, partial, weights = refs[parts:]
    logs = log_sum([p[...] for p in part_refs])
    lowest = jnp.min(logs)

    @pl.when(lowest >= LOWEST)
    def _():
        left = jnp.exp2(top_ref[...] - level_ref[...])
        left_ref[...] = left
        right_ref[...] = jnp.exp2(-logs)
        mass_ref[...] = jnp.ones_like(logs)
        sums_ref[...] = row_sums(tile_ref, right_ref, partial) * left

    @pl.when(lowest < LOWEST)
    def _():
        left_ref[...] = jnp.ones_like(left_ref)
        mass_ref[...] = jnp.exp2(logs)
        right_ref[...] = logs
        weights[...] = column_form(level_ref[...])
        partial[...] = jnp.zeros_like(partial)

        def body(block, _):
            rows = pl.ds(pl.multiple_of(block * TALL, TALL), TALL)
            level = weights[rows, 0:1]

            def column_block(column, _):
                columns = pl.ds(pl.multiple_of(column * WIDE, WIDE), WIDE)
                exponent = exponent_block(crawl_ref, bench_ref, shift_ref, rows, columns)
                value = jnp.exp2(exponent - level - right_ref[:, columns])
                soft_ref[rows, columns] = value
                partial[rows, :] += sum(value[:, lane:lane + LANES] for lane in range(0, WIDE, LANES))
                return _

            return lax.fori_loop(0, tile_ref.shape[1] // WIDE, column_block, _)

        lax.fori_loop(0, tile_ref.shape[0] // TALL, body, 0)
        right_ref[...] = jnp.ones_like(right_ref)
        sums_ref[...] = row_form(partial[...])


def second_column_kernel(parts, soft_ref, left_ref, right_ref, *refs):
    part_refs, (inverse_ref, out_ref, weights) = refs[:parts], refs[parts:]
    inverse = left_ref[...] / sum(p[...] for p in part_refs)
    inverse_ref[...] = inverse
    weights[...] = column_form(inverse)
    column_sums(soft_ref, weights, out_ref, right_ref)


def second_row_kernel(parts, soft_ref, inverse_ref, right_ref, cotangent_ref, *refs):
    part_refs, (scaled_ref, out_ref, partial) = refs[:parts], refs[parts:]
    scaled_ref[...] = cotangent_ref[...] / sum(p[...] for p in part_refs) * right_ref[...]
    out_ref[...] = row_sums(soft_ref, scaled_ref, partial) * inverse_ref[...]


def first_column_kernel(parts, soft_ref, inverse_ref, right_ref, cotangent_ref, *refs):
    part_refs, (scaled_ref, out_ref, weights) = refs[:parts], refs[parts:]
    scaled = (cotangent_ref[...] - sum(p[...] for p in part_refs)) * inverse_ref[...]
    scaled_ref[...] = scaled
    weights[...] = column_form(-scaled)
    column_sums(soft_ref, weights, out_ref, right_ref)


def first_row_kernel(parts, soft_ref, left_ref, right_ref, *refs):
    part_refs, (back_ref, out_ref, partial) = refs[:parts], refs[parts:]
    back_ref[...] = sum(p[...] for p in part_refs) * right_ref[...]
    out_ref[...] = -row_sums(soft_ref, back_ref, partial) * left_ref[...]


def ring_order(n):
    return [*range(0, n, 2), *range(n - 1, 0, -2)]


def ring_share(n, at):
    me = lax.axis_index("rows")
    place = lax.rem(lax.select(lax.rem(me, 2) == 0, me // 2, n - 1 - me // 2) + at, n)
    return lax.select(place < n // 2, 2 * place, 2 * (n - 1 - place) + 1)


def thirds(x):
    parts = []
    for _ in range(3):
        parts.append(x.astype(jnp.bfloat16).astype(F32))
        x = x - parts[-1]
    return parts


def early_kernel(soft_ref, inverse_ref, scaled_ref, left_ref, scaled2_ref, right_ref, back_ref, mass_ref, *refs):
    first_ref, early_ref, row_parts, column_parts = refs
    row_parts[...] = jnp.zeros_like(row_parts)
    column_parts[...] = jnp.zeros_like(column_parts)
    at = 0
    for row, column in ((inverse_ref, scaled2_ref), (scaled_ref, right_ref), (left_ref, back_ref)):
        r, c = thirds(-row[...]), thirds(column[...])
        for i, j in ((0, 0), (0, 1), (1, 0), (1, 1), (0, 2), (2, 0)):
            row_parts[at:at + 1, :] = r[i]
            column_parts[at:at + 1, :] = c[j]
            at += 1

    def body(block, _):
        rows = pl.ds(pl.multiple_of(block * TALL, TALL), TALL)
        r = row_parts[:, rows].astype(jnp.bfloat16)
        for at in range(0, soft_ref.shape[1], WIDE):
            span = slice(at, at + WIDE)
            factor = lax.dot_general(
                r, column_parts[:, span].astype(jnp.bfloat16), (((0,), (0,)), ((), ())), preferred_element_type=F32)
            early_ref[rows, span] = soft_ref[rows, span] * factor
        return _

    lax.fori_loop(0, soft_ref.shape[0] // TALL, body, 0)
    mass = mass_ref[...]

    @pl.when(jnp.max(jnp.abs(mass - 1.0)) > 0.0)
    def _():
        def scale(block, _):
            rows = pl.ds(pl.multiple_of(block * 8, 8), 8)
            first_ref[rows, :] = soft_ref[rows, :] * mass_ref[...]
            return _

        lax.fori_loop(0, soft_ref.shape[0] // 8, scale, 0)


def score_grad(early, first, last):
    return (early + first * last).astype(jnp.bfloat16)


def far_kernel(parts, n, first_ref, early_ref, left_ref, crawl_ref, *refs):
    part_refs, (last_ref, *piece_refs, flat) = refs[:parts], refs[parts:]
    last_ref[...] = column_form(-left_ref[...] * sum(p[...] for p in part_refs))
    if not piece_refs:
        return
    width = flat.shape[1]
    start = ring_share(n, n // 2) * width
    flat[...] = jnp.zeros_like(flat)

    def body(block, _):
        rows = pl.ds(pl.multiple_of(block * TALL, TALL), TALL)
        last = last_ref[rows, :]
        pieces = []
        for lane in range(0, width, LANES):
            span = pl.ds(pl.multiple_of(start + lane, LANES), LANES)
            pieces.append(score_grad(early_ref[rows, span], first_ref[rows, span], last))
        grad = jnp.concatenate(pieces, axis=1)
        flat[...] += lax.dot_general(crawl_ref[rows, :], grad, (((0,), (0,)), ((), ())), preferred_element_type=F32)
        return _

    lax.fori_loop(0, first_ref.shape[0] // TALL, body, 0)
    half = width // 2
    for k, piece in enumerate(piece_refs):
        piece[...] = jnp.transpose(flat[:, k * half:(k + 1) * half])


def gradient_kernel(n, places, first_ref, early_ref, last_ref, crawl_ref, bench_ref, *refs):
    keep_ref, send_ref, *piece_refs, flat, whole, total = refs
    flat[...] = jnp.zeros_like(flat)

    def body(block, _):
        rows = pl.ds(pl.multiple_of(block * TALL, TALL), TALL)
        last = last_ref[rows, :]
        x = crawl_ref[rows, :]
        acc = jnp.zeros((TALL, LANES), F32)
        for at in range(0, first_ref.shape[1], WIDE):
            pieces = []
            for lane in range(at, at + WIDE, LANES):
                span = slice(lane, lane + LANES)
                pieces.append(score_grad(early_ref[rows, span], first_ref[rows, span], last))
            grad = jnp.concatenate(pieces, axis=1)
            acc += jnp.dot(grad, bench_ref[at:at + WIDE, :], preferred_element_type=F32)
            flat[:, at:at + WIDE] += lax.dot_general(x, grad, (((0,), (0,)), ((), ())), preferred_element_type=F32)
        total[rows, :] = acc
        return _

    lax.fori_loop(0, first_ref.shape[0] // TALL, body, 0)
    me = lax.axis_index("cols")
    quarter = total.shape[0] // 4
    for k, (ref, low) in enumerate(((keep_ref, 0), (send_ref, 0), (keep_ref, quarter), (send_ref, quarter))):
        start = pl.multiple_of(lax.bitwise_xor(me, k) * quarter, quarter)
        ref[low:low + quarter, :] = total[pl.ds(start, quarter), :]
    whole[...] = jnp.transpose(flat[...])
    height = piece_refs[0].shape[0]
    for k, piece in enumerate(piece_refs):
        start = ring_share(n, places[k // 2]) * 2 * height + k % 2 * height
        piece[...] = whole[pl.ds(pl.multiple_of(start, height), height), :]


def placing_kernel(n, *refs):
    (own_ref, beside_ref, pair_ref, *pieces), (crawl_out, bench_out, sems) = refs[:-3], refs[-3:]
    me = lax.axis_index("cols")
    quarter = own_ref.shape[0]
    moves = []
    for k, piece in ((0, own_ref), (2, beside_ref), (1, pair_ref.at[:quarter]), (3, pair_ref.at[quarter:])):
        start = pl.multiple_of(lax.bitwise_xor(me, k) * quarter, quarter)
        moves.append((piece, crawl_out.at[pl.ds(start, quarter)]))
    height = pieces[0].shape[0]
    for at, piece in enumerate(pieces):
        start = pl.multiple_of(ring_share(n, at // 2) * 2 * height + at % 2 * height, height)
        moves.append((piece, bench_out.at[pl.ds(start, height)]))
    copies = [pltpu.make_async_copy(source, target, sems.at[k]) for k, (source, target) in enumerate(moves)]
    for copy in copies:
        copy.start()
    for copy in copies:
        copy.wait()


def call(kernel, args, outs, scratch, aliases=None):
    return pl.pallas_call(
        kernel,
        in_specs=[pl.BlockSpec(memory_space=pltpu.VMEM)] * len(args),
        out_specs=[pl.BlockSpec(memory_space=pltpu.VMEM)] * len(outs),
        out_shape=outs,
        scratch_shapes=[pltpu.VMEM(shape, F32) for shape in scratch],
        input_output_aliases=aliases or {},
        compiler_params=pltpu.CompilerParams(vmem_limit_bytes=LIMIT),
    )(*args)


def shaped(*shape, kind=F32):
    return jax.ShapeDtypeStruct(shape, kind)


def resident(*shape, kind=F32):
    return pltpu.VMEM(shape, kind)


def kept(x):
    return pltpu.with_memory_space_constraint(x, pltpu.VMEM)


def exchange(x, axis, stride, size):
    n = lax.axis_size(axis)
    return [x] + [lax.ppermute(x, axis, [(i, i ^ (k * stride)) for i in range(n)]) for k in range(1, size)]


def spread(x, axis, first, join):
    n = lax.axis_size(axis)
    stride, size = 1, min(first, n)
    while True:
        parts = exchange(x, axis, stride, size)
        stride *= size
        if stride == n:
            return parts
        x = join(parts)
        size = min(4, n // stride)


def ring_all_reduce(pieces, n):
    order = ring_order(n)
    up = [(order[p], order[(p + 1) % n]) for p in range(n)]
    down = [(b, a) for a, b in up]
    far = n // 2
    mine = [[pieces[2 * at], pieces[2 * at + 1]] for at in range(n)]

    def ahead(x):
        return lax.ppermute(x, "rows", up)

    def behind(x):
        return lax.ppermute(x, "rows", down)

    rise, fall = [ahead(mine[far][0]), None], [None, behind(mine[far][1])]
    for step in range(far - 1, 0, -1):
        rise = [ahead(m if r is None else m + r) for m, r in zip(mine[step], rise)]
        fall = [behind(m if f is None else m + f) for m, f in zip(mine[-step], fall)]
    own = [m + r + f for m, r, f in zip(mine[0], rise, fall)]
    found = {0: own}
    rise = fall = own
    for step in range(1, far):
        rise, fall = [ahead(r) for r in rise], [behind(f) for f in fall]
        found[n - step], found[step] = rise, fall
    found[far] = [ahead(rise[0]), behind(fall[1])]
    return [half for at in range(n) for half in found[at]]


def quarter_all_reduce(keep, send):
    quarter = keep.shape[0] // 2
    keep = keep + exchange(send, "cols", 1, 2)[1]
    own = keep[:quarter] + exchange(keep[quarter:], "cols", 2, 2)[1]
    beside = exchange(own, "cols", 2, 2)[1]
    return own, beside, exchange(jnp.concatenate([own, beside]), "cols", 1, 2)[1]


def per_device(crawl, bench, start_duals, row_cotangent, col_cotangent):
    rows, columns = crawl.shape[0], bench.shape[0]
    row_cotangent = row_cotangent.reshape(1, rows)
    col_cotangent = col_cotangent.reshape(1, columns)
    row, column, tall = shaped(1, rows), shaped(1, columns), (rows, LANES)
    tile_shape = resident(rows, columns)

    def over_cols(x, join=sum):
        return spread(x, "cols", 4, join)

    def over_rows(x, join=sum):
        n = lax.axis_size("rows")
        if n > 8:
            return spread(x, "rows", 4, join)
        copies = jnp.broadcast_to(x.reshape(1, -1, LANES), (n, columns // LANES, LANES))
        return [join(list(lax.all_to_all(copies, "rows", 0, 0))).reshape(1, columns)]

    tile, top, local, crawl, bench, shift = pl.pallas_call(
        row_level_kernel,
        in_specs=[pl.BlockSpec(memory_space=pltpu.HBM)] * 3,
        out_specs=[pl.BlockSpec(memory_space=pltpu.VMEM)] * 6,
        out_shape=[tile_shape, row, row, resident(*crawl.shape, kind=crawl.dtype), resident(*bench.shape, kind=bench.dtype),
                   resident(1, columns)],
        scratch_shapes=[pltpu.VMEM(tall, F32)] * 2 + [pltpu.SemaphoreType.DMA((6,))],
        compiler_params=pltpu.CompilerParams(vmem_limit_bytes=LIMIT),
    )(*(pltpu.with_memory_space_constraint(x, pltpu.HBM) for x in (crawl, bench, start_duals.reshape(1, columns))))
    crawl, bench, shift = kept(crawl), kept(bench), kept(shift)
    parts = over_cols(local, log_sum)
    level, local = call(
        functools.partial(column_level_kernel, len(parts)),
        [kept(tile), top, *parts, crawl, bench, shift], [row, column], [tall])
    parts = over_rows(local, log_sum)
    soft, left, right, mass, local = call(
        functools.partial(soft_kernel, len(parts)),
        [kept(tile), top, level, *parts, crawl, bench, shift], [tile_shape, row, column, column, row],
        [tall, tall], aliases={0: 0})
    soft = kept(soft)
    parts = over_cols(local)
    inverse, local = call(
        functools.partial(second_column_kernel, len(parts)), [soft, left, right, *parts], [row, column], [tall])
    parts = over_rows(local)
    scaled2, local = call(
        functools.partial(second_row_kernel, len(parts)),
        [soft, inverse, right, col_cotangent, *parts], [column, row], [tall])
    parts = over_cols(local)
    scaled, local = call(
        functools.partial(first_column_kernel, len(parts)),
        [soft, inverse, right, row_cotangent, *parts], [row, column], [tall])
    parts = over_rows(local)
    back, local = call(
        functools.partial(first_row_kernel, len(parts)), [soft, left, right, *parts], [column, row], [tall])
    parts = over_cols(local)
    n = lax.axis_size("rows")
    width = bench.shape[1]
    share = columns // n
    piece = shaped(share // 2, width)
    ahead = share % (2 * LANES) == 0
    first, early = call(
        early_kernel, [soft, inverse, scaled, left, scaled2, right, back, mass],
        [tile_shape, tile_shape], [(32, rows), (32, columns)], aliases={0: 0})
    first, early = kept(first), kept(early)
    last, *far = call(
        functools.partial(far_kernel, len(parts), n), [first, early, left, crawl, *parts],
        [shaped(*tall)] + [piece] * (2 * ahead), [(LANES, share)])
    places = [at for at in range(n) if at != n // 2 or not ahead]
    keep, send, *pieces = call(
        functools.partial(gradient_kernel, n, places),
        [first, early, last, crawl, bench],
        [shaped(rows // 2, width)] * 2 + [piece] * (2 * len(places)), [(LANES, columns), (columns, LANES), tall])
    if ahead:
        pieces[n:n] = far
    pieces = ring_all_reduce(pieces, n)
    quarters = quarter_all_reduce(keep, send)
    crawl_grad, bench_grad = pl.pallas_call(
        functools.partial(placing_kernel, n),
        in_specs=[pl.BlockSpec(memory_space=pltpu.VMEM)] * (3 + len(pieces)),
        out_specs=[pl.BlockSpec(memory_space=pl.ANY)] * 2,
        out_shape=[shaped(rows, width), shaped(columns, width)],
        scratch_shapes=[pltpu.SemaphoreType.DMA((4 + len(pieces),))],
        compiler_params=pltpu.CompilerParams(vmem_limit_bytes=LIMIT),
    )(*map(kept, (*quarters, *pieces)))
    return (crawl_grad, bench_grad)


def solution(mesh):
    placed = (P("rows", None), P("cols", None), P("cols"), P("rows"), P("cols"))
    return jax.shard_map(
        per_device,
        mesh=mesh,
        in_specs=placed,
        out_specs=(P("rows", None), P("cols", None)),
        check_vma=False,
    )
```

```python
import functools
import math

import jax
import jax.numpy as jnp
from jax import lax
from jax.experimental import pallas as pl
from jax.experimental.pallas import tpu as pltpu
from jax.sharding import PartitionSpec as P

EPSILON = 0.05
KAPPA = math.log2(math.e) / EPSILON
LOWEST = -64.0
LANES = 128
WIDE = 1024
TALL = 1024
LIMIT = 8 * 2**20
F32 = jnp.float32


def transposed_dot(a, b):
    return lax.dot_general(a, b, (((1,), (1,)), ((), ())), preferred_element_type=F32)


def column_form(row):
    return jnp.transpose(jnp.broadcast_to(row, (LANES, row.shape[1])))


def row_form(partial):
    return jnp.sum(jnp.transpose(partial), axis=0, keepdims=True)


def log_sum(parts):
    top = functools.reduce(jnp.maximum, parts)
    return top + jnp.log2(sum(jnp.exp2(p - top) for p in parts))


def row_sums(tile_ref, weights_ref, partial_ref):
    height = 64

    def body(block, _):
        rows = pl.ds(pl.multiple_of(block * height, height), height)
        acc = jnp.zeros((height, LANES), F32)
        for at in range(0, tile_ref.shape[1], LANES):
            acc += tile_ref[rows, at:at + LANES] * weights_ref[:, at:at + LANES]
        partial_ref[rows, :] = acc
        return _

    lax.fori_loop(0, tile_ref.shape[0] // height, body, 0)
    return row_form(partial_ref[...])


def column_sums(tile_ref, weights_ref, out_ref, scale_ref=None):
    starts = range(0, tile_ref.shape[1], LANES)

    def body(block, accs):
        for half in range(2):
            rows = pl.ds(pl.multiple_of(block * 16 + half * 8, 8), 8)
            weights = weights_ref[rows, :]
            accs = tuple(acc + tile_ref[rows, at:at + LANES] * weights for acc, at in zip(accs, starts))
        return accs

    accs = lax.fori_loop(0, tile_ref.shape[0] // 16, body, tuple(jnp.zeros((8, LANES), F32) for _ in starts))
    for acc, at in zip(accs, starts):
        total = jnp.sum(acc, axis=0, keepdims=True)
        out_ref[:, at:at + LANES] = total if scale_ref is None else total * scale_ref[:, at:at + LANES]


def exponent_block(crawl_ref, bench_ref, shift_ref, rows, columns):
    scores = transposed_dot(crawl_ref[rows, :], bench_ref[columns, :])
    return scores * KAPPA + shift_ref[:, columns]


def row_level_kernel(crawl_hbm, bench_hbm, duals_hbm, tile_ref, top_ref, level_ref, crawl_ref, bench_ref, shift_ref,
                     top_scratch, sum_scratch, sems):
    height = 64
    chunks = 4
    part = bench_ref.shape[0] // chunks
    copies = [pltpu.make_async_copy(crawl_hbm, crawl_ref, sems.at[chunks]),
              pltpu.make_async_copy(duals_hbm, shift_ref, sems.at[chunks + 1])]
    fetches = [
        pltpu.make_async_copy(bench_hbm.at[k * part:(k + 1) * part], bench_ref.at[k * part:(k + 1) * part], sems.at[k])
        for k in range(chunks)]
    for copy in (*copies, *fetches):
        copy.start()
    for copy in copies:
        copy.wait()
    shift_ref[...] = shift_ref[...] * KAPPA

    def fill(block, _, fetches=()):
        rows = pl.ds(pl.multiple_of(block * TALL, TALL), TALL)
        top = jnp.full((TALL, LANES), -jnp.inf, F32)
        for at in range(0, tile_ref.shape[1], WIDE):
            for k, fetch in enumerate(fetches):
                if at <= k * part < at + WIDE:
                    fetch.wait()
            exponent = exponent_block(crawl_ref, bench_ref, shift_ref, rows, pl.ds(at, WIDE))
            tile_ref[rows, at:at + WIDE] = exponent
            for lane in range(0, WIDE, LANES):
                top = jnp.maximum(top, exponent[:, lane:lane + LANES])
        top_scratch[rows, :] = top
        return _

    fill(0, 0, fetches)
    lax.fori_loop(1, tile_ref.shape[0] // TALL, fill, 0)

    def power(block, _):
        rows = pl.ds(pl.multiple_of(block * height, height), height)
        top = jnp.broadcast_to(jnp.max(top_scratch[rows, :], axis=1, keepdims=True), (height, LANES))
        acc = jnp.zeros((height, LANES), F32)
        for at in range(0, tile_ref.shape[1], LANES):
            value = jnp.exp2(tile_ref[rows, at:at + LANES] - top)
            tile_ref[rows, at:at + LANES] = value
            acc += value
        top_scratch[rows, :] = top
        sum_scratch[rows, :] = acc
        return _

    lax.fori_loop(0, tile_ref.shape[0] // height, power, 0)
    top = jnp.transpose(top_scratch[...])[0:1, :]
    top_ref[...] = top
    level_ref[...] = top + jnp.log2(row_form(sum_scratch[...]))


def column_level_kernel(parts, tile_ref, top_ref, *refs):
    part_refs, (crawl_ref, bench_ref, shift_ref, level_ref, out_ref, weights) = refs[:parts], refs[parts:]
    level = log_sum([p[...] for p in part_refs])
    level_ref[...] = level
    weights[...] = column_form(jnp.exp2(top_ref[...] - level))
    column_sums(tile_ref, weights, out_ref)
    out_ref[...] = jnp.log2(out_ref[...])

    @pl.when(jnp.min(out_ref[...]) < LOWEST)
    def _():
        weights[...] = column_form(level)
        blocks = tile_ref.shape[0] // TALL

        def column_block(column, _):
            columns = pl.ds(pl.multiple_of(column * WIDE, WIDE), WIDE)

            def logs(block):
                rows = pl.ds(pl.multiple_of(block * TALL, TALL), TALL)
                return exponent_block(crawl_ref, bench_ref, shift_ref, rows, columns) - weights[rows, 0:1]

            top = lax.fori_loop(
                0, blocks, lambda b, t: jnp.maximum(t, jnp.max(logs(b), axis=0, keepdims=True)),
                jnp.full((1, WIDE), -jnp.inf, F32))
            total = lax.fori_loop(
                0, blocks, lambda b, t: t + jnp.sum(jnp.exp2(logs(b) - top), axis=0, keepdims=True),
                jnp.zeros((1, WIDE), F32))
            out_ref[:, columns] = top + jnp.log2(total)
            return _

        lax.fori_loop(0, tile_ref.shape[1] // WIDE, column_block, 0)


def soft_kernel(parts, tile_ref, top_ref, level_ref, *refs):
    part_refs = refs[:parts]
    crawl_ref, bench_ref, shift_ref, soft_ref, left_ref, right_ref, mass_ref, sums_ref, partial, weights = refs[parts:]
    logs = log_sum([p[...] for p in part_refs])
    lowest = jnp.min(logs)

    @pl.when(lowest >= LOWEST)
    def _():
        left = jnp.exp2(top_ref[...] - level_ref[...])
        left_ref[...] = left
        right_ref[...] = jnp.exp2(-logs)
        mass_ref[...] = jnp.ones_like(logs)
        sums_ref[...] = row_sums(tile_ref, right_ref, partial) * left

    @pl.when(lowest < LOWEST)
    def _():
        left_ref[...] = jnp.ones_like(left_ref)
        mass_ref[...] = jnp.exp2(logs)
        right_ref[...] = logs
        weights[...] = column_form(level_ref[...])
        partial[...] = jnp.zeros_like(partial)

        def body(block, _):
            rows = pl.ds(pl.multiple_of(block * TALL, TALL), TALL)
            level = weights[rows, 0:1]

            def column_block(column, _):
                columns = pl.ds(pl.multiple_of(column * WIDE, WIDE), WIDE)
                exponent = exponent_block(crawl_ref, bench_ref, shift_ref, rows, columns)
                value = jnp.exp2(exponent - level - right_ref[:, columns])
                soft_ref[rows, columns] = value
                partial[rows, :] += sum(value[:, lane:lane + LANES] for lane in range(0, WIDE, LANES))
                return _

            return lax.fori_loop(0, tile_ref.shape[1] // WIDE, column_block, _)

        lax.fori_loop(0, tile_ref.shape[0] // TALL, body, 0)
        right_ref[...] = jnp.ones_like(right_ref)
        sums_ref[...] = row_form(partial[...])


def second_column_kernel(parts, soft_ref, left_ref, right_ref, *refs):
    part_refs, (inverse_ref, out_ref, weights) = refs[:parts], refs[parts:]
    inverse = left_ref[...] / sum(p[...] for p in part_refs)
    inverse_ref[...] = inverse
    weights[...] = column_form(inverse)
    column_sums(soft_ref, weights, out_ref, right_ref)


def second_row_kernel(parts, soft_ref, inverse_ref, right_ref, cotangent_ref, *refs):
    part_refs, (scaled_ref, out_ref, partial) = refs[:parts], refs[parts:]
    scaled_ref[...] = cotangent_ref[...] / sum(p[...] for p in part_refs) * right_ref[...]
    out_ref[...] = row_sums(soft_ref, scaled_ref, partial) * inverse_ref[...]


def first_column_kernel(parts, soft_ref, inverse_ref, right_ref, cotangent_ref, *refs):
    part_refs, (scaled_ref, out_ref, weights) = refs[:parts], refs[parts:]
    scaled = (cotangent_ref[...] - sum(p[...] for p in part_refs)) * inverse_ref[...]
    scaled_ref[...] = scaled
    weights[...] = column_form(-scaled)
    column_sums(soft_ref, weights, out_ref, right_ref)


def first_row_kernel(parts, soft_ref, left_ref, right_ref, *refs):
    part_refs, (back_ref, out_ref, partial) = refs[:parts], refs[parts:]
    back_ref[...] = sum(p[...] for p in part_refs) * right_ref[...]
    out_ref[...] = -row_sums(soft_ref, back_ref, partial) * left_ref[...]


def ring_order(n):
    return [*range(0, n, 2), *range(n - 1, 0, -2)]


def ring_share(n, at):
    me = lax.axis_index("rows")
    place = lax.rem(lax.select(lax.rem(me, 2) == 0, me // 2, n - 1 - me // 2) + at, n)
    return lax.select(place < n // 2, 2 * place, 2 * (n - 1 - place) + 1)


def thirds(x):
    parts = []
    for _ in range(3):
        parts.append(x.astype(jnp.bfloat16).astype(F32))
        x = x - parts[-1]
    return parts


def early_kernel(soft_ref, inverse_ref, scaled_ref, left_ref, scaled2_ref, right_ref, back_ref, mass_ref, *refs):
    first_ref, early_ref, row_parts, column_parts = refs
    row_parts[...] = jnp.zeros_like(row_parts)
    column_parts[...] = jnp.zeros_like(column_parts)
    at = 0
    for row, column in ((inverse_ref, scaled2_ref), (scaled_ref, right_ref), (left_ref, back_ref)):
        r, c = thirds(-row[...]), thirds(column[...])
        for i, j in ((0, 0), (0, 1), (1, 0), (1, 1), (0, 2), (2, 0)):
            row_parts[at:at + 1, :] = r[i]
            column_parts[at:at + 1, :] = c[j]
            at += 1

    def body(block, _):
        rows = pl.ds(pl.multiple_of(block * TALL, TALL), TALL)
        r = row_parts[:, rows].astype(jnp.bfloat16)
        for at in range(0, soft_ref.shape[1], WIDE):
            span = slice(at, at + WIDE)
            factor = lax.dot_general(
                r, column_parts[:, span].astype(jnp.bfloat16), (((0,), (0,)), ((), ())), preferred_element_type=F32)
            early_ref[rows, span] = soft_ref[rows, span] * factor
        return _

    lax.fori_loop(0, soft_ref.shape[0] // TALL, body, 0)
    mass = mass_ref[...]

    @pl.when(jnp.max(jnp.abs(mass - 1.0)) > 0.0)
    def _():
        def scale(block, _):
            rows = pl.ds(pl.multiple_of(block * 8, 8), 8)
            first_ref[rows, :] = soft_ref[rows, :] * mass_ref[...]
            return _

        lax.fori_loop(0, soft_ref.shape[0] // 8, scale, 0)


def score_grad(early, first, last):
    return (early + first * last).astype(jnp.bfloat16)


def far_kernel(parts, n, first_ref, early_ref, left_ref, crawl_ref, *refs):
    part_refs, (last_ref, *piece_refs, flat) = refs[:parts], refs[parts:]
    last_ref[...] = column_form(-left_ref[...] * sum(p[...] for p in part_refs))
    if not piece_refs:
        return
    width = flat.shape[1]
    start = ring_share(n, n // 2) * width
    flat[...] = jnp.zeros_like(flat)

    def body(block, _):
        rows = pl.ds(pl.multiple_of(block * TALL, TALL), TALL)
        last = last_ref[rows, :]
        pieces = []
        for lane in range(0, width, LANES):
            span = pl.ds(pl.multiple_of(start + lane, LANES), LANES)
            pieces.append(score_grad(early_ref[rows, span], first_ref[rows, span], last))
        grad = jnp.concatenate(pieces, axis=1)
        flat[...] += lax.dot_general(crawl_ref[rows, :], grad, (((0,), (0,)), ((), ())), preferred_element_type=F32)
        return _

    lax.fori_loop(0, first_ref.shape[0] // TALL, body, 0)
    half = width // 2
    for k, piece in enumerate(piece_refs):
        piece[...] = jnp.transpose(flat[:, k * half:(k + 1) * half])


def gradient_kernel(n, places, first_ref, early_ref, last_ref, crawl_ref, bench_ref, *refs):
    keep_ref, send_ref, *piece_refs, flat, whole, total = refs
    flat[...] = jnp.zeros_like(flat)

    def body(block, _):
        rows = pl.ds(pl.multiple_of(block * TALL, TALL), TALL)
        last = last_ref[rows, :]
        x = crawl_ref[rows, :]
        acc = jnp.zeros((TALL, LANES), F32)
        for at in range(0, first_ref.shape[1], WIDE):
            pieces = []
            for lane in range(at, at + WIDE, LANES):
                span = slice(lane, lane + LANES)
                pieces.append(score_grad(early_ref[rows, span], first_ref[rows, span], last))
            grad = jnp.concatenate(pieces, axis=1)
            acc += jnp.dot(grad, bench_ref[at:at + WIDE, :], preferred_element_type=F32)
            flat[:, at:at + WIDE] += lax.dot_general(x, grad, (((0,), (0,)), ((), ())), preferred_element_type=F32)
        total[rows, :] = acc
        return _

    lax.fori_loop(0, first_ref.shape[0] // TALL, body, 0)
    me = lax.axis_index("cols")
    quarter = total.shape[0] // 4
    for k, (ref, low) in enumerate(((keep_ref, 0), (send_ref, 0), (keep_ref, quarter), (send_ref, quarter))):
        start = pl.multiple_of(lax.bitwise_xor(me, k) * quarter, quarter)
        ref[low:low + quarter, :] = total[pl.ds(start, quarter), :]
    whole[...] = jnp.transpose(flat[...])
    height = piece_refs[0].shape[0]
    for k, piece in enumerate(piece_refs):
        start = ring_share(n, places[k // 2]) * 2 * height + k % 2 * height
        piece[...] = whole[pl.ds(pl.multiple_of(start, height), height), :]


def placing_kernel(n, *refs):
    (own_ref, beside_ref, pair_ref, *pieces), (crawl_out, bench_out, sems) = refs[:-3], refs[-3:]
    me = lax.axis_index("cols")
    quarter = own_ref.shape[0]
    moves = []
    for k, piece in ((0, own_ref), (2, beside_ref), (1, pair_ref.at[:quarter]), (3, pair_ref.at[quarter:])):
        start = pl.multiple_of(lax.bitwise_xor(me, k) * quarter, quarter)
        moves.append((piece, crawl_out.at[pl.ds(start, quarter)]))
    height = pieces[0].shape[0]
    for at, piece in enumerate(pieces):
        start = pl.multiple_of(ring_share(n, at // 2) * 2 * height + at % 2 * height, height)
        moves.append((piece, bench_out.at[pl.ds(start, height)]))
    copies = [pltpu.make_async_copy(source, target, sems.at[k]) for k, (source, target) in enumerate(moves)]
    for copy in copies:
        copy.start()
    for copy in copies:
        copy.wait()


def call(kernel, args, outs, scratch, aliases=None):
    return pl.pallas_call(
        kernel,
        in_specs=[pl.BlockSpec(memory_space=pltpu.VMEM)] * len(args),
        out_specs=[pl.BlockSpec(memory_space=pltpu.VMEM)] * len(outs),
        out_shape=outs,
        scratch_shapes=[pltpu.VMEM(shape, F32) for shape in scratch],
        input_output_aliases=aliases or {},
        compiler_params=pltpu.CompilerParams(vmem_limit_bytes=LIMIT),
    )(*args)


def shaped(*shape, kind=F32):
    return jax.ShapeDtypeStruct(shape, kind)


def resident(*shape, kind=F32):
    return pltpu.VMEM(shape, kind)


def kept(x):
    return pltpu.with_memory_space_constraint(x, pltpu.VMEM)


def exchange(x, axis, stride, size):
    n = lax.axis_size(axis)
    return [x] + [lax.ppermute(x, axis, [(i, i ^ (k * stride)) for i in range(n)]) for k in range(1, size)]


def spread(x, axis, first, join):
    n = lax.axis_size(axis)
    stride, size = 1, min(first, n)
    while True:
        parts = exchange(x, axis, stride, size)
        stride *= size
        if stride == n:
            return parts
        x = join(parts)
        size = min(4, n // stride)


def ring_all_reduce(pieces, n):
    order = ring_order(n)
    up = [(order[p], order[(p + 1) % n]) for p in range(n)]
    down = [(b, a) for a, b in up]
    far = n // 2
    mine = [[pieces[2 * at], pieces[2 * at + 1]] for at in range(n)]

    def ahead(x):
        return lax.ppermute(x, "rows", up)

    def behind(x):
        return lax.ppermute(x, "rows", down)

    rise, fall = [ahead(mine[far][0]), None], [None, behind(mine[far][1])]
    for step in range(far - 1, 0, -1):
        rise = [ahead(m if r is None else m + r) for m, r in zip(mine[step], rise)]
        fall = [behind(m if f is None else m + f) for m, f in zip(mine[-step], fall)]
    own = [m + r + f for m, r, f in zip(mine[0], rise, fall)]
    found = {0: own}
    rise = fall = own
    for step in range(1, far):
        rise, fall = [ahead(r) for r in rise], [behind(f) for f in fall]
        found[n - step], found[step] = rise, fall
    found[far] = [ahead(rise[0]), behind(fall[1])]
    return [half for at in range(n) for half in found[at]]


def quarter_all_reduce(keep, send):
    quarter = keep.shape[0] // 2
    keep = keep + exchange(send, "cols", 1, 2)[1]
    own = keep[:quarter] + exchange(keep[quarter:], "cols", 2, 2)[1]
    beside = exchange(own, "cols", 2, 2)[1]
    return own, beside, exchange(jnp.concatenate([own, beside]), "cols", 1, 2)[1]


def per_device(crawl, bench, start_duals, row_cotangent, col_cotangent):
    rows, columns = crawl.shape[0], bench.shape[0]
    row_cotangent = row_cotangent.reshape(1, rows)
    col_cotangent = col_cotangent.reshape(1, columns)
    row, column, tall = shaped(1, rows), shaped(1, columns), (rows, LANES)
    tile_shape = resident(rows, columns)

    def over_cols(x, join=sum):
        return spread(x, "cols", 4, join)

    def over_rows(x, join=sum):
        n = lax.axis_size("rows")
        if n > 8:
            return spread(x, "rows", 4, join)
        copies = jnp.broadcast_to(x.reshape(1, -1, LANES), (n, columns // LANES, LANES))
        return [join(list(lax.all_to_all(copies, "rows", 0, 0))).reshape(1, columns)]

    tile, top, local, crawl, bench, shift = pl.pallas_call(
        row_level_kernel,
        in_specs=[pl.BlockSpec(memory_space=pltpu.HBM)] * 3,
        out_specs=[pl.BlockSpec(memory_space=pltpu.VMEM)] * 6,
        out_shape=[tile_shape, row, row, resident(*crawl.shape, kind=crawl.dtype), resident(*bench.shape, kind=bench.dtype),
                   resident(1, columns)],
        scratch_shapes=[pltpu.VMEM(tall, F32)] * 2 + [pltpu.SemaphoreType.DMA((6,))],
        compiler_params=pltpu.CompilerParams(vmem_limit_bytes=LIMIT),
    )(*(pltpu.with_memory_space_constraint(x, pltpu.HBM) for x in (crawl, bench, start_duals.reshape(1, columns))))
    crawl, bench, shift = kept(crawl), kept(bench), kept(shift)
    parts = over_cols(local, log_sum)
    level, local = call(
        functools.partial(column_level_kernel, len(parts)),
        [kept(tile), top, *parts, crawl, bench, shift], [row, column], [tall])
    parts = over_rows(local, log_sum)
    soft, left, right, mass, local = call(
        functools.partial(soft_kernel, len(parts)),
        [kept(tile), top, level, *parts, crawl, bench, shift], [tile_shape, row, column, column, row],
        [tall, tall], aliases={0: 0})
    soft = kept(soft)
    parts = over_cols(local)
    inverse, local = call(
        functools.partial(second_column_kernel, len(parts)), [soft, left, right, *parts], [row, column], [tall])
    parts = over_rows(local)
    scaled2, local = call(
        functools.partial(second_row_kernel, len(parts)),
        [soft, inverse, right, col_cotangent, *parts], [column, row], [tall])
    parts = over_cols(local)
    scaled, local = call(
        functools.partial(first_column_kernel, len(parts)),
        [soft, inverse, right, row_cotangent, *parts], [row, column], [tall])
    parts = over_rows(local)
    back, local = call(
        functools.partial(first_row_kernel, len(parts)), [soft, left, right, *parts], [column, row], [tall])
    parts = over_cols(local)
    n = lax.axis_size("rows")
    width = bench.shape[1]
    share = columns // n
    piece = shaped(share // 2, width)
    ahead = share % (2 * LANES) == 0
    first, early = call(
        early_kernel, [soft, inverse, scaled, left, scaled2, right, back, mass],
        [tile_shape, tile_shape], [(32, rows), (32, columns)], aliases={0: 0})
    first, early = kept(first), kept(early)
    last, *far = call(
        functools.partial(far_kernel, len(parts), n), [first, early, left, crawl, *parts],
        [shaped(*tall)] + [piece] * (2 * ahead), [(LANES, share)])
    places = [at for at in range(n) if at != n // 2 or not ahead]
    keep, send, *pieces = call(
        functools.partial(gradient_kernel, n, places),
        [first, early, last, crawl, bench],
        [shaped(rows // 2, width)] * 2 + [piece] * (2 * len(places)), [(LANES, columns), (columns, LANES), tall])
    if ahead:
        pieces[n:n] = far
    pieces = ring_all_reduce(pieces, n)
    quarters = quarter_all_reduce(keep, send)
    crawl_grad, bench_grad = pl.pallas_call(
        functools.partial(placing_kernel, n),
        in_specs=[pl.BlockSpec(memory_space=pltpu.VMEM)] * (3 + len(pieces)),
        out_specs=[pl.BlockSpec(memory_space=pl.ANY)] * 2,
        out_shape=[shaped(rows, width), shaped(columns, width)],
        scratch_shapes=[pltpu.SemaphoreType.DMA((4 + len(pieces),))],
        compiler_params=pltpu.CompilerParams(vmem_limit_bytes=LIMIT),
    )(*map(kept, (*quarters, *pieces)))
    return (crawl_grad, bench_grad)


def solution(mesh):
    placed = (P("rows", None), P("cols", None), P("cols"), P("rows"), P("cols"))
    return jax.shard_map(
        per_device,
        mesh=mesh,
        in_specs=placed,
        out_specs=(P("rows", None), P("cols", None)),
        check_vma=False,
    )
```

```python
import functools
import math

import jax
import jax.numpy as jnp
from jax import lax
from jax.experimental import pallas as pl
from jax.experimental.pallas import tpu as pltpu
from jax.sharding import PartitionSpec as P

EPSILON = 0.05
KAPPA = math.log2(math.e) / EPSILON
LOWEST = -64.0
LANES = 128
WIDE = 512
TALL = 1024
LIMIT = 8 * 2**20
F32 = jnp.float32


def transposed_dot(a, b):
    return lax.dot_general(a, b, (((1,), (1,)), ((), ())), preferred_element_type=F32)


def column_form(row):
    return jnp.transpose(jnp.broadcast_to(row, (LANES, row.shape[1])))


def row_form(partial):
    return jnp.sum(jnp.transpose(partial), axis=0, keepdims=True)


def log_sum(parts):
    top = functools.reduce(jnp.maximum, parts)
    return top + jnp.log2(sum(jnp.exp2(p - top) for p in parts))


def row_sums(tile_ref, weights_ref, partial_ref):
    height = 128

    def body(block, _):
        rows = pl.ds(pl.multiple_of(block * height, height), height)
        acc = jnp.zeros((height, LANES), F32)
        for at in range(0, tile_ref.shape[1], LANES):
            acc += tile_ref[rows, at:at + LANES] * weights_ref[:, at:at + LANES]
        partial_ref[rows, :] = acc
        return _

    lax.fori_loop(0, tile_ref.shape[0] // height, body, 0)
    return row_form(partial_ref[...])


def column_sums(tile_ref, weights_ref, out_ref, scale_ref=None):
    starts = range(0, tile_ref.shape[1], LANES)

    def body(block, accs):
        for half in range(2):
            rows = pl.ds(pl.multiple_of(block * 16 + half * 8, 8), 8)
            weights = weights_ref[rows, :]
            accs = tuple(acc + tile_ref[rows, at:at + LANES] * weights for acc, at in zip(accs, starts))
        return accs

    accs = lax.fori_loop(0, tile_ref.shape[0] // 16, body, tuple(jnp.zeros((8, LANES), F32) for _ in starts))
    for acc, at in zip(accs, starts):
        total = jnp.sum(acc, axis=0, keepdims=True)
        out_ref[:, at:at + LANES] = total if scale_ref is None else total * scale_ref[:, at:at + LANES]


def exponent_block(crawl_ref, bench_ref, shift_ref, rows, columns):
    scores = transposed_dot(crawl_ref[rows, :], bench_ref[columns, :])
    return scores * KAPPA + shift_ref[:, columns]


def row_level_kernel(crawl_hbm, bench_hbm, duals_hbm, tile_ref, top_ref, level_ref, crawl_ref, bench_ref, shift_ref,
                     top_scratch, sum_scratch, sems):
    height = 128
    chunks = 4
    part = bench_ref.shape[0] // chunks
    copies = [pltpu.make_async_copy(crawl_hbm, crawl_ref, sems.at[chunks]),
              pltpu.make_async_copy(duals_hbm, shift_ref, sems.at[chunks + 1])]
    fetches = [
        pltpu.make_async_copy(bench_hbm.at[k * part:(k + 1) * part], bench_ref.at[k * part:(k + 1) * part], sems.at[k])
        for k in range(chunks)]
    for copy in (*copies, *fetches):
        copy.start()
    for copy in copies:
        copy.wait()
    shift_ref[...] = shift_ref[...] * KAPPA

    def fill(block, _, fetches=()):
        rows = pl.ds(pl.multiple_of(block * TALL, TALL), TALL)
        top = jnp.full((TALL, LANES), -jnp.inf, F32)
        for at in range(0, tile_ref.shape[1], WIDE):
            for k, fetch in enumerate(fetches):
                if at <= k * part < at + WIDE:
                    fetch.wait()
            exponent = exponent_block(crawl_ref, bench_ref, shift_ref, rows, pl.ds(at, WIDE))
            tile_ref[rows, at:at + WIDE] = exponent
            for lane in range(0, WIDE, LANES):
                top = jnp.maximum(top, exponent[:, lane:lane + LANES])
        top_scratch[rows, :] = top
        return _

    fill(0, 0, fetches)
    lax.fori_loop(1, tile_ref.shape[0] // TALL, fill, 0)

    def power(block, _):
        rows = pl.ds(pl.multiple_of(block * height, height), height)
        top = jnp.broadcast_to(jnp.max(top_scratch[rows, :], axis=1, keepdims=True), (height, LANES))
        acc = jnp.zeros((height, LANES), F32)
        for at in range(0, tile_ref.shape[1], LANES):
            value = jnp.exp2(tile_ref[rows, at:at + LANES] - top)
            tile_ref[rows, at:at + LANES] = value
            acc += value
        top_scratch[rows, :] = top
        sum_scratch[rows, :] = acc
        return _

    lax.fori_loop(0, tile_ref.shape[0] // height, power, 0)
    top = jnp.transpose(top_scratch[...])[0:1, :]
    top_ref[...] = top
    level_ref[...] = top + jnp.log2(row_form(sum_scratch[...]))


def column_level_kernel(parts, tile_ref, top_ref, *refs):
    part_refs, (crawl_ref, bench_ref, shift_ref, level_ref, out_ref, weights) = refs[:parts], refs[parts:]
    level = log_sum([p[...] for p in part_refs])
    level_ref[...] = level
    weights[...] = column_form(jnp.exp2(top_ref[...] - level))
    column_sums(tile_ref, weights, out_ref)
    out_ref[...] = jnp.log2(out_ref[...])

    @pl.when(jnp.min(out_ref[...]) < LOWEST)
    def _():
        weights[...] = column_form(level)
        blocks = tile_ref.shape[0] // TALL

        def column_block(column, _):
            columns = pl.ds(pl.multiple_of(column * WIDE, WIDE), WIDE)

            def logs(block):
                rows = pl.ds(pl.multiple_of(block * TALL, TALL), TALL)
                return exponent_block(crawl_ref, bench_ref, shift_ref, rows, columns) - weights[rows, 0:1]

            top = lax.fori_loop(
                0, blocks, lambda b, t: jnp.maximum(t, jnp.max(logs(b), axis=0, keepdims=True)),
                jnp.full((1, WIDE), -jnp.inf, F32))
            total = lax.fori_loop(
                0, blocks, lambda b, t: t + jnp.sum(jnp.exp2(logs(b) - top), axis=0, keepdims=True),
                jnp.zeros((1, WIDE), F32))
            out_ref[:, columns] = top + jnp.log2(total)
            return _

        lax.fori_loop(0, tile_ref.shape[1] // WIDE, column_block, 0)


def soft_kernel(parts, tile_ref, top_ref, level_ref, *refs):
    part_refs = refs[:parts]
    crawl_ref, bench_ref, shift_ref, soft_ref, left_ref, right_ref, mass_ref, sums_ref, partial, weights = refs[parts:]
    logs = log_sum([p[...] for p in part_refs])
    lowest = jnp.min(logs)

    @pl.when(lowest >= LOWEST)
    def _():
        left = jnp.exp2(top_ref[...] - level_ref[...])
        left_ref[...] = left
        right_ref[...] = jnp.exp2(-logs)
        mass_ref[...] = jnp.ones_like(logs)
        sums_ref[...] = row_sums(tile_ref, right_ref, partial) * left

    @pl.when(lowest < LOWEST)
    def _():
        left_ref[...] = jnp.ones_like(left_ref)
        mass_ref[...] = jnp.exp2(logs)
        right_ref[...] = logs
        weights[...] = column_form(level_ref[...])
        partial[...] = jnp.zeros_like(partial)

        def body(block, _):
            rows = pl.ds(pl.multiple_of(block * TALL, TALL), TALL)
            level = weights[rows, 0:1]

            def column_block(column, _):
                columns = pl.ds(pl.multiple_of(column * WIDE, WIDE), WIDE)
                exponent = exponent_block(crawl_ref, bench_ref, shift_ref, rows, columns)
                value = jnp.exp2(exponent - level - right_ref[:, columns])
                soft_ref[rows, columns] = value
                partial[rows, :] += sum(value[:, lane:lane + LANES] for lane in range(0, WIDE, LANES))
                return _

            return lax.fori_loop(0, tile_ref.shape[1] // WIDE, column_block, _)

        lax.fori_loop(0, tile_ref.shape[0] // TALL, body, 0)
        right_ref[...] = jnp.ones_like(right_ref)
        sums_ref[...] = row_form(partial[...])


def second_column_kernel(parts, soft_ref, left_ref, right_ref, *refs):
    part_refs, (inverse_ref, out_ref, weights) = refs[:parts], refs[parts:]
    inverse = left_ref[...] / sum(p[...] for p in part_refs)
    inverse_ref[...] = inverse
    weights[...] = column_form(inverse)
    column_sums(soft_ref, weights, out_ref, right_ref)


def second_row_kernel(parts, soft_ref, inverse_ref, right_ref, cotangent_ref, *refs):
    part_refs, (scaled_ref, out_ref, partial) = refs[:parts], refs[parts:]
    scaled_ref[...] = cotangent_ref[...] / sum(p[...] for p in part_refs) * right_ref[...]
    out_ref[...] = row_sums(soft_ref, scaled_ref, partial) * inverse_ref[...]


def first_column_kernel(parts, soft_ref, inverse_ref, right_ref, cotangent_ref, *refs):
    part_refs, (scaled_ref, out_ref, weights) = refs[:parts], refs[parts:]
    scaled = (cotangent_ref[...] - sum(p[...] for p in part_refs)) * inverse_ref[...]
    scaled_ref[...] = scaled
    weights[...] = column_form(-scaled)
    column_sums(soft_ref, weights, out_ref, right_ref)


def first_row_kernel(parts, soft_ref, left_ref, right_ref, *refs):
    part_refs, (back_ref, out_ref, partial) = refs[:parts], refs[parts:]
    back_ref[...] = sum(p[...] for p in part_refs) * right_ref[...]
    out_ref[...] = -row_sums(soft_ref, back_ref, partial) * left_ref[...]


def ring_order(n):
    return [*range(0, n, 2), *range(n - 1, 0, -2)]


def ring_share(n, at):
    me = lax.axis_index("rows")
    place = lax.rem(lax.select(lax.rem(me, 2) == 0, me // 2, n - 1 - me // 2) + at, n)
    return lax.select(place < n // 2, 2 * place, 2 * (n - 1 - place) + 1)


def thirds(x):
    parts = []
    for _ in range(3):
        parts.append(x.astype(jnp.bfloat16).astype(F32))
        x = x - parts[-1]
    return parts


def early_kernel(soft_ref, inverse_ref, scaled_ref, left_ref, scaled2_ref, right_ref, back_ref, mass_ref, *refs):
    first_ref, early_ref, row_parts, column_parts = refs
    row_parts[...] = jnp.zeros_like(row_parts)
    column_parts[...] = jnp.zeros_like(column_parts)
    at = 0
    for row, column in ((inverse_ref, scaled2_ref), (scaled_ref, right_ref), (left_ref, back_ref)):
        r, c = thirds(-row[...]), thirds(column[...])
        for i, j in ((0, 0), (0, 1), (1, 0), (1, 1), (0, 2), (2, 0)):
            row_parts[at:at + 1, :] = r[i]
            column_parts[at:at + 1, :] = c[j]
            at += 1

    def body(block, _):
        rows = pl.ds(pl.multiple_of(block * TALL, TALL), TALL)
        r = row_parts[:, rows].astype(jnp.bfloat16)
        for at in range(0, soft_ref.shape[1], WIDE):
            span = slice(at, at + WIDE)
            factor = lax.dot_general(
                r, column_parts[:, span].astype(jnp.bfloat16), (((0,), (0,)), ((), ())), preferred_element_type=F32)
            early_ref[rows, span] = soft_ref[rows, span] * factor
        return _

    lax.fori_loop(0, soft_ref.shape[0] // TALL, body, 0)
    mass = mass_ref[...]

    @pl.when(jnp.max(jnp.abs(mass - 1.0)) > 0.0)
    def _():
        def scale(block, _):
            rows = pl.ds(pl.multiple_of(block * 8, 8), 8)
            first_ref[rows, :] = soft_ref[rows, :] * mass_ref[...]
            return _

        lax.fori_loop(0, soft_ref.shape[0] // 8, scale, 0)


def score_grad(early, first, last):
    return (early + first * last).astype(jnp.bfloat16)


def far_kernel(parts, n, first_ref, early_ref, left_ref, crawl_ref, *refs):
    part_refs, (last_ref, *piece_refs, flat) = refs[:parts], refs[parts:]
    last_ref[...] = column_form(-left_ref[...] * sum(p[...] for p in part_refs))
    if not piece_refs:
        return
    width = flat.shape[1]
    start = ring_share(n, n // 2) * width
    flat[...] = jnp.zeros_like(flat)

    def body(block, _):
        rows = pl.ds(pl.multiple_of(block * TALL, TALL), TALL)
        last = last_ref[rows, :]
        pieces = []
        for lane in range(0, width, LANES):
            span = pl.ds(pl.multiple_of(start + lane, LANES), LANES)
            pieces.append(score_grad(early_ref[rows, span], first_ref[rows, span], last))
        grad = jnp.concatenate(pieces, axis=1)
        flat[...] += lax.dot_general(crawl_ref[rows, :], grad, (((0,), (0,)), ((), ())), preferred_element_type=F32)
        return _

    lax.fori_loop(0, first_ref.shape[0] // TALL, body, 0)
    half = width // 2
    for k, piece in enumerate(piece_refs):
        piece[...] = jnp.transpose(flat[:, k * half:(k + 1) * half])


def gradient_kernel(n, places, first_ref, early_ref, last_ref, crawl_ref, bench_ref, *refs):
    keep_ref, send_ref, *piece_refs, flat, whole, total = refs
    flat[...] = jnp.zeros_like(flat)

    def body(block, _):
        rows = pl.ds(pl.multiple_of(block * TALL, TALL), TALL)
        last = last_ref[rows, :]
        x = crawl_ref[rows, :]
        acc = jnp.zeros((TALL, LANES), F32)
        for at in range(0, first_ref.shape[1], WIDE):
            pieces = []
            for lane in range(at, at + WIDE, LANES):
                span = slice(lane, lane + LANES)
                pieces.append(score_grad(early_ref[rows, span], first_ref[rows, span], last))
            grad = jnp.concatenate(pieces, axis=1)
            acc += jnp.dot(grad, bench_ref[at:at + WIDE, :], preferred_element_type=F32)
            flat[:, at:at + WIDE] += lax.dot_general(x, grad, (((0,), (0,)), ((), ())), preferred_element_type=F32)
        total[rows, :] = acc
        return _

    lax.fori_loop(0, first_ref.shape[0] // TALL, body, 0)
    me = lax.axis_index("cols")
    quarter = total.shape[0] // 4
    for k, (ref, low) in enumerate(((keep_ref, 0), (send_ref, 0), (keep_ref, quarter), (send_ref, quarter))):
        start = pl.multiple_of(lax.bitwise_xor(me, k) * quarter, quarter)
        ref[low:low + quarter, :] = total[pl.ds(start, quarter), :]
    whole[...] = jnp.transpose(flat[...])
    height = piece_refs[0].shape[0]
    for k, piece in enumerate(piece_refs):
        start = ring_share(n, places[k // 2]) * 2 * height + k % 2 * height
        piece[...] = whole[pl.ds(pl.multiple_of(start, height), height), :]


def placing_kernel(n, *refs):
    (own_ref, beside_ref, pair_ref, *pieces), (crawl_out, bench_out, sems) = refs[:-3], refs[-3:]
    me = lax.axis_index("cols")
    quarter = own_ref.shape[0]
    moves = []
    for k, piece in ((0, own_ref), (2, beside_ref), (1, pair_ref.at[:quarter]), (3, pair_ref.at[quarter:])):
        start = pl.multiple_of(lax.bitwise_xor(me, k) * quarter, quarter)
        moves.append((piece, crawl_out.at[pl.ds(start, quarter)]))
    height = pieces[0].shape[0]
    for at, piece in enumerate(pieces):
        start = pl.multiple_of(ring_share(n, at // 2) * 2 * height + at % 2 * height, height)
        moves.append((piece, bench_out.at[pl.ds(start, height)]))
    copies = [pltpu.make_async_copy(source, target, sems.at[k]) for k, (source, target) in enumerate(moves)]
    for copy in copies:
        copy.start()
    for copy in copies:
        copy.wait()


def call(kernel, args, outs, scratch, aliases=None):
    return pl.pallas_call(
        kernel,
        in_specs=[pl.BlockSpec(memory_space=pltpu.VMEM)] * len(args),
        out_specs=[pl.BlockSpec(memory_space=pltpu.VMEM)] * len(outs),
        out_shape=outs,
        scratch_shapes=[pltpu.VMEM(shape, F32) for shape in scratch],
        input_output_aliases=aliases or {},
        compiler_params=pltpu.CompilerParams(vmem_limit_bytes=LIMIT),
    )(*args)


def shaped(*shape, kind=F32):
    return jax.ShapeDtypeStruct(shape, kind)


def resident(*shape, kind=F32):
    return pltpu.VMEM(shape, kind)


def kept(x):
    return pltpu.with_memory_space_constraint(x, pltpu.VMEM)


def exchange(x, axis, stride, size):
    n = lax.axis_size(axis)
    return [x] + [lax.ppermute(x, axis, [(i, i ^ (k * stride)) for i in range(n)]) for k in range(1, size)]


def spread(x, axis, first, join):
    n = lax.axis_size(axis)
    stride, size = 1, min(first, n)
    while True:
        parts = exchange(x, axis, stride, size)
        stride *= size
        if stride == n:
            return parts
        x = join(parts)
        size = min(4, n // stride)


def ring_all_reduce(pieces, n):
    order = ring_order(n)
    up = [(order[p], order[(p + 1) % n]) for p in range(n)]
    down = [(b, a) for a, b in up]
    far = n // 2
    mine = [[pieces[2 * at], pieces[2 * at + 1]] for at in range(n)]

    def ahead(x):
        return lax.ppermute(x, "rows", up)

    def behind(x):
        return lax.ppermute(x, "rows", down)

    rise, fall = [ahead(mine[far][0]), None], [None, behind(mine[far][1])]
    for step in range(far - 1, 0, -1):
        rise = [ahead(m if r is None else m + r) for m, r in zip(mine[step], rise)]
        fall = [behind(m if f is None else m + f) for m, f in zip(mine[-step], fall)]
    own = [m + r + f for m, r, f in zip(mine[0], rise, fall)]
    found = {0: own}
    rise = fall = own
    for step in range(1, far):
        rise, fall = [ahead(r) for r in rise], [behind(f) for f in fall]
        found[n - step], found[step] = rise, fall
    found[far] = [ahead(rise[0]), behind(fall[1])]
    return [half for at in range(n) for half in found[at]]


def quarter_all_reduce(keep, send):
    quarter = keep.shape[0] // 2
    keep = keep + exchange(send, "cols", 1, 2)[1]
    own = keep[:quarter] + exchange(keep[quarter:], "cols", 2, 2)[1]
    beside = exchange(own, "cols", 2, 2)[1]
    return own, beside, exchange(jnp.concatenate([own, beside]), "cols", 1, 2)[1]


def per_device(crawl, bench, start_duals, row_cotangent, col_cotangent):
    rows, columns = crawl.shape[0], bench.shape[0]
    row_cotangent = row_cotangent.reshape(1, rows)
    col_cotangent = col_cotangent.reshape(1, columns)
    row, column, tall = shaped(1, rows), shaped(1, columns), (rows, LANES)
    tile_shape = resident(rows, columns)

    def over_cols(x, join=sum):
        return spread(x, "cols", 4, join)

    def over_rows(x, join=sum):
        n = lax.axis_size("rows")
        if n > 8:
            return spread(x, "rows", 4, join)
        copies = jnp.broadcast_to(x.reshape(1, -1, LANES), (n, columns // LANES, LANES))
        return [join(list(lax.all_to_all(copies, "rows", 0, 0))).reshape(1, columns)]

    tile, top, local, crawl, bench, shift = pl.pallas_call(
        row_level_kernel,
        in_specs=[pl.BlockSpec(memory_space=pltpu.HBM)] * 3,
        out_specs=[pl.BlockSpec(memory_space=pltpu.VMEM)] * 6,
        out_shape=[tile_shape, row, row, resident(*crawl.shape, kind=crawl.dtype), resident(*bench.shape, kind=bench.dtype),
                   resident(1, columns)],
        scratch_shapes=[pltpu.VMEM(tall, F32)] * 2 + [pltpu.SemaphoreType.DMA((6,))],
        compiler_params=pltpu.CompilerParams(vmem_limit_bytes=LIMIT),
    )(*(pltpu.with_memory_space_constraint(x, pltpu.HBM) for x in (crawl, bench, start_duals.reshape(1, columns))))
    crawl, bench, shift = kept(crawl), kept(bench), kept(shift)
    parts = over_cols(local, log_sum)
    level, local = call(
        functools.partial(column_level_kernel, len(parts)),
        [kept(tile), top, *parts, crawl, bench, shift], [row, column], [tall])
    parts = over_rows(local, log_sum)
    soft, left, right, mass, local = call(
        functools.partial(soft_kernel, len(parts)),
        [kept(tile), top, level, *parts, crawl, bench, shift], [tile_shape, row, column, column, row],
        [tall, tall], aliases={0: 0})
    soft = kept(soft)
    parts = over_cols(local)
    inverse, local = call(
        functools.partial(second_column_kernel, len(parts)), [soft, left, right, *parts], [row, column], [tall])
    parts = over_rows(local)
    scaled2, local = call(
        functools.partial(second_row_kernel, len(parts)),
        [soft, inverse, right, col_cotangent, *parts], [column, row], [tall])
    parts = over_cols(local)
    scaled, local = call(
        functools.partial(first_column_kernel, len(parts)),
        [soft, inverse, right, row_cotangent, *parts], [row, column], [tall])
    parts = over_rows(local)
    back, local = call(
        functools.partial(first_row_kernel, len(parts)), [soft, left, right, *parts], [column, row], [tall])
    parts = over_cols(local)
    n = lax.axis_size("rows")
    width = bench.shape[1]
    share = columns // n
    piece = shaped(share // 2, width)
    ahead = share % (2 * LANES) == 0
    first, early = call(
        early_kernel, [soft, inverse, scaled, left, scaled2, right, back, mass],
        [tile_shape, tile_shape], [(32, rows), (32, columns)], aliases={0: 0})
    first, early = kept(first), kept(early)
    last, *far = call(
        functools.partial(far_kernel, len(parts), n), [first, early, left, crawl, *parts],
        [shaped(*tall)] + [piece] * (2 * ahead), [(LANES, share)])
    places = [at for at in range(n) if at != n // 2 or not ahead]
    keep, send, *pieces = call(
        functools.partial(gradient_kernel, n, places),
        [first, early, last, crawl, bench],
        [shaped(rows // 2, width)] * 2 + [piece] * (2 * len(places)), [(LANES, columns), (columns, LANES), tall])
    if ahead:
        pieces[n:n] = far
    pieces = ring_all_reduce(pieces, n)
    quarters = quarter_all_reduce(keep, send)
    crawl_grad, bench_grad = pl.pallas_call(
        functools.partial(placing_kernel, n),
        in_specs=[pl.BlockSpec(memory_space=pltpu.VMEM)] * (3 + len(pieces)),
        out_specs=[pl.BlockSpec(memory_space=pl.ANY)] * 2,
        out_shape=[shaped(rows, width), shaped(columns, width)],
        scratch_shapes=[pltpu.SemaphoreType.DMA((4 + len(pieces),))],
        compiler_params=pltpu.CompilerParams(vmem_limit_bytes=LIMIT),
    )(*map(kept, (*quarters, *pieces)))
    return (crawl_grad, bench_grad)


def solution(mesh):
    placed = (P("rows", None), P("cols", None), P("cols"), P("rows"), P("cols"))
    return jax.shard_map(
        per_device,
        mesh=mesh,
        in_specs=placed,
        out_specs=(P("rows", None), P("cols", None)),
        check_vma=False,
    )
```
